32 devices in a mesh: seq: 8 (over z, y), head: 4 (over x, core).
Axes of the slice: x: 2, y: 2, z: 4, core: 2. Of those that a mesh axis runs over, the one named last changes fastest.
Arguments:
- tokens: bfloat16 [16384, 512], P('seq'), may hold values from -6 to 6
- cotangent: bfloat16 [16384, 512], P('seq'), may hold values from -6 to 6
- frames: int32 [32], replicated, may hold values from 1 to 16, 256 in all
- qkv_weight: float32 [3, 512, 512], P(None, 'seq', 'head'), may hold values from -0.53033009 to 0.53033009
- qkv_first: float32 [3, 512, 512], P(None, 'seq', 'head'), may hold values from -224 to 224
- qkv_second: float32 [3, 512, 512], P(None, 'seq', 'head'), may hold values from 491.52 to 9830.4
- out_weight: float32 [512, 512], P('head', 'seq'), may hold values from -3 to 3
- out_first: float32 [512, 512], P('head', 'seq'), may hold values from -56 to 56
- out_second: float32 [512, 512], P('head', 'seq'), may hold values from 26.2144 to 524.288
- up_weight: float32 [512, 2048], P('seq', 'head'), may hold values from -0.53033009 to 0.53033009
- up_first: float32 [512, 2048], P('seq', 'head'), may hold values from -192 to 192
- up_second: float32 [512, 2048], P('seq', 'head'), may hold values from 327.68 to 6717.44
- down_weight: float32 [2048, 512], P('head', 'seq'), may hold values from -0.26516504 to 0.26516504
- down_first: float32 [2048, 512], P('head', 'seq'), may hold values from -320 to 320
- down_second: float32 [2048, 512], P('head', 'seq'), may hold values from 851.968 to 17203.2
- norm_params: float32 [4, 512], P(None, 'seq'), may hold values from -1 to 1.8, as said below
- norm_first: float32 [4, 512], P(None, 'seq'), may hold values from -768 to 768
- norm_second: float32 [4, 512], P(None, 'seq'), may hold values from 5406.72 to 108134.4
Outputs:
- block_out: bfloat16 [16384, 512], P('seq')
- input_grad: float32 [16384, 512], P('seq')
- qkv_grad: float32 [3, 512, 512], P(None, 'seq', 'head')
- qkv_first_new: float32 [3, 512, 512], P(None, 'seq', 'head')
- qkv_second_new: float32 [3, 512, 512], P(None, 'seq', 'head')
- qkv_new: float32 [3, 512, 512], P(None, 'seq', 'head')
- qkv_copy: bfloat16 [3, 512, 512], P(None, 'seq', 'head')
- out_grad: float32 [512, 512], P('head', 'seq')
- out_first_new: float32 [512, 512], P('head', 'seq')
- out_second_new: float32 [512, 512], P('head', 'seq')
- out_new: float32 [512, 512], P('head', 'seq')
- out_copy: bfloat16 [512, 512], P('head', 'seq')
- up_grad: float32 [512, 2048], P('seq', 'head')
- up_first_new: float32 [512, 2048], P('seq', 'head')
- up_second_new: float32 [512, 2048], P('seq', 'head')
- up_new: float32 [512, 2048], P('seq', 'head')
- up_copy: bfloat16 [512, 2048], P('seq', 'head')
- down_grad: float32 [2048, 512], P('head', 'seq')
- down_first_new: float32 [2048, 512], P('head', 'seq')
- down_second_new: float32 [2048, 512], P('head', 'seq')
- down_new: float32 [2048, 512], P('head', 'seq')
- down_copy: bfloat16 [2048, 512], P('head', 'seq')
- norm_grad: float32 [4, 512], P(None, 'seq')
- norm_first_new: float32 [4, 512], P(None, 'seq')
- norm_second_new: float32 [4, 512], P(None, 'seq')
- norm_new: float32 [4, 512], P(None, 'seq')
- norm_copy: bfloat16 [4, 512], P(None, 'seq')
- norms: float32 [5, 2], replicated
The draws below stay inside these ranges and needn't reach their ends.
Inputs may be any that keep to these rules, and one draw needn't show every extreme that they name: frames of each clip, summing to 256; the longest clip has exactly 16. `norm_params`: gains positive, shifts of either sign.
All inputs are finite; a program needn't handle non-finite values.
Results may differ from the reference program's by a relative error of at most 0.012.
The reference program's roundings to bfloat16 on the way count: a program that leaves them out, or rounds other values in their place, can miss the bound.
Values may be sent and summed in bfloat16 or wider, within the bound.
A program may use at most 320 MiB of HBM per device.

```python
import math
import jax
import jax.numpy as jnp
import numpy as np
from jax import lax

D = 512
HEADS = 8
HEAD_DIM = 64
FF = 2048
FRAME_TOKENS = 64
MOST_FRAMES = 16
STEP = 5
TOK_DEV = 2048
TOKENS = 16384
FRAMES_ALL = 256
CLIPS = 32


def along_ramp(shape, dim, start, finish):
    count = shape[dim]
    places = jax.lax.broadcasted_iota(jnp.float32, shape, dim) / jnp.float32(max(count - 1, 1))
    return start * (finish / start) ** places


def ramped_weight(key, shape, dim, fan_in, start, finish):
    values = jnp.clip(jax.random.normal(key, shape, jnp.float32), -6.0, 6.0)
    return values * fan_in ** (-0.5) * along_ramp(shape, dim, start, finish)


def ramped_square(key, shape, dim, base, start, finish):
    spread = jnp.exp(jax.random.uniform(key, shape, jnp.float32, -0.6931, 0.6931))
    return base * spread * along_ramp(shape, dim, start, finish)


def draw_qkv_weight(key, part):
    key = jax.random.fold_in(key, 11)
    return ramped_weight(key, (3, D, D), 1, D, 0.5, 1.5)


def draw_out_weight(key, part):
    key = jax.random.fold_in(key, 12)
    return ramped_weight(key, (D, D), 1, D // 32, 0.5, 1.5)


def draw_up_weight(key, part):
    key = jax.random.fold_in(key, 13)
    return ramped_weight(key, (D, FF), 0, D, 0.5, 1.5)


def draw_down_weight(key, part):
    key = jax.random.fold_in(key, 14)
    return ramped_weight(key, (FF, D), 1, FF, 0.5, 1.5)


def draw_qkv_second(key, part):
    key = jax.random.fold_in(key, 21)
    return ramped_square(key, (3, D, D), 1, 0.12 * TOKENS, 2.0, 0.67)


def draw_out_second(key, part):
    key = jax.random.fold_in(key, 22)
    return ramped_square(key, (D, D), 1, 0.0064 * TOKENS, 2.0, 0.67)


def draw_up_second(key, part):
    key = jax.random.fold_in(key, 23)
    return ramped_square(key, (D, FF), 0, 0.081 * TOKENS, 2.0, 0.67)


def draw_down_second(key, part):
    key = jax.random.fold_in(key, 24)
    return ramped_square(key, (FF, D), 1, 0.21 * TOKENS, 2.0, 0.67)


def draw_norm_second(key, part):
    key = jax.random.fold_in(key, 25)
    return ramped_square(key, (4, D), 1, 1.32 * TOKENS, 2.0, 0.67)


def draw_norm_params(key, part):
    key = jax.random.fold_in(key, 7)
    gain_key, shift_key = jax.random.split(key)
    gains = jax.random.uniform(gain_key, (2, D), jnp.float32, 0.9, 1.1) * along_ramp((2, D), 1, 0.6, 1.5)
    shifts = jnp.clip(0.25 * jax.random.normal(shift_key, (2, D), jnp.float32), -1.0, 1.0)
    return jnp.stack([gains[0], shifts[0], gains[1], shifts[1]])


def levels(stream_key, shape, pieces, low, top_value):
    def one(dim, shards_of):
        steps = jax.random.uniform(jax.random.fold_in(jax.random.fold_in(stream_key, 6), dim), (shards_of,), jnp.float32, low / len(pieces), top_value / len(pieces))
        return jnp.repeat(jnp.exp(steps), shape[dim] // shards_of).reshape((-1,) + (1,) * (len(shape) - dim - 1))

    gain = one(*pieces[0])
    for cut in pieces[1:]:
        gain = gain * one(*cut)
    return gain


def profile(count, total, most, skew):
    weights = [(1 << 20) // math.isqrt(rank ** skew) + 1 for rank in range(2, count + 1)]
    surplus, given = total - most - (count - 1), [1] * (count - 1)
    while surplus > 0:
        movable = [i for i in range(count - 1) if given[i] < most]
        pool, remaining = sum([weights[i] for i in movable]), surplus
        for i in movable:
            more = min(most - given[i], max(1, remaining * weights[i] // pool), surplus)
            given[i] = given[i] + more
            surplus = surplus - more
    return np.array([most] + given)


def ragged_sizes(rng, count, total, limit, lean):
    if count == 2:
        one = jax.random.randint(rng, (), max(1, total - limit), min(limit, total - 1) + 1)
        return jnp.stack([one, total - one])
    lengths = jnp.asarray(profile(count, total, limit, lean), jnp.int32)
    couples = (count - 1) // 2
    donor, receiver = lengths[1:1 + 2 * couples:2], lengths[2:2 + 2 * couples:2]
    room = jnp.minimum(donor - 1, limit - receiver)
    moved = jax.random.randint(jax.random.fold_in(rng, 1), (couples,), 0, 1 << 20) % (room + 1)
    lengths = lengths.at[1:1 + 2 * couples:2].set(donor - moved).at[2:2 + 2 * couples:2].set(receiver + moved)
    return lengths[jax.random.permutation(jax.random.fold_in(rng, 2), count)]


def gaussian(own_key, dims, scale, bound, cuts=(), held_as=jnp.bfloat16):
    entries = jax.random.normal(own_key, dims, jnp.float32) * scale
    if len(cuts) > 0:
        entries = levels(own_key, dims, cuts, -0.22, 0.18) * entries
    return jnp.clip(entries, min=-bound, max=bound).astype(held_as)


def setup_inputs(seed: int = 0) -> dict:
    key_of = jax.random.split(jax.random.key(seed), 19)
    return {
        "tokens": gaussian(key_of[0], (TOKENS, D), 1.0, 6.0, ((0, 8),)),
        "cotangent": gaussian(key_of[1], (TOKENS, D), 1.0, 6.0, ((0, 8),)),
        "frames": ragged_sizes(key_of[2], CLIPS, FRAMES_ALL, MOST_FRAMES, 1).astype(jnp.int32),
        "qkv_weight": draw_qkv_weight(jax.random.fold_in(key_of[18], 71), 0),
        "qkv_first": gaussian(key_of[4], (3, D, D), (0.3 * TOKENS ** 0.5), 224.0, ((1, 8), (2, 4)), jnp.float32),
        "qkv_second": draw_qkv_second(jax.random.fold_in(key_of[18], 71), 0),
        "out_weight": draw_out_weight(jax.random.fold_in(key_of[18], 71), 0),
        "out_first": gaussian(key_of[7], (D, D), (0.07 * TOKENS ** 0.5), 56.0, ((0, 4), (1, 8)), jnp.float32),
        "out_second": draw_out_second(jax.random.fold_in(key_of[18], 71), 0),
        "up_weight": draw_up_weight(jax.random.fold_in(key_of[18], 71), 0),
        "up_first": gaussian(key_of[10], (D, FF), (0.25 * TOKENS ** 0.5), 192.0, ((0, 8), (1, 4)), jnp.float32),
        "up_second": draw_up_second(jax.random.fold_in(key_of[18], 71), 0),
        "down_weight": draw_down_weight(jax.random.fold_in(key_of[18], 71), 0),
        "down_first": gaussian(key_of[13], (FF, D), (0.4 * TOKENS ** 0.5), 320.0, ((0, 4), (1, 8)), jnp.float32),
        "down_second": draw_down_second(jax.random.fold_in(key_of[18], 71), 0),
        "norm_params": draw_norm_params(jax.random.fold_in(key_of[18], 71), 0),
        "norm_first": gaussian(key_of[16], (4, D), (TOKENS ** 0.5), 768.0, ((1, 8),), jnp.float32),
        "norm_second": draw_norm_second(jax.random.fold_in(key_of[18], 71), 0),
    }


@jax.custom_vjp
def low(v):
    return lax.optimization_barrier(v.astype(jnp.bfloat16)).astype(jnp.float32)

@jax.custom_vjp
def low_back(v):
    return v

def low_keep(v):
    return (low(v), None)

def low_pass(kept, grad):
    return (grad,)

def back_keep(v):
    return (v, None)

def back_low(kept, grad):
    return (low(grad),)
low.defvjp(low_keep, low_pass)
low_back.defvjp(back_keep, back_low)
EPS_NORM = 1e-05
BETA_ONE = 0.5
BETA_TWO = 0.6
RATE = 0.3
DECAY = 0.01
EPS_ADAM = 1e-06
MASKED = -1e+30
PRECISE = lax.Precision.HIGHEST

def rounded_both(values):
    return low_back(low(values))

def layer_norm(values, gain_row, shift_row):
    average = lax.optimization_barrier(jnp.mean(values, axis=-1, keepdims=True))
    centered = values - average
    variance = lax.optimization_barrier(jnp.mean(centered * centered, axis=-1, keepdims=True))
    return centered * lax.rsqrt(variance + EPS_NORM) * gain_row + shift_row

def clip_numbers(frames):
    clip_ends = jnp.cumsum(frames).astype(jnp.int32)
    frame_index = jnp.arange(TOKENS, dtype=jnp.int32) // FRAME_TOKENS
    return lax.optimization_barrier(jnp.sum((frame_index[:, None] >= clip_ends[None, :]).astype(jnp.int32), axis=1)).astype(jnp.int32)

def forward(inputs, qkv_weight, out_weight, up_weight, down_weight, norm_params, clip_ids):
    gains = low(norm_params)
    first = layer_norm(inputs, gains[0], gains[1])
    projected = jnp.einsum('td,sde->ste', low(first), low(qkv_weight), precision=PRECISE)
    queries = rounded_both(projected[0]).reshape(TOKENS, HEADS, HEAD_DIM)
    keys_all = rounded_both(projected[1]).reshape(TOKENS, HEADS, HEAD_DIM)
    values_all = rounded_both(projected[2]).reshape(TOKENS, HEADS, HEAD_DIM)
    window = MOST_FRAMES * FRAME_TOKENS
    span = window + TOK_DEV
    padding = jnp.zeros((window, HEADS, HEAD_DIM), jnp.float32)
    padded_keys = jnp.concatenate([padding, keys_all], axis=0)
    padded_values = jnp.concatenate([padding, values_all], axis=0)
    padded_clips = jnp.concatenate([jnp.full((window,), -1, jnp.int32), clip_ids]).astype(jnp.int32)
    score_scale = HEAD_DIM ** (-0.5)

    @jax.checkpoint
    def attend(first_row):
        block_queries = lax.dynamic_slice_in_dim(queries, first_row, TOK_DEV, 0)
        block_keys = lax.dynamic_slice_in_dim(padded_keys, first_row, span, 0)
        block_values = lax.dynamic_slice_in_dim(padded_values, first_row, span, 0)
        query_clips = lax.dynamic_slice_in_dim(clip_ids, first_row, TOK_DEV, 0)
        key_clips = lax.dynamic_slice_in_dim(padded_clips, first_row, span, 0)
        query_frames = (first_row + jnp.arange(TOK_DEV, dtype=jnp.int32)) // FRAME_TOKENS
        key_frames = (first_row - window + jnp.arange(span, dtype=jnp.int32)) // FRAME_TOKENS
        allowed = (query_clips[:, None] == key_clips[None, :]) & (key_frames[None, :] <= query_frames[:, None])
        scores = low_back(score_scale * jnp.einsum('qhd,khd->hqk', block_queries, block_keys, precision=PRECISE))
        masked = jnp.where(allowed[None], scores, MASKED)
        highest = lax.optimization_barrier(jnp.max(masked, axis=-1, keepdims=True))
        log_total = highest + jnp.log(lax.optimization_barrier(jnp.sum(jnp.exp(masked - highest), axis=-1, keepdims=True)))
        probability = low(jnp.exp(masked - log_total))
        return jnp.einsum('hqk,khd->qhd', probability, block_values, precision=PRECISE)
    starts = jnp.arange(TOKENS // TOK_DEV, dtype=jnp.int32) * TOK_DEV
    attended = lax.map(attend, starts).reshape(TOKENS, HEADS * HEAD_DIM)
    attn_out = low_back(jnp.dot(rounded_both(attended), low(out_weight), precision=PRECISE))
    resid = inputs + attn_out
    second = layer_norm(resid, gains[2], gains[3])
    upper = low_back(jnp.dot(low(second), low(up_weight), precision=PRECISE))
    active = low(jax.nn.gelu(upper, approximate=True))
    mlp_out = low_back(jnp.dot(active, low(down_weight), precision=PRECISE))
    return resid + mlp_out

def lamb_step(master, moment, square, gradient):
    new_first = BETA_ONE * moment + (1.0 - BETA_ONE) * gradient
    new_second = BETA_TWO * square + (1.0 - BETA_TWO) * gradient * gradient
    direction = new_first / (1.0 - BETA_ONE ** STEP) / (jnp.sqrt(new_second / (1.0 - BETA_TWO ** STEP)) + EPS_ADAM) + DECAY * master
    weight_norm = jnp.sqrt(jnp.sum(master * master))
    update_norm = jnp.sqrt(jnp.sum(direction * direction))
    new_master = master - RATE * (weight_norm / update_norm) * direction
    return (new_first, new_second, new_master, weight_norm, update_norm)

def reference(tokens, cotangent, frames, qkv_weight, qkv_first, qkv_second, out_weight, out_first, out_second, up_weight, up_first, up_second, down_weight, down_first, down_second, norm_params, norm_first, norm_second):
    clip_ids = clip_numbers(frames)
    inputs = tokens.astype(jnp.float32)

    def layer(values, weight_a, weight_b, weight_c, weight_d, weight_e):
        return forward(values, weight_a, weight_b, weight_c, weight_d, weight_e, clip_ids)
    output, pullback = jax.vjp(layer, inputs, qkv_weight, out_weight, up_weight, down_weight, norm_params)
    grads = pullback(cotangent.astype(jnp.float32))
    masters = (qkv_weight, out_weight, up_weight, down_weight, norm_params)
    moments = (qkv_first, out_first, up_first, down_first, norm_first)
    squares = (qkv_second, out_second, up_second, down_second, norm_second)
    result = []
    weight_norms = []
    update_norms = []
    for master, moment, square, gradient in zip(masters, moments, squares, grads[1:]):
        new_first, new_second, new_master, weight_norm, update_norm = lamb_step(master, moment, square, gradient)
        result.append((gradient, new_first, new_second, new_master, new_master.astype(jnp.bfloat16)))
        weight_norms.append(weight_norm)
        update_norms.append(update_norm)
    norms = jnp.stack([jnp.stack(weight_norms), jnp.stack(update_norms)], axis=1)
    return (output.astype(jnp.bfloat16), grads[0], result[0][0], result[0][1], result[0][2], result[0][3], result[0][4], result[1][0], result[1][1], result[1][2], result[1][3], result[1][4], result[2][0], result[2][1], result[2][2], result[2][3], result[2][4], result[3][0], result[3][1], result[3][2], result[3][3], result[3][4], result[4][0], result[4][1], result[4][2], result[4][3], result[4][4], norms)
```

```python
import functools

import jax
import jax.numpy as jnp
from jax import lax
from jax.experimental import pallas as pl
from jax.experimental.pallas import tpu as pltpu
from jax.sharding import PartitionSpec as P

HEAD_DIM = 64
FRAME_TOKENS = 64
MOST_FRAMES = 16
STEP = 5

EPS_NORM = 1e-05
BETA_ONE = 0.5
BETA_TWO = 0.6
RATE = 0.3
DECAY = 0.01
EPS_ADAM = 1e-06
MASKED = -1e30

MESH = pl.DeviceIdType.MESH
F32 = jnp.float32
BF16 = jnp.bfloat16
TILE = 128
KEYS = MOST_FRAMES * FRAME_TOKENS + TILE
ROWS = 64

DOWN, UP, OUT, QKV = range(4)


def nn(a, b):
    return lax.dot_general(a, b, (((1,), (0,)), ((), ())), preferred_element_type=F32)


def nt(a, b):
    return lax.dot_general(a, b, (((1,), (1,)), ((), ())), preferred_element_type=F32)


def tn(a, b):
    return lax.dot_general(a, b, (((0,), (0,)), ((), ())), preferred_element_type=F32)


def normalize(values):
    average = jnp.mean(values, axis=-1, keepdims=True)
    centered = values - average
    variance = jnp.mean(centered * centered, axis=-1, keepdims=True)
    inverse = lax.rsqrt(variance + EPS_NORM)
    return centered * inverse, inverse


def norm_back(gradient, normed, inverse, gain_row):
    scaled = gradient * gain_row
    return inverse * (
        scaled
        - jnp.mean(scaled, axis=-1, keepdims=True)
        - normed * jnp.mean(scaled * normed, axis=-1, keepdims=True)
    )


def gelu_both(inner):
    root = 0.7978845608028654
    cube = 0.044715
    square = inner * inner
    curved = jnp.tanh(root * inner * (1.0 + cube * square))
    half = 0.5 * (1.0 + curved)
    value = inner * half
    slope = half + 0.5 * inner * (1.0 - curved * curved) * (root * (1.0 + 3.0 * cube * square))
    return value, slope


def lamb_direction(master, moment, square, gradient):
    new_first = BETA_ONE * moment + (1.0 - BETA_ONE) * gradient
    new_second = BETA_TWO * square + (1.0 - BETA_TWO) * gradient * gradient
    direction = (
        new_first
        / (1.0 - BETA_ONE**STEP)
        / (jnp.sqrt(new_second / (1.0 - BETA_TWO**STEP)) + EPS_ADAM)
        + DECAY * master
    )
    return new_first, new_second, direction


def flat(block):
    pieces, rows, columns = block.shape
    if rows % 16:
        block = block.astype(F32)
    return block.reshape(pieces * rows, columns).astype(BF16)


def cut(matrix, pieces):
    rows, columns = matrix.shape
    return matrix.reshape(pieces, rows // pieces, columns).astype(BF16)


def layer_kernel(
    seq_count,
    head_count,
    tok,
    cot,
    frames,
    qkv_w,
    out_w,
    up_w,
    down_w,
    norm_w,
    qkv_m,
    qkv_u,
    out_m,
    out_u,
    up_m,
    up_u,
    down_m,
    down_u,
    norm_m,
    norm_u,
    block_out,
    input_grad,
    qkv_g,
    out_g,
    up_g,
    down_g,
    norm_g,
    squares,
    w_qkv,
    w_out,
    w_up,
    w_down,
    norm_parts,
    norm_full,
    ext,
    cot_own,
    h1,
    h1_t,
    q_all,
    k_all,
    v_all,
    prob,
    attended,
    resid,
    h2,
    h2_t,
    cot_t,
    mlp,
    dh2,
    wide_a,
    wide_b,
    act,
    dup,
    low_out,
    dr_low,
    d_att,
    dk_acc,
    dv_acc,
    dq_all,
    dk_all,
    dv_all,
    dh1,
    halo_low,
    halo_in,
    g_down,
    g_up,
    g_out,
    g_qkv,
    c_down,
    c_up,
    c_out,
    c_qkv,
    x_down,
    x_up,
    x_out,
    x_qkv,
    s_down,
    s_up,
    s_out,
    s_qkv,
    norm_sum,
    norm_c,
    norm_x,
    norm_s,
    sq_c,
    sq_x,
    sq_s,
    loc_sem,
    halo_sem,
    normp_sem,
    ags_send,
    ags_recv,
    agx_sem,
    agc_sem,
    rsc_sem,
    rsx_sem,
    rss_send,
    rss_recv,
    small_sem,
    norm_s_send,
    norm_s_recv,
    sq_s_send,
    sq_s_recv,
    out_sem,
    back_sem,
):
    S, H = seq_count, head_count
    T = cot_own.shape[0]
    R = qkv_w.shape[1]
    s = lax.axis_index("seq")
    h = lax.axis_index("head")
    hx = lax.div(h, 2)
    hc = lax.rem(h, 2)
    other_core = (s, h + 1 - 2 * hc)
    other_x = (s, lax.rem(h + 2, H))
    mine = hc * 2 + hx
    near = hc * 2 + 1 - hx
    mine_pair = hc * 2
    other_pair = (1 - hc) * 2
    total = S * H
    place = s * H + h

    def device_at(number):
        number = lax.rem(number + total, total)
        return (lax.div(number, H), lax.rem(number, H))

    def seq_peer(i):
        return lax.rem(s + i, S)

    def remote(src, dst, send, recv, device):
        return pltpu.make_async_remote_copy(
            src_ref=src, dst_ref=dst, send_sem=send, recv_sem=recv, device_id=device, device_id_type=MESH
        )

    def rows_of(index, count):
        return pl.ds(pl.multiple_of(index * count, count), count)

    cot_copy = pltpu.make_async_copy(cot.at[rows_of(h, T)], cot_own, loc_sem.at[3])
    cot_copy.start()

    def ext_copy(chunk):
        return pltpu.make_async_copy(
            tok.at[rows_of(jnp.maximum(h - 2 + chunk, 0), T)], ext.at[pl.ds(chunk * T, T)], loc_sem.at[chunk]
        )

    for chunk in range(3):

        @pl.when(h - 2 + chunk >= 0)
        def _():
            ext_copy(chunk).start()

    for t in range(3):
        w_qkv[mine, s, :, t * 128 : (t + 1) * 128] = qkv_w[t].astype(BF16)
    w_out[mine, s] = out_w[...].astype(BF16)
    w_up[mine, s] = up_w[...].astype(BF16)
    w_down[mine, s] = down_w[...].astype(BF16)
    norm_full[...] = jnp.zeros_like(norm_full)
    norm_full[0:4, 0:R] = norm_w[...].astype(BF16).astype(F32)
    norm_parts[s] = pltpu.roll(norm_full[...], s * R, axis=1)

    barrier = pltpu.get_barrier_semaphore()

    def greet(i, carry):
        pl.semaphore_signal(barrier, inc=1, device_id=(seq_peer(i), h), device_id_type=MESH)
        return carry

    lax.fori_loop(1, S, greet, 0)
    for device in (other_core, other_x, device_at(place + 1), device_at(place + 2)):
        pl.semaphore_signal(barrier, inc=1, device_id=device, device_id_type=MESH)
    pl.semaphore_wait(barrier, S - 1 + 4)

    kinds_w = {DOWN: w_down, UP: w_up, OUT: w_out, QKV: w_qkv}

    def gather_seq(kind, i):
        buffer = kinds_w[kind]
        return remote(
            buffer.at[mine, s], buffer.at[mine, s], ags_send.at[kind, i], ags_recv.at[kind, s], (seq_peer(i), h)
        )

    def gather_seq_start(kind):
        def one(i, carry):
            gather_seq(kind, i).start()
            return carry

        lax.fori_loop(1, S, one, 0)

    def gather_seq_wait(kind):
        buffer = kinds_w[kind]

        def one(i, carry):
            peer = seq_peer(i)
            remote(
                buffer.at[mine, peer],
                buffer.at[mine, peer],
                ags_send.at[kind, i],
                ags_recv.at[kind, peer],
                (peer, h),
            ).wait_recv()
            return carry

        lax.fori_loop(1, S, one, 0)

    def gather_x(kind, group):
        buffer = kinds_w[kind]
        return remote(buffer.at[group], buffer.at[group], agx_sem.at[0, kind], agx_sem.at[1, kind], other_x)

    def gather_core(kind, pair):
        buffer = kinds_w[kind]
        return remote(
            buffer.at[pl.ds(pair, 2)],
            buffer.at[pl.ds(pair, 2)],
            agc_sem.at[0, kind],
            agc_sem.at[1, kind],
            other_core,
        )

    def norm_part(i):
        return remote(
            norm_parts.at[s], norm_parts.at[s], normp_sem.at[0, i], normp_sem.at[1, s], (seq_peer(i), h)
        )

    def norm_part_start(i, carry):
        norm_part(i).start()
        return carry

    lax.fori_loop(1, S, norm_part_start, 0)
    gather_seq_start(QKV)

    def halo_copy(chunk):
        return remote(
            tok.at[rows_of(jnp.minimum(h - 2 + chunk + H, H - 1), T)],
            ext.at[pl.ds(chunk * T, T)],
            halo_sem.at[0, chunk],
            halo_sem.at[1, chunk],
            (seq_peer(1), h),
        )

    for chunk in range(2):

        @pl.when(h - 2 + chunk < 0)
        def _():
            halo_copy(chunk).start()

    for kind in (OUT, UP, DOWN):
        gather_seq_start(kind)

    first_frame = place * (T // FRAME_TOKENS)
    own_frames = T // FRAME_TOKENS

    def clip_step(c, carry):
        end, lows = carry
        start = end
        end = start + frames[c]
        lows = tuple(
            jnp.where((start <= first_frame + f) & (first_frame + f < end), start, lows[f])
            for f in range(own_frames)
        )
        return end, lows

    _, clip_low = lax.fori_loop(
        0, frames.shape[0], clip_step, (jnp.int32(0), tuple(jnp.int32(0) for _ in range(own_frames)))
    )

    def norm_part_wait(i, carry):
        peer = seq_peer(i)
        remote(
            norm_parts.at[peer], norm_parts.at[peer], normp_sem.at[0, i], normp_sem.at[1, peer], (peer, h)
        ).wait_recv()
        return carry

    lax.fori_loop(1, S, norm_part_wait, 0)
    norm_full[...] = lax.fori_loop(
        0, S, lambda i, carry: carry + norm_parts[i], jnp.zeros(norm_full.shape, F32)
    )

    for chunk in range(3):

        @pl.when(h - 2 + chunk >= 0)
        def _():
            ext_copy(chunk).wait()

        if chunk < 2:

            @pl.when(h - 2 + chunk < 0)
            def _():
                halo_copy(chunk).wait_recv()

    gain_one, shift_one = norm_full[0:1, :], norm_full[1:2, :]
    gain_two, shift_two = norm_full[2:3, :], norm_full[3:4, :]

    def first_norm(b, carry):
        at = rows_of(b, ROWS)
        normed, _ = normalize(ext[at, :].astype(F32))
        h1[at, :] = (normed * gain_one + shift_one).astype(BF16)
        return carry

    lax.fori_loop(0, 3 * T // ROWS, first_norm, 0)

    gather_seq_wait(QKV)
    gather_x(QKV, mine).start()
    gather_x(QKV, near).wait_recv()
    gather_core(QKV, mine_pair).start()
    for chunk in range(3):
        h1_t[:, chunk * T : (chunk + 1) * T] = h1[chunk * T : (chunk + 1) * T, :].T
    cot_copy.wait()
    cot_t[...] = cot_own[...].T
    gather_core(QKV, other_pair).wait_recv()

    def project(p, carry):
        weight = flat(w_qkv[p])
        for chunk in range(3):
            at = pl.ds(chunk * T, T)
            if chunk == 2:
                out = nn(h1[at, :], weight)
                q_all[p] = out[:, 0:128].astype(BF16) * jnp.asarray(HEAD_DIM**-0.5, BF16)
                out = out[:, 128:384]
            else:
                out = nn(h1[at, :], weight[:, 128:384])
            k_all[p, at, :] = out[:, 0:128].astype(BF16)
            v_all[p, at, :] = out[:, 128:256].astype(BF16)
        return carry

    lax.fori_loop(0, H, project, 0)

    lane = lax.broadcasted_iota(jnp.int32, (1, 128), 1)
    first_head = jnp.where(lane < HEAD_DIM, 1.0, 0.0).astype(BF16)
    second_head = jnp.where(lane < HEAD_DIM, 0.0, 1.0).astype(BF16)
    feature = lax.broadcasted_iota(jnp.int32, (128, TILE), 0)

    def two_heads(block):
        return jnp.concatenate([block * first_head, block * second_head], axis=0)

    def own_halves(block):
        return jnp.where(feature < HEAD_DIM, block[:, 0:TILE], block[:, TILE : 2 * TILE])

    key_frames = KEYS // FRAME_TOKENS

    def bias_of(i):
        query_lane = lax.broadcasted_iota(jnp.int32, (key_frames, 1, 2 * TILE), 2)
        later = lax.rem(query_lane, TILE) >= FRAME_TOKENS
        low = jnp.where(later, clip_low[2 * i + 1], clip_low[2 * i])
        high = first_frame + 2 * i + later.astype(jnp.int32)
        key_frame = (
            first_frame
            - MOST_FRAMES
            + 2 * i
            + lax.broadcasted_iota(jnp.int32, (key_frames, 1, 2 * TILE), 0)
        )
        return jnp.where((key_frame >= low) & (key_frame <= high), 0.0, MASKED).astype(F32)

    biases = [bias_of(i) for i in range(T // TILE)]

    def attend(p, carry):
        for i in range(T // TILE):
            own = pl.ds(i * TILE, TILE)
            window = pl.ds(i * TILE, KEYS)
            queries = two_heads(q_all[p, own, :])
            scores = nt(k_all[p, window, :], queries)
            scores = (scores.reshape(key_frames, FRAME_TOKENS, 2 * TILE) + biases[i]).reshape(KEYS, 2 * TILE)
            highest = jnp.max(scores, axis=0, keepdims=True)
            powers = jnp.exp(scores - highest)
            inverse = 1.0 / jnp.sum(powers, axis=0, keepdims=True)
            low = (powers * inverse).astype(BF16)
            prob[p, i] = low
            mixed = own_halves(tn(v_all[p, window, :], low))
            attended[p, own, :] = mixed.T.astype(BF16)
        return carry

    lax.fori_loop(0, 1, attend, 0)
    gather_seq_wait(OUT)
    gather_x(OUT, mine).start()
    lax.fori_loop(1, 2, attend, 0)
    gather_x(OUT, near).wait_recv()
    gather_core(OUT, mine_pair).start()
    gather_seq_wait(UP)
    gather_x(UP, mine).start()
    lax.fori_loop(2, 3, attend, 0)
    gather_seq_wait(DOWN)
    gather_x(DOWN, mine).start()
    lax.fori_loop(3, 4, attend, 0)
    gather_x(UP, near).wait_recv()
    gather_core(UP, mine_pair).start()
    gather_core(OUT, other_pair).wait_recv()

    acc = nt(attended[0], flat(w_out[0]))
    for p in range(1, H):
        acc = acc + nt(attended[p], flat(w_out[p]))
    resid[...] = acc

    def second_norm(b, carry):
        at = rows_of(b, ROWS)
        whole = ext[pl.ds(pl.multiple_of(2 * T + b * ROWS, ROWS), ROWS), :].astype(F32) + resid[at, :]
        resid[at, :] = whole
        normed, _ = normalize(whole)
        h2[at, :] = (normed * gain_two + shift_two).astype(BF16)
        return carry

    lax.fori_loop(0, T // ROWS, second_norm, 0)
    h2_t[...] = h2[...].T
    gather_x(DOWN, near).wait_recv()
    gather_core(DOWN, mine_pair).start()
    gather_core(UP, other_pair).wait_recv()
    gather_core(DOWN, other_pair).wait_recv()

    mlp[...] = jnp.zeros_like(mlp)
    dh2[...] = jnp.zeros_like(dh2)

    def hidden(c, carry):
        up_block = flat(w_up[c])
        down_block = flat(w_down[c])
        wide_a[...] = nn(h2[...], up_block)
        wide_b[...] = nn(cot_own[...], down_block)

        def pointwise(b, inner):
            at = rows_of(b, ROWS)
            value, slope = gelu_both(wide_a[at, :])
            act[at, :] = value.astype(BF16)
            dup[at, :] = (wide_b[at, :] * slope).astype(BF16)
            return inner

        lax.fori_loop(0, T // ROWS, pointwise, 0)
        mlp[...] += nt(act[...], down_block)
        dh2[...] += nt(dup[...], up_block)
        g_down[c] = cut(nn(cot_t[...], act[...]), S)
        g_up[c] = cut(nn(h2_t[...], dup[...]), S)
        return carry

    lax.fori_loop(0, H, hidden, 0)

    grads = {DOWN: g_down, UP: g_up, OUT: g_out, QKV: g_qkv}
    from_core = {DOWN: c_down, UP: c_up, OUT: c_out, QKV: c_qkv}
    from_x = {DOWN: x_down, UP: x_up, OUT: x_out, QKV: x_qkv}
    from_seq = {DOWN: s_down, UP: s_up, OUT: s_out, QKV: s_qkv}

    def scatter_core(kind):
        return remote(
            grads[kind].at[pl.ds(other_pair, 2)],
            from_core[kind],
            rsc_sem.at[0, kind],
            rsc_sem.at[1, kind],
            other_core,
        )

    def scatter_core_sum(kind):
        scatter_core(kind).wait_recv()
        for gx in range(2):
            group = mine_pair + gx

            def add(b, carry):
                grads[kind][group, b] = (
                    grads[kind][group, b].astype(F32) + from_core[kind][gx, b].astype(F32)
                ).astype(BF16)
                return carry

            lax.fori_loop(0, S, add, 0)

    def scatter_x(kind):
        return remote(
            grads[kind].at[near], from_x[kind], rsx_sem.at[0, kind], rsx_sem.at[1, kind], other_x
        )

    def scatter_x_sum(kind):
        scatter_x(kind).wait_recv()

        def add(b, carry):
            grads[kind][mine, b] = (
                grads[kind][mine, b].astype(F32) + from_x[kind][b].astype(F32)
            ).astype(BF16)
            return carry

        lax.fori_loop(0, S, add, 0)

    def scatter_seq(kind, i):
        peer = seq_peer(i)
        return remote(
            grads[kind].at[mine, peer],
            from_seq[kind].at[s],
            rss_send.at[kind, i],
            rss_recv.at[kind, s],
            (peer, h),
        )

    def scatter_seq_start(kind):
        def one(i, carry):
            scatter_seq(kind, i).start()
            return carry

        lax.fori_loop(1, S, one, 0)

    def scatter_seq_sum(kind):
        landed = from_seq[kind]

        def one(i, carry):
            peer = seq_peer(i)
            remote(
                grads[kind].at[mine, peer],
                landed.at[peer],
                rss_send.at[kind, i],
                rss_recv.at[kind, peer],
                (peer, h),
            ).wait_recv()
            return carry

        lax.fori_loop(1, S, one, 0)

        def add(i, carry):
            return carry + landed[seq_peer(i)].astype(F32)

        return lax.fori_loop(1, S, add, grads[kind][mine, s].astype(F32))

    scatter_core(DOWN).start()
    scatter_core(UP).start()

    def finish_rows(target, low, at_sem):
        def slab(head):
            return target.at[rows_of(head, T)]

        keep = pltpu.make_async_copy(low, slab(h), out_sem.at[at_sem, 0])
        to_x = remote(low, slab(h), out_sem.at[at_sem, 1], out_sem.at[at_sem, 2], other_x)
        to_core = remote(low, slab(h), out_sem.at[at_sem, 3], out_sem.at[at_sem, 4], other_core)
        near_head = other_x[1]
        passed = remote(
            slab(near_head), slab(near_head), out_sem.at[at_sem, 5], out_sem.at[at_sem, 6], other_core
        )
        return keep, to_x, to_core, passed

    def sum_out(b, carry):
        at = rows_of(b, ROWS)
        low_out[at, :] = (resid[at, :] + mlp[at, :]).astype(BF16)
        return carry

    lax.fori_loop(0, T // ROWS, sum_out, 0)
    out_copies = finish_rows(block_out, low_out, 0)
    for copy in out_copies[:3]:
        copy.start()

    def second_back(b, carry):
        gain_sum, shift_sum = carry
        at = rows_of(b, ROWS)
        normed, inverse = normalize(resid[at, :])
        grad = dh2[at, :]
        mixed = cot_own[at, :].astype(F32) + norm_back(grad, normed, inverse, gain_two)
        resid[at, :] = mixed
        dr_low[at, :] = mixed.astype(BF16)
        gain_sum = gain_sum + jnp.sum(grad * normed, axis=0, keepdims=True)
        shift_sum = shift_sum + jnp.sum(grad, axis=0, keepdims=True)
        return gain_sum, shift_sum

    zero_row = jnp.zeros((1, resid.shape[1]), F32)
    gain_two_grad, shift_two_grad = lax.fori_loop(0, T // ROWS, second_back, (zero_row, zero_row))

    h2_t[...] = dr_low[...].T
    for p in range(H):
        d_att[p] = nn(dr_low[...], flat(w_out[p])).astype(BF16)
        g_out[p] = cut(nn(h2_t[...], attended[p]), S)
    scatter_core(OUT).start()
    scatter_core_sum(DOWN)
    scatter_x(DOWN).start()
    scatter_core_sum(UP)
    scatter_x(UP).start()

    def attend_back(p, carry):
        dk_acc[...] = jnp.zeros_like(dk_acc)
        dv_acc[...] = jnp.zeros_like(dv_acc)
        for i in range(T // TILE):
            own = pl.ds(i * TILE, TILE)
            window = pl.ds(i * TILE, KEYS)
            grad = d_att[p, own, :]
            stacked = two_heads(grad)
            queries = two_heads(q_all[p, own, :])
            products = (grad.astype(F32) * attended[p, own, :].astype(F32)).T
            delta = jnp.concatenate(
                [
                    jnp.sum(products[0:HEAD_DIM], axis=0, keepdims=True),
                    jnp.sum(products[HEAD_DIM:128], axis=0, keepdims=True),
                ],
                axis=1,
            )
            keys = k_all[p, window, :]
            low = prob[p, i]
            d_prob = nt(v_all[p, window, :], stacked)
            d_scores = (low.astype(F32) * (d_prob - delta)).astype(BF16)
            dv_acc[window, :] += nn(low, stacked)
            dk_acc[window, :] += nn(d_scores, queries)
            mixed = own_halves(tn(keys, d_scores)) * (HEAD_DIM**-0.5)
            dq_all[p, own, :] = mixed.T.astype(BF16)
        dk_all[p] = dk_acc[...].astype(BF16)
        dv_all[p] = dv_acc[...].astype(BF16)
        columns = [
            nn(h1_t[:, 2 * T : 3 * T], dq_all[p]),
            nn(h1_t[...], dk_all[p]),
            nn(h1_t[...], dv_all[p]),
        ]
        g_qkv[p] = cut(jnp.concatenate(columns, axis=1), S)
        return carry

    lax.fori_loop(0, 1, attend_back, 0)
    scatter_core_sum(OUT)
    scatter_x(OUT).start()
    scatter_x_sum(DOWN)
    scatter_seq_start(DOWN)
    lax.fori_loop(1, 2, attend_back, 0)
    scatter_x_sum(UP)
    scatter_seq_start(UP)
    lax.fori_loop(2, 3, attend_back, 0)
    scatter_x_sum(OUT)
    scatter_seq_start(OUT)
    out_copies[1].wait_recv()
    out_copies[3].start()
    lax.fori_loop(3, 4, attend_back, 0)
    scatter_core(QKV).start()

    dh1[...] = jnp.zeros_like(dh1)

    def back_halo(p, carry):
        weight = flat(w_qkv[p])
        for chunk in range(2):
            at = pl.ds(chunk * T, T)
            dh1[at, :] += nt(dk_all[p, at, :], weight[:, 128:256]) + nt(dv_all[p, at, :], weight[:, 256:384])
        return carry

    lax.fori_loop(0, H, back_halo, 0)

    def round_halo(b, carry):
        at = rows_of(b, ROWS)
        halo_low[at, :] = dh1[at, :].astype(BF16)
        return carry

    lax.fori_loop(0, 2 * T // ROWS, round_halo, 0)

    def back_copy(chunk):
        return remote(
            halo_low.at[pl.ds(chunk * T, T)],
            halo_in.at[chunk],
            back_sem.at[0, chunk],
            back_sem.at[1, chunk],
            device_at(place - 2 + chunk),
        )

    for chunk in range(2):
        back_copy(chunk).start()
    scatter_core_sum(QKV)
    scatter_x(QKV).start()

    def back_own(p, carry):
        weight = flat(w_qkv[p])
        at = pl.ds(2 * T, T)
        dh1[at, :] += (
            nt(dq_all[p], weight[:, 0:128])
            + nt(dk_all[p, at, :], weight[:, 128:256])
            + nt(dv_all[p, at, :], weight[:, 256:384])
        )
        return carry

    lax.fori_loop(0, H, back_own, 0)

    def first_sums(b, carry):
        gain_sum, shift_sum = carry
        at = rows_of(b, ROWS)
        normed, _ = normalize(ext[at, :].astype(F32))
        grad = dh1[at, :]
        return (
            gain_sum + jnp.sum(grad * normed, axis=0, keepdims=True),
            shift_sum + jnp.sum(grad, axis=0, keepdims=True),
        )

    gain_one_grad, shift_one_grad = lax.fori_loop(0, 3 * T // ROWS, first_sums, (zero_row, zero_row))
    norm_sum[...] = jnp.concatenate(
        [gain_one_grad, shift_one_grad, gain_two_grad, shift_two_grad, jnp.zeros((4, zero_row.shape[1]), F32)],
        axis=0,
    )
    norm_to_core = remote(norm_sum, norm_c, small_sem.at[0], small_sem.at[1], other_core)
    norm_to_core.start()
    norm_to_core.wait()
    norm_sum[...] += norm_c[...]
    norm_to_x = remote(norm_sum, norm_x, small_sem.at[2], small_sem.at[3], other_x)
    norm_to_x.start()
    scatter_x_sum(QKV)
    scatter_seq_start(QKV)
    norm_to_x.wait()
    norm_sum[...] += norm_x[...]

    def norm_seq(i):
        return remote(
            norm_sum, norm_s.at[s], norm_s_send.at[i], norm_s_recv.at[s], (seq_peer(i), h)
        )

    def norm_seq_start(i, carry):
        norm_seq(i).start()
        return carry

    lax.fori_loop(1, S, norm_seq_start, 0)

    for chunk in range(2):
        back_copy(chunk).wait_recv()

    def first_back(b, carry):
        at = rows_of(b, ROWS)
        below = pl.ds(pl.multiple_of(2 * T + b * ROWS, ROWS), ROWS)
        normed, inverse = normalize(ext[below, :].astype(F32))
        grad = dh1[below, :] + halo_in[0, at, :].astype(F32) + halo_in[1, at, :].astype(F32)
        dr_low[at, :] = (resid[at, :] + norm_back(grad, normed, inverse, gain_one)).astype(BF16)
        return carry

    lax.fori_loop(0, T // ROWS, first_back, 0)
    grad_copies = finish_rows(input_grad, dr_low, 1)
    for copy in grad_copies[:3]:
        copy.start()

    down_total = scatter_seq_sum(DOWN)
    down_g[...] = down_total
    up_total = scatter_seq_sum(UP)
    up_g[...] = up_total
    out_total = scatter_seq_sum(OUT)
    out_g[...] = out_total

    def sums_of(master, moment, square, gradient):
        _, _, direction = lamb_direction(master, moment, square, gradient)
        return jnp.sum(master * master), jnp.sum(direction * direction)

    down_sums = sums_of(down_w[...], down_m[...], down_u[...], down_total)
    up_sums = sums_of(up_w[...], up_m[...], up_u[...], up_total)
    out_sums = sums_of(out_w[...], out_m[...], out_u[...], out_total)

    qkv_total = scatter_seq_sum(QKV)
    weight_sum, update_sum = jnp.float32(0.0), jnp.float32(0.0)
    for t in range(3):
        part = qkv_total[:, t * 128 : (t + 1) * 128]
        qkv_g[t] = part
        sums = sums_of(qkv_w[t], qkv_m[t], qkv_u[t], part)
        weight_sum, update_sum = weight_sum + sums[0], update_sum + sums[1]
    qkv_sums = (weight_sum, update_sum)

    def norm_seq_wait(i, carry):
        peer = seq_peer(i)
        remote(norm_sum, norm_s.at[peer], norm_s_send.at[i], norm_s_recv.at[peer], (peer, h)).wait_recv()
        return carry + norm_s[peer]

    norm_total = lax.fori_loop(1, S, norm_seq_wait, norm_sum[...])
    width = norm_total.shape[1]
    norm_mine = pltpu.roll(norm_total, lax.rem(width - s * R, width), axis=1)[0:4, 0:R]
    norm_g[...] = norm_mine
    once = jnp.where(h == 0, 1.0, 0.0).astype(F32)
    norm_sums = sums_of(norm_w[...], norm_m[...], norm_u[...], norm_mine)
    norm_sums = (norm_sums[0] * once, norm_sums[1] * once)

    row = lax.broadcasted_iota(jnp.int32, (8, 128), 0)
    column = lax.broadcasted_iota(jnp.int32, (8, 128), 1)
    both = jnp.zeros((8, 128), F32)
    for number, pair in enumerate((qkv_sums, out_sums, up_sums, down_sums, norm_sums)):
        for which in range(2):
            both = jnp.where((row == number) & (column == which), pair[which], both)
    squares[...] = both

    def sq_seq(i):
        return remote(squares, sq_s.at[s], sq_s_send.at[i], sq_s_recv.at[s], (seq_peer(i), h))

    def sq_seq_start(i, carry):
        sq_seq(i).start()
        return carry

    def sq_seq_wait(i, carry):
        peer = seq_peer(i)
        remote(squares, sq_s.at[peer], sq_s_send.at[i], sq_s_recv.at[peer], (peer, h)).wait_recv()
        return carry + sq_s[peer]

    def sq_seq_sent(i, carry):
        sq_seq(i).wait_send()
        return carry

    lax.fori_loop(1, S, sq_seq_start, 0)
    both = lax.fori_loop(1, S, sq_seq_wait, both)
    lax.fori_loop(1, S, sq_seq_sent, 0)
    squares[...] = both
    sq_to_x = remote(squares, sq_x, small_sem.at[4], small_sem.at[5], other_x)
    sq_to_x.start()
    sq_to_x.wait()
    both = both + sq_x[...]
    squares[...] = both
    sq_to_core = remote(squares, sq_c, small_sem.at[6], small_sem.at[7], other_core)
    sq_to_core.start()
    sq_to_core.wait()
    squares[...] = both + sq_c[...]

    grad_copies[1].wait_recv()
    grad_copies[3].start()
    for copies in (out_copies, grad_copies):
        keep, to_x, to_core, passed = copies
        keep.wait()
        to_x.wait_send()
        to_core.wait_send()
        passed.wait_send()
        to_core.wait_recv()
        passed.wait_recv()

    for chunk in range(2):

        @pl.when(h - 2 + chunk < 0)
        def _():
            halo_copy(chunk).wait_send()

        back_copy(chunk).wait_send()
    for kind in (QKV, OUT, UP, DOWN):
        gather_x(kind, mine).wait_send()
        gather_core(kind, mine_pair).wait_send()
        scatter_core(kind).wait_send()
        scatter_x(kind).wait_send()

    def drain(i, carry):
        norm_part(i).wait_send()
        norm_seq(i).wait_send()
        for kind in (QKV, OUT, UP, DOWN):
            gather_seq(kind, i).wait_send()
            scatter_seq(kind, i).wait_send()
        return carry

    lax.fori_loop(1, S, drain, 0)


def run_layer(mesh_sizes, tok, cot, frames, weights, moments, seconds):
    S, H = mesh_sizes
    rows_dev, width = tok.shape
    T = rows_dev // H
    R = weights[0].shape[1]
    assert H == 4 and 2 * T == MOST_FRAMES * FRAME_TOKENS and R * S == width
    hidden = weights[2].shape[1]
    any_space = pl.BlockSpec(memory_space=pl.ANY)
    vmem = pl.BlockSpec(memory_space=pltpu.VMEM)
    smem = pl.BlockSpec(memory_space=pltpu.SMEM)
    dma = pltpu.SemaphoreType.DMA
    out_shape = (
        jax.ShapeDtypeStruct((rows_dev, width), BF16),
        jax.ShapeDtypeStruct((rows_dev, width), BF16),
        *[jax.ShapeDtypeStruct(w.shape, F32) for w in weights],
        jax.ShapeDtypeStruct((8, 128), F32),
    )
    cols = {DOWN: hidden, UP: hidden, OUT: 128, QKV: 384}
    order = (DOWN, UP, OUT, QKV)
    scratch = [
        *[pltpu.VMEM((H, S, R, cols[kind]), BF16) for kind in (QKV, OUT, UP, DOWN)],
        pltpu.VMEM((S, 8, width), F32),
        pltpu.VMEM((8, width), F32),
        pltpu.VMEM((3 * T, width), BF16),
        pltpu.VMEM((T, width), BF16),
        pltpu.VMEM((3 * T, width), BF16),
        pltpu.VMEM((width, 3 * T), BF16),
        pltpu.VMEM((H, T, 128), BF16),
        pltpu.VMEM((H, 3 * T, 128), BF16),
        pltpu.VMEM((H, 3 * T, 128), BF16),
        pltpu.VMEM((H, T // TILE, KEYS, 2 * TILE), BF16),
        pltpu.VMEM((H, T, 128), BF16),
        pltpu.VMEM((T, width), F32),
        pltpu.VMEM((T, width), BF16),
        pltpu.VMEM((width, T), BF16),
        pltpu.VMEM((width, T), BF16),
        pltpu.VMEM((T, width), F32),
        pltpu.VMEM((T, width), F32),
        pltpu.VMEM((T, hidden), F32),
        pltpu.VMEM((T, hidden), F32),
        pltpu.VMEM((T, hidden), BF16),
        pltpu.VMEM((T, hidden), BF16),
        pltpu.VMEM((T, width), BF16),
        pltpu.VMEM((T, width), BF16),
        pltpu.VMEM((H, T, 128), BF16),
        pltpu.VMEM((3 * T, 128), F32),
        pltpu.VMEM((3 * T, 128), F32),
        pltpu.VMEM((H, T, 128), BF16),
        pltpu.VMEM((H, 3 * T, 128), BF16),
        pltpu.VMEM((H, 3 * T, 128), BF16),
        pltpu.VMEM((3 * T, width), F32),
        pltpu.VMEM((2 * T, width), BF16),
        pltpu.VMEM((2, T, width), BF16),
        *[pltpu.VMEM((H, S, R, cols[kind]), BF16) for kind in order],
        *[pltpu.VMEM((2, S, R, cols[kind]), BF16) for kind in order],
        *[pltpu.VMEM((S, R, cols[kind]), BF16) for kind in order],
        *[pltpu.VMEM((S, R, cols[kind]), BF16) for kind in order],
        pltpu.VMEM((8, width), F32),
        pltpu.VMEM((8, width), F32),
        pltpu.VMEM((8, width), F32),
        pltpu.VMEM((S, 8, width), F32),
        pltpu.VMEM((8, 128), F32),
        pltpu.VMEM((8, 128), F32),
        pltpu.VMEM((S, 8, 128), F32),
        dma((4,)),
        dma((2, 2)),
        dma((2, S)),
        dma((4, S)),
        dma((4, S)),
        dma((2, 4)),
        dma((2, 4)),
        dma((2, 4)),
        dma((2, 4)),
        dma((4, S)),
        dma((4, S)),
        dma((8,)),
        dma((S,)),
        dma((S,)),
        dma((S,)),
        dma((S,)),
        dma((2, 7)),
        dma((2, 2)),
    ]
    operands = [tok, cot, frames, *weights]
    for moment, second in zip(moments, seconds):
        operands += [moment, second]
    return pl.pallas_call(
        functools.partial(layer_kernel, S, H),
        out_shape=out_shape,
        in_specs=[any_space, any_space, smem] + [vmem] * (len(operands) - 3),
        out_specs=(any_space, any_space) + (vmem,) * 6,
        scratch_shapes=scratch,
        compiler_params=pltpu.CompilerParams(
            collective_id=0, has_side_effects=True, vmem_limit_bytes=63 * 2**20
        ),
        name="layer",
    )(*operands)


def update_kernel(*refs):
    grads, masters, firsts, seconds = refs[0:5], refs[5:10], refs[10:15], refs[15:20]
    squares = refs[20]
    outs, norms = refs[21:46], refs[46]
    roots = jnp.sqrt(squares[...])
    for number in range(5):
        outs_here = outs[5 * number : 5 * number + 5]
        ratio = roots[number : number + 1, 0:1] / roots[number : number + 1, 1:2]
        pieces = range(grads[number].shape[0]) if grads[number].ndim == 3 else (slice(None),)
        for piece in pieces:
            gradient, master = grads[number][piece], masters[number][piece]
            first, second, direction = lamb_direction(
                master, firsts[number][piece], seconds[number][piece], gradient
            )
            new_master = master - RATE * ratio * direction
            outs_here[0][piece] = gradient
            outs_here[1][piece] = first
            outs_here[2][piece] = second
            outs_here[3][piece] = new_master
            outs_here[4][piece] = new_master.astype(BF16)
    norms[...] = roots[0:5, 0:2]


def run_update(grads, masters, firsts, seconds, squares):
    vmem = pl.BlockSpec(memory_space=pltpu.VMEM)
    operands = [*grads, *masters, *firsts, *seconds, squares]
    out_shape = []
    for grad in grads:
        out_shape += [jax.ShapeDtypeStruct(grad.shape, F32)] * 4 + [jax.ShapeDtypeStruct(grad.shape, BF16)]
    out_shape.append(jax.ShapeDtypeStruct((5, 2), F32))
    return pl.pallas_call(
        update_kernel,
        out_shape=tuple(out_shape),
        in_specs=[vmem] * len(operands),
        out_specs=(vmem,) * len(out_shape),
        name="update",
    )(*operands)


def local(mesh_sizes, *arrays):
    tokens, cotangent, frames = arrays[0:3]
    tensors = [list(arrays[3 + 3 * i : 6 + 3 * i]) for i in range(5)]
    for i in (1, 3):
        tensors[i] = [array.T for array in tensors[i]]
    masters, firsts, seconds = ([tensor[i] for tensor in tensors] for i in range(3))
    results = run_layer(mesh_sizes, tokens, cotangent, frames, masters, firsts, seconds)
    block_out, input_grad, grads, squares = results[0], results[1], results[2:7], results[7]
    updated = run_update(grads, masters, firsts, seconds, squares)
    outs = [block_out, input_grad.astype(F32)]
    for i in range(5):
        five = updated[5 * i : 5 * i + 5]
        outs += [array.T for array in five] if i in (1, 3) else list(five)
    outs.append(updated[25])
    return tuple(outs)


def solution(mesh):
    qkv, turned, straight, row = P(None, "seq", "head"), P("head", "seq"), P("seq", "head"), P(None, "seq")
    kinds = (qkv, turned, straight, turned, row)
    in_specs = [P("seq", None), P("seq", None), P()]
    out_specs = [P("seq", None), P("seq", None)]
    for kind in kinds:
        in_specs += [kind] * 3
        out_specs += [kind] * 5
    out_specs.append(P())
    return jax.shard_map(
        functools.partial(local, (mesh.shape["seq"], mesh.shape["head"])),
        mesh=mesh,
        in_specs=tuple(in_specs),
        out_specs=tuple(out_specs),
        check_vma=False,
    )
```

```python
import functools

import jax
import jax.numpy as jnp
from jax import lax
from jax.experimental import pallas as pl
from jax.experimental.pallas import tpu as pltpu
from jax.sharding import PartitionSpec as P

HEAD_DIM = 64
FRAME_TOKENS = 64
MOST_FRAMES = 16
STEP = 5

EPS_NORM = 1e-05
BETA_ONE = 0.5
BETA_TWO = 0.6
RATE = 0.3
DECAY = 0.01
EPS_ADAM = 1e-06
MASKED = -1e30

MESH = pl.DeviceIdType.MESH
F32 = jnp.float32
BF16 = jnp.bfloat16
TILE = 128
KEYS = MOST_FRAMES * FRAME_TOKENS + TILE
ROWS = 256

DOWN, UP, OUT, QKV = range(4)


def nn(a, b):
    return lax.dot_general(a, b, (((1,), (0,)), ((), ())), preferred_element_type=F32)


def nt(a, b):
    return lax.dot_general(a, b, (((1,), (1,)), ((), ())), preferred_element_type=F32)


def tn(a, b):
    return lax.dot_general(a, b, (((0,), (0,)), ((), ())), preferred_element_type=F32)


def normalize(values):
    average = jnp.mean(values, axis=-1, keepdims=True)
    centered = values - average
    variance = jnp.mean(centered * centered, axis=-1, keepdims=True)
    inverse = lax.rsqrt(variance + EPS_NORM)
    return centered * inverse, inverse


def norm_back(gradient, normed, inverse, gain_row):
    scaled = gradient * gain_row
    return inverse * (
        scaled
        - jnp.mean(scaled, axis=-1, keepdims=True)
        - normed * jnp.mean(scaled * normed, axis=-1, keepdims=True)
    )


def gelu_both(inner):
    root = 0.7978845608028654
    cube = 0.044715
    square = inner * inner
    curved = jnp.tanh(root * inner * (1.0 + cube * square))
    half = 0.5 * (1.0 + curved)
    value = inner * half
    slope = half + 0.5 * inner * (1.0 - curved * curved) * (root * (1.0 + 3.0 * cube * square))
    return value, slope


def lamb_direction(master, moment, square, gradient):
    new_first = BETA_ONE * moment + (1.0 - BETA_ONE) * gradient
    new_second = BETA_TWO * square + (1.0 - BETA_TWO) * gradient * gradient
    direction = (
        new_first
        / (1.0 - BETA_ONE**STEP)
        / (jnp.sqrt(new_second / (1.0 - BETA_TWO**STEP)) + EPS_ADAM)
        + DECAY * master
    )
    return new_first, new_second, direction


def flat(block):
    pieces, both, rows, columns = block.shape
    if rows % 16:
        block = block.astype(F32)
    return block.reshape(pieces * both * rows, columns).astype(BF16)


def cut(matrix, pieces):
    rows, columns = matrix.shape
    return matrix.reshape(pieces, 2, rows // (2 * pieces), columns).astype(BF16)


NAMES = (
    "w_qkv", "w_out", "w_up", "w_down", "norm_parts", "norm_full", "ext", "cot_own", "h1", "h1_t",
    "k_all", "v_all", "prob", "attended", "resid", "h2", "h2_t", "cot_t", "mlp", "dh2", "wide",
    "act", "dup", "low_out", "delta",
    "halo_in", "g_down", "g_up", "g_out", "c_down", "c_up", "c_out",
    "c_qkv", "e_down", "e_up", "e_out", "x_down", "x_out", "t_qkv", "k_t", "v_t", "from_cross", "scores", "inverse", "stack_q", "s_down",
    "s_up", "s_out", "s_qkv", "norm_sum", "norm_c", "norm_x", "norm_s", "sq_s", "near_rows", "loc_sem",
    "halo_sem", "normp_sem", "gz_send", "gz_recv", "gf_sem", "gs_sem", "gc_sem", "sc_sem", "se_sem", "sx_sem",
    "sz_send", "sz_recv", "sq_sem", "small_sem", "norm_s_sem", "sq_s_sem", "out_sem", "back_sem",
)


def layer_kernel(seq_count, head_count, *refs):
    tok, cot, frames = refs[0:3]
    qkv_w, out_w, up_w, down_w, norm_w = refs[3:8]
    moment_refs = refs[8:18]
    block_out, input_grad, qkv_g, out_g, up_g, down_g, norm_g, squares = refs[18:26]
    scratch = dict(zip(NAMES, refs[26:-10], strict=True))
    moments = refs[-10:]
    qkv_m, qkv_u, out_m, out_u, up_m, up_u, down_m, down_u, norm_m, norm_u = moments
    (w_qkv, w_out, w_up, w_down, norm_parts, norm_full, ext, cot_own, h1, h1_t, k_all, v_all) = (
        scratch[name] for name in NAMES[0:12]
    )
    (prob, attended, resid, h2, h2_t, cot_t, mlp, dh2, wide, act, dup, low_out) = (
        scratch[name] for name in NAMES[12:24]
    )
    delta, halo_in, scores, inverse, stack_q = (
        scratch[name] for name in ("delta", "halo_in", "scores", "inverse", "stack_q")
    )
    norm_sum, norm_c, norm_x, norm_s, sq_s, near_rows = (
        scratch[name] for name in ("norm_sum", "norm_c", "norm_x", "norm_s", "sq_s", "near_rows")
    )
    (loc_sem, halo_sem, normp_sem, gz_send, gz_recv, gf_sem, gs_sem, gc_sem, sc_sem, se_sem, sx_sem) = (
        scratch[name] for name in NAMES[-19:-8]
    )
    sz_send, sz_recv, sq_sem, k_t, v_t, from_cross = (
        scratch[name] for name in ("sz_send", "sz_recv", "sq_sem", "k_t", "v_t", "from_cross")
    )
    small_sem, norm_s_sem, sq_s_sem, out_sem, back_sem = (scratch[name] for name in NAMES[-5:])

    dk_all, dv_all, dq_all, dh1, d_scores, dr_low = k_all, v_all, attended, mlp, act, h2
    S, H = seq_count, head_count
    N = S // 2
    T = cot_own.shape[0]
    R = qkv_w.shape[1]
    hidden = up_w.shape[1]
    s = lax.axis_index("seq")
    h = lax.axis_index("head")
    hx = lax.div(h, 2)
    hc = lax.rem(h, 2)
    ring = lax.div(s, 2)
    side = lax.rem(s, 2)
    other_core = (s, h + 1 - 2 * hc)
    other_x = (s, lax.rem(h + 2, H))
    other_side = (s + 1 - 2 * side, h)
    mine = hc * 2 + hx
    near = hc * 2 + 1 - hx
    mine_pair = hc * 2
    other_pair = (1 - hc) * 2
    total = S * H
    place = s * H + mine

    def device_at(number):
        number = lax.rem(number + total, total)
        block = lax.rem(number, H)
        return (lax.div(number, H), lax.rem(block, 2) * 2 + lax.div(block, 2))

    def seq_peer(i):
        return lax.rem(s + i, S)

    def remote(src, dst, send, recv, device):
        return pltpu.make_async_remote_copy(
            src_ref=src, dst_ref=dst, send_sem=send, recv_sem=recv, device_id=device, device_id_type=MESH
        )

    def rows_of(index, count):
        return pl.ds(pl.multiple_of(index * count, count), count)

    def each(low, high, step):
        def one(i, carry):
            step(i)
            return carry

        lax.fori_loop(low, high, one, 0)

    cot_copy = pltpu.make_async_copy(cot.at[rows_of(mine, T)], cot_own, loc_sem.at[3])
    cot_copy.start()

    def ext_copy(chunk):
        return pltpu.make_async_copy(
            tok.at[rows_of(jnp.maximum(mine - 2 + chunk, 0), T)],
            ext.at[pl.ds(chunk * T, T)],
            loc_sem.at[chunk],
        )

    for chunk in (2, 1, 0):

        @pl.when(mine - 2 + chunk >= 0)
        def _():
            ext_copy(chunk).start()

    moment_copies = [
        pltpu.make_async_copy(source, target, loc_sem.at[4 + k])
        for k, (source, target) in enumerate(zip(moment_refs, moments))
    ]
    for copy in moment_copies:
        copy.start()

    for t in range(3):
        w_qkv[mine, ring, side, :, t * 128 : (t + 1) * 128] = qkv_w[t].astype(BF16)
    norm_parts[s] = jnp.zeros(norm_parts.shape[1:], F32)
    norm_parts[s, 0:4, 0:R] = norm_w[...].astype(BF16).astype(F32)

    barrier = pltpu.get_barrier_semaphore()

    def greet(device):
        pl.semaphore_signal(barrier, inc=1, device_id=device, device_id_type=MESH)

    each(1, total, lambda i: greet(device_at(place + i)))
    pl.semaphore_wait(barrier, total - 1)

    spans = {
        QKV: w_qkv,
        OUT: w_out,
        UP: w_up,
        DOWN: w_down,
    }
    side_first = {QKV: True, OUT: False, UP: True, DOWN: False}
    all_ring, both_sides = pl.ds(0, N), pl.ds(0, 2)

    def piece(kind, group, a, b):
        return spans[kind].at[group, a, b]

    def ring_peer(i):
        there = lax.rem(ring + i, N)
        return there, (there * 2 + side, h)

    def gather_ring(kind, i):
        own = piece(kind, mine, ring, side)
        return remote(own, own, gz_send.at[kind, i], gz_recv.at[kind, ring], ring_peer(i)[1])

    def gather_ring_start(kind):
        each(1, N, lambda i: gather_ring(kind, i).start())

    def gather_ring_wait(kind):
        def one(i):
            there, device = ring_peer(i)
            block = piece(kind, mine, there, side)
            remote(block, block, gz_send.at[kind, i], gz_recv.at[kind, there], device).wait_recv()

        each(1, N, one)

    def gather_first(kind, sent):
        if side_first[kind]:
            block, device = piece(kind, mine, all_ring, side if sent else 1 - side), other_side
        else:
            block, device = piece(kind, mine if sent else near, all_ring, side), other_x
        return remote(block, block, gf_sem.at[0, kind], gf_sem.at[1, kind], device)

    def gather_second(kind, sent):
        if side_first[kind]:
            block, device = piece(kind, mine if sent else near, all_ring, both_sides), other_x
        else:
            block = piece(kind, pl.ds(mine_pair, 2), all_ring, side if sent else 1 - side)
            device = other_side
        return remote(block, block, gs_sem.at[0, kind], gs_sem.at[1, kind], device)

    def gather_core(kind, pair):
        block = piece(kind, pl.ds(pair, 2), all_ring, both_sides)
        return remote(block, block, gc_sem.at[0, kind], gc_sem.at[1, kind], other_core)

    def gather_a(kind):
        gather_ring_wait(kind)
        gather_first(kind, True).start()

    def gather_b(kind):
        gather_first(kind, False).wait_recv()
        gather_second(kind, True).start()

    def gather_c(kind):
        gather_second(kind, False).wait_recv()
        gather_core(kind, mine_pair).start()

    def gather_d(kind):
        gather_core(kind, other_pair).wait_recv()

    diagonal = (other_side[0], other_x[1])

    def gather_sent(kind):
        gather_first(kind, True).wait_send()
        gather_second(kind, True).wait_send()
        gather_core(kind, mine_pair).wait_send()
        each(1, N, lambda i: gather_ring(kind, i).wait_send())

    def norm_part(i):
        return remote(
            norm_parts.at[s], norm_parts.at[s], normp_sem.at[0, i], normp_sem.at[1, s], (seq_peer(i), h)
        )

    each(1, S, lambda i: norm_part(i).start())
    gather_ring_start(QKV)

    pieces = 4
    half = T // pieces

    def halo_copy(k):
        return remote(
            tok.at[rows_of(jnp.minimum(mine + 2, H - 1) * pieces + k, half)],
            ext.at[pl.ds(k * half, half)],
            halo_sem.at[0, k],
            halo_sem.at[1, k],
            (seq_peer(1), h),
        )

    def halo_pass(k):
        return remote(
            ext.at[pl.ds(k * half, half)],
            ext.at[pl.ds(T + k * half, half)],
            halo_sem.at[0, pieces + k],
            halo_sem.at[1, pieces + k],
            other_x,
        )

    sends_halo = (hc == 0) & (s < S - 1)
    takes_halo = (hc == 0) & (s > 0)

    @pl.when(sends_halo)
    def _():
        for k in range(pieces):
            halo_copy(k).start()

    @pl.when((hc == 0) & (s == 0))
    def _():
        ext[0:T, :] = jnp.zeros((T, ext.shape[1]), BF16)

    @pl.when((mine == 0) & (s == 0))
    def _():
        ext[T : 2 * T, :] = jnp.zeros((T, ext.shape[1]), BF16)

    w_out[mine, ring, side] = out_w[...].astype(BF16)
    w_up[mine, ring, side] = up_w[...].astype(BF16)
    w_down[mine, ring, side] = down_w[...].astype(BF16)

    first_frame = place * (T // FRAME_TOKENS)
    own_frames = T // FRAME_TOKENS

    def clip_step(c, carry):
        end, lows = carry
        start = end
        end = start + frames[c]
        lows = tuple(
            jnp.where((start <= first_frame + f) & (first_frame + f < end), start, lows[f])
            for f in range(own_frames)
        )
        return end, lows

    _, clip_low = lax.fori_loop(
        0, frames.shape[0], clip_step, (jnp.int32(0), tuple(jnp.int32(0) for _ in range(own_frames)))
    )

    gather_a(QKV)
    def norm_part_wait(i, carry):
        peer = seq_peer(i)
        part = norm_parts.at[peer]
        remote(part, part, normp_sem.at[0, i], normp_sem.at[1, peer], (peer, h)).wait_recv()
        return carry

    lax.fori_loop(1, S, norm_part_wait, 0)
    width = norm_full.shape[1]

    def norm_place(i, carry):
        part = norm_parts[i]
        wide = jnp.concatenate([part, jnp.zeros((8, width - 128), F32)], axis=1)
        return carry + pltpu.roll(wide, i * R, axis=1)

    norm_full[...] = lax.fori_loop(0, S, norm_place, jnp.zeros(norm_full.shape, F32))
    gain_one, shift_one = norm_full[0:1, :], norm_full[1:2, :]
    gain_two, shift_two = norm_full[2:3, :], norm_full[3:4, :]

    def first_norm(chunk):
        def one(b):
            at = pl.ds(pl.multiple_of(chunk * T + b * ROWS, ROWS), ROWS)
            normed, _ = normalize(ext[at, :].astype(F32))
            h1[at, :] = (normed * gain_one + shift_one).astype(BF16)

        each(0, T // ROWS, one)
        h1_t[:, chunk * T : (chunk + 1) * T] = h1[chunk * T : (chunk + 1) * T, :].T

    ext_copy(2).wait()
    first_norm(2)
    @pl.when((mine == 1) & takes_halo)
    def _():
        for k in range(pieces):
            halo_copy(k).wait_recv()
            halo_pass(k).start()

    gather_ring_start(OUT)
    gather_ring_start(UP)
    cot_copy.wait()
    cot_t[...] = cot_own[...].T
    gather_b(QKV)

    @pl.when(mine >= 1)
    def _():
        ext_copy(1).wait()

    @pl.when(mine >= 2)
    def _():
        ext_copy(0).wait()

    @pl.when((mine == 0) & takes_halo)
    def _():
        for k in range(pieces):
            halo_copy(k).wait_recv()

    first_norm(0)

    @pl.when((mine == 0) & takes_halo)
    def _():
        for k in range(pieces):
            halo_pass(k).wait_recv()

    first_norm(1)
    gather_ring_start(DOWN)

    lane = lax.broadcasted_iota(jnp.int32, (1, 128), 1)
    first_head = jnp.where(lane < HEAD_DIM, 1.0, 0.0).astype(BF16)
    second_head = jnp.where(lane < HEAD_DIM, 0.0, 1.0).astype(BF16)
    feature = lax.broadcasted_iota(jnp.int32, (128, TILE), 0)

    def two_heads(block):
        return jnp.concatenate([block * first_head, block * second_head], axis=0)

    def project(p):
        weight = flat(w_qkv[p])
        for chunk in range(3):
            at = pl.ds(chunk * T, T)
            if chunk == 2:
                out = nn(h1[at, :], weight)
                queries = out[:, 0:128].astype(BF16) * jnp.asarray(HEAD_DIM**-0.5, BF16)
                for i in range(T // TILE):
                    stack_q[p, i * 2 * TILE : (i + 1) * 2 * TILE, :] = two_heads(queries[i * TILE : (i + 1) * TILE])
                out = out[:, 128:384]
            else:
                out = nn(h1[at, :], flat(w_qkv[p, :, :, :, 128:384]))
            k_all[p, at, :] = out[:, 0:128].astype(BF16)
            v_all[p, at, :] = out[:, 128:256].astype(BF16)
            k_t[p, :, at] = k_all[p, at, :].T
            v_t[p, :, at] = v_all[p, at, :].T

    def own_halves(block):
        return jnp.where(feature < HEAD_DIM, block[:, 0:TILE], block[:, TILE : 2 * TILE])

    key_frames = KEYS // FRAME_TOKENS

    def bias_of(i):
        query_lane = lax.broadcasted_iota(jnp.int32, (key_frames, 1, 2 * TILE), 2)
        later = lax.rem(query_lane, TILE) >= FRAME_TOKENS
        low = jnp.where(later, clip_low[2 * i + 1], clip_low[2 * i])
        high = first_frame + 2 * i + later.astype(jnp.int32)
        key_frame = (
            first_frame
            - MOST_FRAMES
            + 2 * i
            + lax.broadcasted_iota(jnp.int32, (key_frames, 1, 2 * TILE), 0)
        )
        return jnp.where((key_frame >= low) & (key_frame <= high), 0.0, MASKED).astype(F32)

    biases = [bias_of(i) for i in range(T // TILE)]

    def attend(p, between):
        for i in range(T // TILE):
            for step in between.get(i, ()):
                step()
            own = pl.ds(i * TILE, TILE)
            window = pl.ds(i * TILE, KEYS)
            raw = scores.at[pl.ds(i % 2 * KEYS, KEYS)]
            raw[...] = nt(k_all[p, window, :], stack_q[p, i * 2 * TILE : (i + 1) * 2 * TILE, :])
            highest = jnp.full((8, 2 * TILE), MASKED, F32)
            for c in range(KEYS // TILE):
                block = raw[c * TILE : (c + 1) * TILE, :].reshape(2, FRAME_TOKENS, 2 * TILE)
                block = (block + biases[i][2 * c : 2 * c + 2]).reshape(TILE // 8, 8, 2 * TILE)
                highest = jnp.maximum(highest, jnp.max(block, axis=0))
            shift = biases[i] - jnp.max(highest, axis=0, keepdims=True)
            sums = jnp.zeros((8, 2 * TILE), F32)
            for c in range(KEYS // TILE):
                block = raw[c * TILE : (c + 1) * TILE, :].reshape(2, FRAME_TOKENS, 2 * TILE)
                block = jnp.exp(block + shift[2 * c : 2 * c + 2]).reshape(TILE // 8, 8, 2 * TILE)
                sums = sums + jnp.sum(block, axis=0)
                prob[p, (i + c) * TILE : (i + c + 1) * TILE, i * 2 * TILE : (i + 1) * 2 * TILE] = block.reshape(
                    TILE, 2 * TILE
                ).astype(BF16)
            scale = 1.0 / jnp.sum(sums, axis=0, keepdims=True)
            inverse[p, i] = scale
            low = prob[p, window, i * 2 * TILE : (i + 1) * 2 * TILE]
            mixed = own_halves(nn(v_t[p, :, window], low) * scale)
            attended[p, own, :] = mixed.T.astype(BF16)

    def clear(p):
        for i in range(T // TILE):
            columns = slice(i * 2 * TILE, (i + 1) * 2 * TILE)
            if i:
                prob[p, 0 : i * TILE, columns] = jnp.zeros((i * TILE, 2 * TILE), BF16)
            below = i * TILE + KEYS
            if below < 3 * T:
                prob[p, below : 3 * T, columns] = jnp.zeros((3 * T - below, 2 * TILE), BF16)

    each(0, H, clear)

    do = functools.partial
    project(mine)
    attend(mine, {3: [do(gather_a, OUT)]})
    gather_c(QKV)
    gather_a(UP)
    project(near)
    attend(near, {0: [do(gather_a, DOWN)], 2: [do(gather_b, OUT)]})
    gather_d(QKV)
    project(other_pair)
    attend(other_pair, {0: [do(gather_b, UP)], 1: [do(gather_b, DOWN)], 2: [do(gather_c, OUT)]})
    project(other_pair + 1)
    attend(other_pair + 1, {1: [do(gather_d, OUT)], 3: [do(gather_c, UP)]})
    gather_c(DOWN)

    acc = nt(attended[0], flat(w_out[0]))
    for p in range(1, H):
        acc = acc + nt(attended[p], flat(w_out[p]))
    resid[...] = acc

    def second_norm(b):
        at = rows_of(b, ROWS)
        whole = ext[pl.ds(pl.multiple_of(2 * T + b * ROWS, ROWS), ROWS), :].astype(F32) + resid[at, :]
        resid[at, :] = whole
        normed, _ = normalize(whole)
        h2[at, :] = (normed * gain_two + shift_two).astype(BF16)

    each(0, T // ROWS, second_norm)
    h2_t[...] = h2[...].T
    gather_d(UP)
    gather_d(DOWN)

    endings = ("down", "up", "out", "qkv")
    grads, from_core, from_side, from_x, from_ring, from_quarter = (
        [scratch.get(start + name) for name in endings] for start in ("g_", "c_", "e_", "x_", "s_", "t_")
    )
    grads[QKV] = w_up.at[:, :, :, :, pl.ds(0, w_qkv.shape[-1])]

    def in_order(k):
        return (other_pair, other_pair + 1, near, mine)[k]

    def scatter_core(kind, group, slot):
        return remote(
            grads[kind].at[group],
            from_core[kind].at[slot],
            sc_sem.at[0, kind, slot],
            sc_sem.at[1, kind, slot],
            other_core,
        )

    def scatter_side(kind, group):
        slot = group - mine_pair
        return remote(
            grads[kind].at[group, all_ring, 1 - side],
            from_side[kind].at[slot],
            se_sem.at[0, kind, slot],
            se_sem.at[1, kind, slot],
            other_side,
        )

    at_once = (QKV,)

    def scatter_quarter(kind, which):
        group, part, device = (
            (near, side, other_x),
            (near, 1 - side, diagonal),
            (mine, 1 - side, other_side),
        )[which]
        return remote(
            grads[kind].at[group, all_ring, part],
            from_quarter[kind].at[which],
            sq_sem.at[0, kind, which],
            sq_sem.at[1, kind, which],
            device,
        )

    def quarter_sum(kind):
        for which in range(3):
            scatter_quarter(kind, which).wait_recv()

        def add(b):
            grads[kind][mine, b, side] = (
                grads[kind][mine, b, side].astype(F32)
                + from_quarter[kind][0, b].astype(F32)
                + (from_quarter[kind][1, b].astype(F32) + from_quarter[kind][2, b].astype(F32))
            ).astype(BF16)

        each(0, N, add)
        each(1, N, lambda i: scatter_ring(kind, i).start())

    def cross_x():
        return remote(grads[UP].at[near], from_cross, sx_sem.at[0, UP], sx_sem.at[1, UP], other_x)

    def cross_side():
        return remote(
            grads[UP].at[mine, all_ring, 1 - side],
            from_side[UP].at[0],
            se_sem.at[0, UP, 0],
            se_sem.at[1, UP, 0],
            other_side,
        )

    def cross_a():
        cross_x().wait_recv()

        def add(there, b):
            grads[UP][mine, there, b] = (
                grads[UP][mine, there, b].astype(F32) + from_cross[there, b].astype(F32)
            ).astype(BF16)

        each(0, N, lambda there: add(there, 1 - side))
        cross_side().start()
        each(0, N, lambda there: add(there, side))

    def cross_b():
        cross_side().wait_recv()

        def add(there):
            grads[UP][mine, there, side] = (
                grads[UP][mine, there, side].astype(F32) + from_side[UP][0, there].astype(F32)
            ).astype(BF16)

        each(0, N, add)
        each(1, N, lambda i: scatter_ring(UP, i).start())

    def place_grad(kind, k, matrix):
        group = in_order(k)
        if k < 2:
            grads[kind][group] = cut(matrix, N)
            scatter_core(kind, group, k).start()
        else:
            slot = group - mine_pair
            scatter_core(kind, group, slot).wait_recv()
            grads[kind][group] = cut(matrix + flat(from_core[kind][slot]).astype(F32), N)
            if kind == UP:
                if k == 2:
                    cross_x().start()
            elif kind not in at_once:
                scatter_side(kind, group).start()
            elif k == 2:
                scatter_quarter(kind, 0).start()
                scatter_quarter(kind, 1).start()
            else:
                scatter_quarter(kind, 2).start()

    def scatter_side_sum(kind, group):
        scatter_side(kind, group).wait_recv()
        slot = group - mine_pair

        def add(b):
            grads[kind][group, b, side] = (
                grads[kind][group, b, side].astype(F32) + from_side[kind][slot, b].astype(F32)
            ).astype(BF16)

        each(0, N, add)

    def scatter_x(kind):
        return remote(
            grads[kind].at[near, all_ring, side],
            from_x[kind],
            sx_sem.at[0, kind],
            sx_sem.at[1, kind],
            other_x,
        )

    def scatter_ring(kind, i):
        there, device = ring_peer(i)
        return remote(
            grads[kind].at[mine, there, side],
            from_ring[kind].at[ring],
            sz_send.at[kind, i],
            sz_recv.at[kind, ring],
            device,
        )

    def scatter_a(kind):
        scatter_side_sum(kind, near)
        scatter_x(kind).start()

    def scatter_b(kind):
        scatter_side_sum(kind, mine)
        scatter_x(kind).wait_recv()

        def add(b):
            grads[kind][mine, b, side] = (
                grads[kind][mine, b, side].astype(F32) + from_x[kind][b].astype(F32)
            ).astype(BF16)

        each(0, N, add)
        each(1, N, lambda i: scatter_ring(kind, i).start())

    def scatter_c(kind):
        landed = from_ring[kind]

        def one(i, carry):
            there, device = ring_peer(i)
            remote(
                grads[kind].at[mine, there, side],
                landed.at[there],
                sz_send.at[kind, i],
                sz_recv.at[kind, there],
                device,
            ).wait_recv()
            return carry + landed[there].astype(F32)

        return lax.fori_loop(1, N, one, grads[kind][mine, ring, side].astype(F32))

    mlp[...] = jnp.zeros_like(mlp)
    dh2[...] = jnp.zeros_like(dh2)
    half_hidden = hidden // 2

    def part_of(k, which, column, low_row, high_row):
        buffer = wide if k % 2 == 0 else scores
        start = (2 * which + column) * T
        return buffer.at[pl.ds(start + low_row, high_row - low_row), :]

    def inner(k):
        for column in range(2):
            columns = slice(column * half_hidden, (column + 1) * half_hidden)
            part_of(k, 0, column, 0, T)[...] = nn(h2[...], flat(w_up[in_order(k), :, :, :, columns]))
            part_of(k, 1, column, 0, T)[...] = nn(cot_own[...], flat(w_down[in_order(k), :, :, :, columns]))

    def slot(k):
        return pl.ds(k % 2 * hidden, hidden)

    def pointwise(k):
        for b in range(T // 128):
            for column in range(2):
                low_row, high_row = b * 128, (b + 1) * 128
                value, slope = gelu_both(part_of(k, 0, column, low_row, high_row)[...])
                at = pl.ds(k % 2 * hidden + column * half_hidden, half_hidden)
                act[low_row:high_row, at] = value.astype(BF16)
                dup[low_row:high_row, at] = (part_of(k, 1, column, low_row, high_row)[...] * slope).astype(BF16)

    def outer(k):
        mlp[...] += nt(act[:, slot(k)], flat(w_down[in_order(k)]))
        dh2[...] += nt(dup[:, slot(k)], flat(w_up[in_order(k)]))
        place_grad(DOWN, k, nn(cot_t[...], act[:, slot(k)]))
        place_grad(UP, k, nn(h2_t[...], dup[:, slot(k)]))

    inner(0)
    for k in range(H):
        if k + 1 < H:
            inner(k + 1)
        pointwise(k)
        outer(k)

    def finish_rows(target, low, at_sem):
        def slab(block):
            return target.at[rows_of(block, T)]

        keep = pltpu.make_async_copy(low, slab(mine), out_sem.at[at_sem, 0])
        landed = near_rows.at[at_sem]
        to_x = remote(low, landed, out_sem.at[at_sem, 1], out_sem.at[at_sem, 2], other_x)
        to_core = remote(low, slab(mine), out_sem.at[at_sem, 3], out_sem.at[at_sem, 4], other_core)
        passed = remote(landed, slab(near), out_sem.at[at_sem, 5], out_sem.at[at_sem, 6], other_core)
        store = pltpu.make_async_copy(landed, slab(near), out_sem.at[at_sem, 7])
        return keep, to_x, to_core, passed, store

    def sum_out(b):
        at = rows_of(b, ROWS)
        low_out[at, :] = (resid[at, :] + mlp[at, :]).astype(BF16)

    each(0, T // ROWS, sum_out)
    out_copies = finish_rows(block_out, low_out, 0)

    def second_back(b, carry):
        gain_sum, shift_sum = carry
        at = rows_of(b, ROWS)
        normed, inverse = normalize(resid[at, :])
        grad = dh2[at, :]
        mixed = cot_own[at, :].astype(F32) + norm_back(grad, normed, inverse, gain_two)
        resid[at, :] = mixed
        dr_low[at, :] = mixed.astype(BF16)
        gain_sum = gain_sum + jnp.sum(grad * normed, axis=0, keepdims=True)
        shift_sum = shift_sum + jnp.sum(grad, axis=0, keepdims=True)
        return gain_sum, shift_sum

    zero_row = jnp.zeros((1, width), F32)
    gain_two_grad, shift_two_grad = lax.fori_loop(0, T // ROWS, second_back, (zero_row, zero_row))

    def stack_d(p):
        return h1.at[pl.ds(0, 2 * T), pl.ds(pl.multiple_of(p * 128, 128), 128)]

    lane_first = lax.broadcasted_iota(jnp.int32, (TILE, 128), 1) < HEAD_DIM

    def deltas(p, d_att):
        for i in range(T // TILE):
            own = pl.ds(i * TILE, TILE)
            row = inverse[p, i]
            turned = jnp.concatenate([row[:, 0:TILE], row[:, TILE : 2 * TILE], jnp.zeros((6, TILE), F32)], axis=0).T
            scaled = d_att[i * TILE : (i + 1) * TILE].astype(F32) * jnp.where(lane_first, turned[:, 0:1], turned[:, 1:2])
            low = scaled.astype(BF16)
            stack_d(p)[i * 2 * TILE : (i + 1) * 2 * TILE, :] = two_heads(low)
            products = (low.astype(F32) * attended[p, own, :].astype(F32)).T
            delta[p, :, i * 2 * TILE : (i + 1) * 2 * TILE] = jnp.concatenate(
                [
                    jnp.sum(products[0:HEAD_DIM], axis=0, keepdims=True),
                    jnp.sum(products[HEAD_DIM:128], axis=0, keepdims=True),
                ],
                axis=1,
            )

    h2_t[...] = dr_low[...].T
    for k in range(H):
        p = in_order(k)
        deltas(p, nn(dr_low[...], flat(w_out[p])).astype(BF16))
        place_grad(OUT, k, nn(h2_t[...], attended[p]))

    gather_sent(UP)
    scatter_a(DOWN)
    cross_a()
    for copy in out_copies[:3]:
        copy.start()

    def dq_acc(p, i):
        return wide.at[pl.ds(pl.multiple_of((p * (T // TILE) + i) * TILE, TILE), TILE), pl.ds(0, TILE)]

    def attend_back(chunk, p):
        at = pl.ds(chunk * T, T)
        grads_p = stack_d(p)[...]
        for i in range(T // TILE):
            d_prob = scores.at[pl.ds(i * T, T)]
            d_prob[...] = nt(v_all[p, at, :], grads_p[i * 2 * TILE : (i + 1) * 2 * TILE])
        for r in range(T // TILE):
            rows = slice(r * TILE, (r + 1) * TILE)
            for i in range(T // TILE):
                columns = slice(i * 2 * TILE, (i + 1) * 2 * TILE)
                if (chunk == 0 and i > r) or (chunk == 2 and i < r):
                    d_scores[rows, columns] = jnp.zeros((TILE, 2 * TILE), BF16)
                else:
                    low = prob[p, chunk * T + r * TILE : chunk * T + (r + 1) * TILE, columns].astype(F32)
                    d_scores[rows, columns] = (low * (scores[i * T + r * TILE : i * T + (r + 1) * TILE, :] - delta[p, :, columns])).astype(BF16)
        dv_all[p, at, :] = nn(prob[p, at, :], grads_p).astype(BF16)
        dk_all[p, at, :] = nn(d_scores[...], stack_q[p]).astype(BF16)
        dq_part = nn(k_t[p, :, at], d_scores[...])
        for i in range(T // TILE):
            own = pl.ds(i * TILE, TILE)
            part = own_halves(dq_part[:, i * 2 * TILE : (i + 1) * 2 * TILE])
            if chunk == 0:
                dq_acc(p, i)[...] = part
            elif chunk == 1:
                dq_acc(p, i)[...] += part
            else:
                dq_all[p, own, :] = ((dq_acc(p, i)[...] + part) * (HEAD_DIM**-0.5)).T.astype(BF16)

    def back_copy(chunk):
        return remote(
            dup.at[:, pl.ds(chunk * width, width)],
            halo_in.at[chunk],
            back_sem.at[0, chunk],
            back_sem.at[1, chunk],
            device_at(place - 2 + chunk),
        )

    def sends_back(chunk):
        return place >= 2 - chunk

    def takes_back(chunk):
        return place < total - (2 - chunk)

    for chunk in range(2):

        @pl.when(jnp.logical_not(takes_back(chunk)))
        def _():
            halo_in[chunk] = jnp.zeros(halo_in.shape[1:], BF16)

    def first_sums(chunk, carry):
        def one(b, inner):
            gain_sum, shift_sum = inner
            at = pl.ds(pl.multiple_of(chunk * T + b * ROWS, ROWS), ROWS)
            normed, _ = normalize(ext[at, :].astype(F32))
            grad = dh1[rows_of(b, ROWS), :]
            if chunk < 2:
                dup[rows_of(b, ROWS), chunk * width : (chunk + 1) * width] = grad.astype(BF16)
            return (
                gain_sum + jnp.sum(grad * normed, axis=0, keepdims=True),
                shift_sum + jnp.sum(grad, axis=0, keepdims=True),
            )

        return lax.fori_loop(0, T // ROWS, one, carry)

    def halo_back(p, chunk):
        at = pl.ds(chunk * T, T)
        both = jnp.concatenate([dk_all[p, at, :], dv_all[p, at, :]], axis=1)
        return nt(both, flat(w_qkv[p, :, :, :, 128:384]))

    sums = (zero_row, zero_row)
    for chunk in range(2):
        dh1[...] = jnp.zeros_like(dh1)

        def one(p, chunk=chunk):
            attend_back(chunk, p)
            dh1[...] += halo_back(p, chunk)

        each(0, 2, one)
        if chunk == 1:
            scatter_a(OUT)
        each(2, 4, one)
        sums = first_sums(chunk, sums)

        @pl.when(sends_back(chunk))
        def _():
            back_copy(chunk).start()

        if chunk == 0:
            scatter_b(DOWN)
            cross_b()
        if chunk == 1:
            scatter_b(OUT)
            out_copies[1].wait_recv()
            out_copies[3].start()
            out_copies[4].start()

    dh1[...] = jnp.zeros_like(dh1)
    for k in range(H):
        p = in_order(k)
        each(p, p + 1, lambda q: attend_back(2, q))
        weight = flat(w_qkv[p])
        at = pl.ds(2 * T, T)
        three = jnp.concatenate([dq_all[p], dk_all[p, at, :], dv_all[p, at, :]], axis=1)
        dh1[...] += nt(three, weight)
        both = jnp.concatenate([dk_all[p], dv_all[p]], axis=1)
        columns = [nn(h1_t[:, 2 * T : 3 * T], dq_all[p]), nn(h1_t[...], both)]
        place_grad(QKV, k, jnp.concatenate(columns, axis=1))

    gain_one_grad, shift_one_grad = first_sums(2, sums)
    norm_sum[...] = jnp.concatenate(
        [gain_one_grad, shift_one_grad, gain_two_grad, shift_two_grad, jnp.zeros((4, width), F32)], axis=0
    )
    norm_to_core = remote(norm_sum, norm_c, small_sem.at[0], small_sem.at[1], other_core)
    norm_to_core.start()
    norm_to_core.wait()
    norm_sum[...] += norm_c[...]
    plane = (other_x, other_side, diagonal)
    norm_plane = [
        remote(norm_sum, norm_x.at[k], small_sem.at[2 + k], small_sem.at[5 + k], device)
        for k, device in enumerate(plane)
    ]
    for copy in norm_plane:
        copy.start()

    for chunk in range(2):

        @pl.when(takes_back(chunk))
        def _():
            back_copy(chunk).wait_recv()

    def first_back(b):
        at = rows_of(b, ROWS)
        normed, inverse = normalize(ext[pl.ds(pl.multiple_of(2 * T + b * ROWS, ROWS), ROWS), :].astype(F32))
        grad = dh1[at, :] + halo_in[0, at, :].astype(F32) + halo_in[1, at, :].astype(F32)
        dr_low[at, :] = (resid[at, :] + norm_back(grad, normed, inverse, gain_one)).astype(BF16)

    each(0, T // ROWS, first_back)
    grad_copies = finish_rows(input_grad, dr_low, 1)
    for copy in grad_copies[:3]:
        copy.start()
    quarter_sum(QKV)
    for copy in norm_plane:
        copy.wait()
    norm_sum[...] += norm_x[0] + (norm_x[1] + norm_x[2])

    def norm_ring(i):
        return remote(
            norm_sum, norm_s.at[ring], norm_s_sem.at[0, i], norm_s_sem.at[1, ring], ring_peer(i)[1]
        )

    each(1, N, lambda i: norm_ring(i).start())

    for copy in moment_copies:
        copy.wait()
    down_total = scatter_c(DOWN)
    down_g[...] = down_total
    up_total = scatter_c(UP)
    up_g[...] = up_total
    out_total = scatter_c(OUT)
    out_g[...] = out_total

    def sums_of(master, moment, square, gradient):
        _, _, direction = lamb_direction(master, moment, square, gradient)
        return jnp.sum(master * master), jnp.sum(direction * direction)

    down_sums = sums_of(down_w[...], down_m[...], down_u[...], down_total)
    up_sums = sums_of(up_w[...], up_m[...], up_u[...], up_total)
    out_sums = sums_of(out_w[...], out_m[...], out_u[...], out_total)

    def norm_ring_wait(i, carry):
        there, device = ring_peer(i)
        remote(
            norm_sum, norm_s.at[there], norm_s_sem.at[0, i], norm_s_sem.at[1, there], device
        ).wait_recv()
        return carry + norm_s[there]

    norm_total = lax.fori_loop(1, N, norm_ring_wait, norm_sum[...])
    norm_mine = pltpu.roll(norm_total, lax.rem(width - s * R, width), axis=1)[0:4, 0:R]
    norm_g[...] = norm_mine
    once = jnp.where(h == 0, 1.0, 0.0).astype(F32)
    norm_sums = sums_of(norm_w[...], norm_m[...], norm_u[...], norm_mine)
    norm_sums = (norm_sums[0] * once, norm_sums[1] * once)

    qkv_total = scatter_c(QKV)
    weight_sum, update_sum = jnp.float32(0.0), jnp.float32(0.0)
    for t in range(3):
        part = qkv_total[:, t * 128 : (t + 1) * 128]
        qkv_g[t] = part
        pair = sums_of(qkv_w[t], qkv_m[t], qkv_u[t], part)
        weight_sum, update_sum = weight_sum + pair[0], update_sum + pair[1]
    qkv_sums = (weight_sum, update_sum)

    row = lax.broadcasted_iota(jnp.int32, (8, 128), 0)
    column = lax.broadcasted_iota(jnp.int32, (8, 128), 1)
    both = jnp.zeros((8, 128), F32)
    for number, pair in enumerate((qkv_sums, out_sums, up_sums, down_sums, norm_sums)):
        for which in range(2):
            both = jnp.where((row == which) & (column == number), pair[which], both)
    squares[...] = both

    def sq_copy(i):
        peer = lax.rem(place + i, total)
        return remote(squares, sq_s.at[place], sq_s_sem.at[0, i], sq_s_sem.at[1, place], device_at(peer))

    def sq_wait(i, carry):
        peer = lax.rem(place + i, total)
        remote(
            squares, sq_s.at[peer], sq_s_sem.at[0, i], sq_s_sem.at[1, peer], device_at(peer)
        ).wait_recv()
        return carry

    each(1, total, lambda i: sq_copy(i).start())
    grad_copies[1].wait_recv()
    grad_copies[3].start()
    grad_copies[4].start()
    lax.fori_loop(1, total, sq_wait, 0)
    sq_s[place] = both
    each(1, total, lambda i: sq_copy(i).wait_send())
    squares[...] = lax.fori_loop(0, total, lambda i, carry: carry + sq_s[i], jnp.zeros((8, 128), F32))

    for copies in (out_copies, grad_copies):
        keep, to_x, to_core, passed, store = copies
        keep.wait()
        store.wait()
        to_x.wait_send()
        to_core.wait_send()
        passed.wait_send()
        to_core.wait_recv()
        passed.wait_recv()

    for k in range(pieces):

        @pl.when(sends_halo)
        def _():
            halo_copy(k).wait_send()

        @pl.when((mine == 1) & takes_halo)
        def _():
            halo_pass(k).wait_send()

    for chunk in range(2):

        @pl.when(sends_back(chunk))
        def _():
            back_copy(chunk).wait_send()

    for kind in (QKV, OUT, DOWN):
        gather_sent(kind)
    for kind in (QKV, OUT, UP, DOWN):
        for k in range(2):
            scatter_core(kind, in_order(k), k).wait_send()
        if kind == UP:
            cross_x().wait_send()
            cross_side().wait_send()
        elif kind in at_once:
            for which in range(3):
                scatter_quarter(kind, which).wait_send()
        else:
            scatter_side(kind, near).wait_send()
            scatter_side(kind, mine).wait_send()
            scatter_x(kind).wait_send()

    def drain(i):
        norm_part(i).wait_send()

    each(1, S, drain)

    def drain_ring(i):
        norm_ring(i).wait_send()
        for kind in (QKV, OUT, UP, DOWN):
            scatter_ring(kind, i).wait_send()

    each(1, N, drain_ring)


def run_layer(mesh_sizes, tok, cot, frames, weights, moments, seconds):
    S, H = mesh_sizes
    rows_dev, width = tok.shape
    T = rows_dev // H
    R = weights[0].shape[1]
    N = S // 2
    assert H == 4 and S % 2 == 0 and 2 * T == MOST_FRAMES * FRAME_TOKENS and R * S == width
    hidden = weights[2].shape[1]
    assert hidden == T == 4 * TILE
    any_space = pl.BlockSpec(memory_space=pl.ANY)
    vmem = pl.BlockSpec(memory_space=pltpu.VMEM)
    smem = pl.BlockSpec(memory_space=pltpu.SMEM)
    dma = pltpu.SemaphoreType.DMA
    out_shape = (
        jax.ShapeDtypeStruct((rows_dev, width), BF16),
        jax.ShapeDtypeStruct((rows_dev, width), BF16),
        *[jax.ShapeDtypeStruct(w.shape, F32) for w in weights],
        jax.ShapeDtypeStruct((8, 128), F32),
    )
    cols = {"down": hidden, "up": hidden, "out": 128, "qkv": 384}
    kinds = ("down", "up", "out", "qkv")
    low, full = functools.partial(pltpu.VMEM, dtype=BF16), functools.partial(pltpu.VMEM, dtype=F32)
    scratch = dict(
        norm_parts=full((S, 8, 128)),
        norm_full=full((8, width)),
        ext=low((3 * T, width)),
        cot_own=low((T, width)),
        h1=low((3 * T, width)),
        h1_t=low((width, 3 * T)),
        k_all=low((H, 3 * T, 128)),
        v_all=low((H, 3 * T, 128)),
        prob=low((H, 3 * T, 2 * T)),
        scores=full((2 * KEYS, 2 * TILE)),
        inverse=full((H, T // TILE, 1, 2 * TILE)),
        stack_q=low((H, 2 * T, 128)),
        attended=low((H, T, 128)),
        resid=full((T, width)),
        h2=low((T, width)),
        h2_t=low((width, T)),
        cot_t=low((width, T)),
        mlp=full((T, width)),
        dh2=full((T, width)),
        wide=full((4 * T, 2 * TILE)),
        act=low((T, 2 * hidden)),
        dup=low((T, 2 * hidden)),
        low_out=low((T, width)),
        delta=full((H, 1, 2 * T)),
        halo_in=low((2, T, width)),
        norm_sum=full((8, width)),
        norm_c=full((8, width)),
        norm_x=full((3, 8, width)),
        norm_s=full((N, 8, width)),
        sq_s=full((S * H, 8, 128)),
        k_t=low((H, 128, 3 * T)),
        v_t=low((H, 128, 3 * T)),
        from_cross=low((N, 2, R, hidden)),
        loc_sem=dma((14,)),
        halo_sem=dma((2, 8)),
        normp_sem=dma((2, S)),
        gz_send=dma((4, N)),
        gz_recv=dma((4, N)),
        gf_sem=dma((2, 4)),
        gs_sem=dma((2, 4)),
        gc_sem=dma((2, 4)),
        sc_sem=dma((2, 4, 2)),
        se_sem=dma((2, 4, 2)),
        sx_sem=dma((2, 4)),
        sq_sem=dma((2, 4, 3)),
        sz_send=dma((4, N)),
        sz_recv=dma((4, N)),
        small_sem=dma((14,)),
        norm_s_sem=dma((2, N)),
        sq_s_sem=dma((2, S * H)),
        out_sem=dma((2, 8)),
        near_rows=low((2, T, width)),
        back_sem=dma((2, 2)),
    )
    for kind in kinds:
        scratch["w_" + kind] = low((H, N, 2, R, cols[kind]))
        if kind != "qkv":
            scratch["g_" + kind] = low((H, N, 2, R, cols[kind]))
        scratch["c_" + kind] = low((2, N, 2, R, cols[kind]))
        if kind != "qkv":
            scratch["e_" + kind] = low((2, N, R, cols[kind]))
            if kind != "up":
                scratch["x_" + kind] = low((N, R, cols[kind]))
        else:
            scratch["t_" + kind] = low((3, N, R, cols[kind]))
        scratch["s_" + kind] = low((N, R, cols[kind]))
    operands = [tok, cot, frames, *weights]
    for moment, second in zip(moments, seconds):
        operands += [moment, second]
    return pl.pallas_call(
        functools.partial(layer_kernel, S, H),
        out_shape=out_shape,
        in_specs=[any_space, any_space, smem] + [vmem] * 5 + [any_space] * 10,
        out_specs=(any_space, any_space) + (vmem,) * 6,
        scratch_shapes=[scratch[name] for name in NAMES]
        + [pltpu.VMEM(array.shape, F32) for array in operands[8:18]],
        compiler_params=pltpu.CompilerParams(
            collective_id=0, has_side_effects=True, vmem_limit_bytes=63 * 2**20
        ),
        name="layer",
    )(*operands)


CHUNKS = 4


def update_kernel(count, *refs):
    block_low, grad_low = refs[0:2]
    sources = refs[2:23]
    block_out, input_grad = refs[23:25]
    targets = refs[25 : 25 + count]
    rest = refs[25 + count :]
    loaded, made = rest[0:21], rest[21 : 21 + count]
    low, wide, block, sem, load_sem, store_sem = rest[21 + count :]
    rows = low.shape[1]
    block_load = pltpu.make_async_copy(block_low, block, sem.at[0, 0])
    block_store = pltpu.make_async_copy(block, block_out, sem.at[0, 1])
    loads = [
        pltpu.make_async_copy(grad_low.at[pl.ds(c * rows, rows)], low.at[c], sem.at[1, c]) for c in range(CHUNKS)
    ]
    stores = [
        pltpu.make_async_copy(wide.at[c], input_grad.at[pl.ds(c * rows, rows)], sem.at[2, c])
        for c in range(CHUNKS)
    ]
    small_loads = [
        pltpu.make_async_copy(source, target, load_sem.at[k])
        for k, (source, target) in enumerate(zip(sources, loaded))
    ]
    small_stores = [
        pltpu.make_async_copy(source, target, store_sem.at[k])
        for k, (source, target) in enumerate(zip(made, targets))
    ]
    for copy in loads:
        copy.start()
    for copy in small_loads:
        copy.start()
    block_load.start()
    for c in range(CHUNKS):
        loads[c].wait()
        wide[c] = low[c].astype(F32)
        stores[c].start()
    for copy in small_loads:
        copy.wait()
    grads, masters, firsts, seconds = loaded[0:5], loaded[5:10], loaded[10:15], loaded[15:20]
    roots = jnp.sqrt(loaded[20][...])
    for number in (3, 2, 0, 1, 4):
        outs_here = made[5 * number : 5 * number + 5]
        ratio = roots[0:1, number : number + 1] / roots[1:2, number : number + 1]
        pieces = range(grads[number].shape[0]) if len(grads[number].shape) == 3 else (slice(None),)
        for piece in pieces:
            gradient, master = grads[number][piece], masters[number][piece]
            first, second, direction = lamb_direction(
                master, firsts[number][piece], seconds[number][piece], gradient
            )
            new_master = master - RATE * ratio * direction
            outs_here[0][piece] = gradient
            outs_here[1][piece] = first
            outs_here[2][piece] = second
            outs_here[3][piece] = new_master
            outs_here[4][piece] = new_master.astype(BF16)
        for copy in small_stores[5 * number : 5 * number + 5]:
            copy.start()
    made[25][...] = roots[0:2, 0:5]
    small_stores[25].start()
    block_load.wait()
    block_store.start()
    for copy in (*stores, *small_stores, block_store):
        copy.wait()


def run_update(block_low, grad_low, grads, masters, firsts, seconds, squares):
    any_space = pl.BlockSpec(memory_space=pl.ANY)
    operands = [block_low, grad_low, *grads, *masters, *firsts, *seconds, squares]
    rows, width = block_low.shape
    out_shape = [jax.ShapeDtypeStruct((rows, width), BF16), jax.ShapeDtypeStruct((rows, width), F32)]
    for grad in grads:
        out_shape += [jax.ShapeDtypeStruct(grad.shape, F32)] * 4 + [jax.ShapeDtypeStruct(grad.shape, BF16)]
    out_shape.append(jax.ShapeDtypeStruct((2, 5), F32))
    small = [(array.shape, array.dtype) for array in operands[2:] + out_shape[2:]]
    count = len(out_shape) - 2
    return pl.pallas_call(
        functools.partial(update_kernel, count),
        out_shape=tuple(out_shape),
        in_specs=[any_space] * len(operands),
        out_specs=(any_space,) * len(out_shape),
        scratch_shapes=[pltpu.VMEM(shape, dtype) for shape, dtype in small]
        + [
            pltpu.VMEM((CHUNKS, rows // CHUNKS, width), BF16),
            pltpu.VMEM((CHUNKS, rows // CHUNKS, width), F32),
            pltpu.VMEM((rows, width), BF16),
            pltpu.SemaphoreType.DMA((3, CHUNKS)),
            pltpu.SemaphoreType.DMA((21,)),
            pltpu.SemaphoreType.DMA((count,)),
        ],
        compiler_params=pltpu.CompilerParams(vmem_limit_bytes=63 * 2**20),
        name="update",
    )(*operands)


def local(mesh_sizes, *arrays):
    tokens, cotangent, frames = arrays[0:3]
    tensors = [list(arrays[3 + 3 * i : 6 + 3 * i]) for i in range(5)]
    for i in (1, 3):
        tensors[i] = [array.T for array in tensors[i]]
    masters, firsts, seconds = ([tensor[i] for tensor in tensors] for i in range(3))
    results = run_layer(mesh_sizes, tokens, cotangent, frames, masters, firsts, seconds)
    updated = run_update(results[0], results[1], results[2:7], masters, firsts, seconds, results[7])
    outs = list(updated[0:2])
    for i in range(5):
        five = updated[2 + 5 * i : 7 + 5 * i]
        outs += [array.T for array in five] if i in (1, 3) else list(five)
    outs.append(updated[27].T)
    return tuple(outs)


def solution(mesh):
    qkv, turned, straight, row = P(None, "seq", "head"), P("head", "seq"), P("seq", "head"), P(None, "seq")
    kinds = (qkv, turned, straight, turned, row)
    in_specs = [P("seq", None), P("seq", None), P()]
    out_specs = [P("seq", None), P("seq", None)]
    for kind in kinds:
        in_specs += [kind] * 3
        out_specs += [kind] * 5
    out_specs.append(P())
    return jax.shard_map(
        functools.partial(local, (mesh.shape["seq"], mesh.shape["head"])),
        mesh=mesh,
        in_specs=tuple(in_specs),
        out_specs=tuple(out_specs),
        check_vma=False,
    )
```

```python
import functools

import jax
import jax.numpy as jnp
from jax import lax
from jax.experimental import pallas as pl
from jax.experimental.pallas import tpu as pltpu
from jax.sharding import PartitionSpec as P

HEAD_DIM = 64
FRAME_TOKENS = 64
MOST_FRAMES = 16
STEP = 5

EPS_NORM = 1e-05
BETA_ONE = 0.5
BETA_TWO = 0.6
RATE = 0.3
DECAY = 0.01
EPS_ADAM = 1e-06
MASKED = -1e30

MESH = pl.DeviceIdType.MESH
F32 = jnp.float32
BF16 = jnp.bfloat16
TILE = 128
KEYS = MOST_FRAMES * FRAME_TOKENS + TILE
ROWS = 256

DOWN, UP, OUT, QKV = range(4)


def nn(a, b):
    return lax.dot_general(a, b, (((1,), (0,)), ((), ())), preferred_element_type=F32)


def nt(a, b):
    return lax.dot_general(a, b, (((1,), (1,)), ((), ())), preferred_element_type=F32)


def tn(a, b):
    return lax.dot_general(a, b, (((0,), (0,)), ((), ())), preferred_element_type=F32)


def normalize(values):
    average = jnp.mean(values, axis=-1, keepdims=True)
    centered = values - average
    variance = jnp.mean(centered * centered, axis=-1, keepdims=True)
    inverse = lax.rsqrt(variance + EPS_NORM)
    return centered * inverse, inverse


def norm_back(gradient, normed, inverse, gain_row):
    scaled = gradient * gain_row
    return inverse * (
        scaled
        - jnp.mean(scaled, axis=-1, keepdims=True)
        - normed * jnp.mean(scaled * normed, axis=-1, keepdims=True)
    )


def gelu_both(inner):
    root = 0.7978845608028654
    cube = 0.044715
    square = inner * inner
    curved = jnp.tanh(root * inner * (1.0 + cube * square))
    half = 0.5 * (1.0 + curved)
    value = inner * half
    slope = half + 0.5 * inner * (1.0 - curved * curved) * (root * (1.0 + 3.0 * cube * square))
    return value, slope


def lamb_direction(master, moment, square, gradient):
    new_first = BETA_ONE * moment + (1.0 - BETA_ONE) * gradient
    new_second = BETA_TWO * square + (1.0 - BETA_TWO) * gradient * gradient
    direction = (
        new_first
        / (1.0 - BETA_ONE**STEP)
        / (jnp.sqrt(new_second / (1.0 - BETA_TWO**STEP)) + EPS_ADAM)
        + DECAY * master
    )
    return new_first, new_second, direction


def flat(block):
    pieces, both, rows, columns = block.shape
    if rows % 16:
        block = block.astype(F32)
    return block.reshape(pieces * both * rows, columns).astype(BF16)


def cut(matrix, pieces):
    rows, columns = matrix.shape
    return matrix.reshape(pieces, 2, rows // (2 * pieces), columns).astype(BF16)


NAMES = (
    "w_qkv", "w_out", "w_up", "w_down", "norm_parts", "norm_full", "ext", "cot_own", "h1", "h1_t",
    "k_all", "v_all", "prob", "attended", "resid", "h2", "h2_t", "cot_t", "mlp", "dh2", "wide",
    "act", "dup", "low_out", "delta",
    "halo_in", "g_down", "g_up", "g_out", "c_down", "c_up", "c_out",
    "c_qkv", "e_down", "e_up", "e_out", "x_down", "x_out", "e_qkv", "x_qkv", "k_t", "v_t", "from_cross", "scores", "inverse", "stack_q", "s_down",
    "s_up", "s_out", "s_qkv", "norm_sum", "norm_c", "norm_x", "norm_s", "sq_s", "near_rows", "loc_sem",
    "halo_sem", "normp_sem", "gz_send", "gz_recv", "gf_sem", "gs_sem", "gc_sem", "sc_sem", "se_sem", "sx_sem",
    "sz_send", "sz_recv", "small_sem", "norm_s_sem", "sq_s_sem", "out_sem", "back_sem",
)


def layer_kernel(seq_count, head_count, *refs):
    tok, cot, frames = refs[0:3]
    qkv_w, out_w, up_w, down_w, norm_w = refs[3:8]
    moment_refs = refs[8:18]
    block_out, input_grad, qkv_g, out_g, up_g, down_g, norm_g, squares = refs[18:26]
    scratch = dict(zip(NAMES, refs[26:-10], strict=True))
    moments = refs[-10:]
    qkv_m, qkv_u, out_m, out_u, up_m, up_u, down_m, down_u, norm_m, norm_u = moments
    (w_qkv, w_out, w_up, w_down, norm_parts, norm_full, ext, cot_own, h1, h1_t, k_all, v_all) = (
        scratch[name] for name in NAMES[0:12]
    )
    (prob, attended, resid, h2, h2_t, cot_t, mlp, dh2, wide, act, dup, low_out) = (
        scratch[name] for name in NAMES[12:24]
    )
    delta, halo_in, scores, inverse, stack_q = (
        scratch[name] for name in ("delta", "halo_in", "scores", "inverse", "stack_q")
    )
    norm_sum, norm_c, norm_x, norm_s, sq_s, near_rows = (
        scratch[name] for name in ("norm_sum", "norm_c", "norm_x", "norm_s", "sq_s", "near_rows")
    )
    (loc_sem, halo_sem, normp_sem, gz_send, gz_recv, gf_sem, gs_sem, gc_sem, sc_sem, se_sem, sx_sem) = (
        scratch[name] for name in NAMES[-18:-7]
    )
    sz_send, sz_recv, k_t, v_t, from_cross = (
        scratch[name] for name in ("sz_send", "sz_recv", "k_t", "v_t", "from_cross")
    )
    small_sem, norm_s_sem, sq_s_sem, out_sem, back_sem = (scratch[name] for name in NAMES[-5:])

    dk_all, dv_all, dq_all, dh1, d_scores, dr_low = k_all, v_all, attended, mlp, act, h2
    S, H = seq_count, head_count
    N = S // 2
    T = cot_own.shape[0]
    R = qkv_w.shape[1]
    hidden = up_w.shape[1]
    s = lax.axis_index("seq")
    h = lax.axis_index("head")
    hx = lax.div(h, 2)
    hc = lax.rem(h, 2)
    ring = lax.div(s, 2)
    side = lax.rem(s, 2)
    other_core = (s, h + 1 - 2 * hc)
    other_x = (s, lax.rem(h + 2, H))
    other_side = (s + 1 - 2 * side, h)
    mine = hc * 2 + hx
    near = hc * 2 + 1 - hx
    mine_pair = hc * 2
    other_pair = (1 - hc) * 2
    total = S * H
    place = s * H + mine

    def device_at(number):
        number = lax.rem(number + total, total)
        block = lax.rem(number, H)
        return (lax.div(number, H), lax.rem(block, 2) * 2 + lax.div(block, 2))

    def seq_peer(i):
        return lax.rem(s + i, S)

    def remote(src, dst, send, recv, device):
        return pltpu.make_async_remote_copy(
            src_ref=src, dst_ref=dst, send_sem=send, recv_sem=recv, device_id=device, device_id_type=MESH
        )

    def rows_of(index, count):
        return pl.ds(pl.multiple_of(index * count, count), count)

    def each(low, high, step):
        def one(i, carry):
            step(i)
            return carry

        lax.fori_loop(low, high, one, 0)

    cot_copy = pltpu.make_async_copy(cot.at[rows_of(mine, T)], cot_own, loc_sem.at[3])
    cot_copy.start()

    def ext_copy(chunk):
        return pltpu.make_async_copy(
            tok.at[rows_of(jnp.maximum(mine - 2 + chunk, 0), T)],
            ext.at[pl.ds(chunk * T, T)],
            loc_sem.at[chunk],
        )

    for chunk in (2, 1, 0):

        @pl.when(mine - 2 + chunk >= 0)
        def _():
            ext_copy(chunk).start()

    moment_copies = [
        pltpu.make_async_copy(source, target, loc_sem.at[4 + k])
        for k, (source, target) in enumerate(zip(moment_refs, moments))
    ]
    for copy in moment_copies:
        copy.start()

    for t in range(3):
        w_qkv[mine, ring, side, :, t * 128 : (t + 1) * 128] = qkv_w[t].astype(BF16)
    norm_parts[s] = jnp.zeros(norm_parts.shape[1:], F32)
    norm_parts[s, 0:4, 0:R] = norm_w[...].astype(BF16).astype(F32)

    barrier = pltpu.get_barrier_semaphore()

    def greet(device):
        pl.semaphore_signal(barrier, inc=1, device_id=device, device_id_type=MESH)

    each(1, total, lambda i: greet(device_at(place + i)))
    pl.semaphore_wait(barrier, total - 1)

    spans = {
        QKV: w_qkv,
        OUT: w_out,
        UP: w_up,
        DOWN: w_down,
    }
    side_first = {QKV: True, OUT: False, UP: True, DOWN: False}
    all_ring, both_sides = pl.ds(0, N), pl.ds(0, 2)

    def piece(kind, group, a, b):
        return spans[kind].at[group, a, b]

    def ring_peer(i):
        there = lax.rem(ring + i, N)
        return there, (there * 2 + side, h)

    def gather_ring(kind, i):
        own = piece(kind, mine, ring, side)
        return remote(own, own, gz_send.at[kind, i], gz_recv.at[kind, ring], ring_peer(i)[1])

    def gather_ring_start(kind):
        each(1, N, lambda i: gather_ring(kind, i).start())

    def gather_ring_wait(kind):
        def one(i):
            there, device = ring_peer(i)
            block = piece(kind, mine, there, side)
            remote(block, block, gz_send.at[kind, i], gz_recv.at[kind, there], device).wait_recv()

        each(1, N, one)

    def gather_first(kind, sent):
        if side_first[kind]:
            block, device = piece(kind, mine, all_ring, side if sent else 1 - side), other_side
        else:
            block, device = piece(kind, mine if sent else near, all_ring, side), other_x
        return remote(block, block, gf_sem.at[0, kind], gf_sem.at[1, kind], device)

    def gather_second(kind, sent, late):
        if side_first[kind]:
            block = piece(kind, mine if sent else near, all_ring, 1 - side if late else side)
            device = other_x
        else:
            block = piece(kind, near if late else mine, all_ring, side if sent else 1 - side)
            device = other_side
        part = int(late)
        return remote(block, block, gs_sem.at[0, kind, part], gs_sem.at[1, kind, part], device)

    def gather_core(kind, pair):
        block = piece(kind, pl.ds(pair, 2), all_ring, both_sides)
        return remote(block, block, gc_sem.at[0, kind], gc_sem.at[1, kind], other_core)

    def gather_a(kind):
        gather_ring_wait(kind)
        gather_first(kind, True).start()
        gather_second(kind, True, False).start()

    def gather_b(kind):
        gather_first(kind, False).wait_recv()
        gather_second(kind, True, True).start()

    def gather_c(kind):
        gather_second(kind, False, False).wait_recv()
        gather_second(kind, False, True).wait_recv()
        gather_core(kind, mine_pair).start()

    def gather_d(kind):
        gather_core(kind, other_pair).wait_recv()

    diagonal = (other_side[0], other_x[1])

    def gather_sent(kind):
        gather_first(kind, True).wait_send()
        gather_second(kind, True, False).wait_send()
        gather_second(kind, True, True).wait_send()
        gather_core(kind, mine_pair).wait_send()
        each(1, N, lambda i: gather_ring(kind, i).wait_send())

    def norm_part(i):
        return remote(
            norm_parts.at[s], norm_parts.at[s], normp_sem.at[0, i], normp_sem.at[1, s], (seq_peer(i), h)
        )

    each(1, S, lambda i: norm_part(i).start())
    gather_ring_start(QKV)

    pieces = 4
    half = T // pieces

    def halo_copy(k):
        return remote(
            tok.at[rows_of(jnp.minimum(mine + 2, H - 1) * pieces + k, half)],
            ext.at[pl.ds(k * half, half)],
            halo_sem.at[0, k],
            halo_sem.at[1, k],
            (seq_peer(1), h),
        )

    def halo_pass(k):
        return remote(
            ext.at[pl.ds(k * half, half)],
            ext.at[pl.ds(T + k * half, half)],
            halo_sem.at[0, pieces + k],
            halo_sem.at[1, pieces + k],
            other_x,
        )

    sends_halo = (hc == 0) & (s < S - 1)
    takes_halo = (hc == 0) & (s > 0)

    @pl.when(sends_halo)
    def _():
        for k in range(pieces):
            halo_copy(k).start()

    @pl.when((hc == 0) & (s == 0))
    def _():
        ext[0:T, :] = jnp.zeros((T, ext.shape[1]), BF16)

    @pl.when((mine == 0) & (s == 0))
    def _():
        ext[T : 2 * T, :] = jnp.zeros((T, ext.shape[1]), BF16)

    w_out[mine, ring, side] = out_w[...].astype(BF16)
    w_up[mine, ring, side] = up_w[...].astype(BF16)
    w_down[mine, ring, side] = down_w[...].astype(BF16)

    first_frame = place * (T // FRAME_TOKENS)
    own_frames = T // FRAME_TOKENS

    def clip_step(c, carry):
        end, lows = carry
        start = end
        end = start + frames[c]
        lows = tuple(
            jnp.where((start <= first_frame + f) & (first_frame + f < end), start, lows[f])
            for f in range(own_frames)
        )
        return end, lows

    _, clip_low = lax.fori_loop(
        0, frames.shape[0], clip_step, (jnp.int32(0), tuple(jnp.int32(0) for _ in range(own_frames)))
    )

    gather_a(QKV)
    def norm_part_wait(i, carry):
        peer = seq_peer(i)
        part = norm_parts.at[peer]
        remote(part, part, normp_sem.at[0, i], normp_sem.at[1, peer], (peer, h)).wait_recv()
        return carry

    lax.fori_loop(1, S, norm_part_wait, 0)
    width = norm_full.shape[1]

    def norm_place(i, carry):
        part = norm_parts[i]
        wide = jnp.concatenate([part, jnp.zeros((8, width - 128), F32)], axis=1)
        return carry + pltpu.roll(wide, i * R, axis=1)

    norm_full[...] = lax.fori_loop(0, S, norm_place, jnp.zeros(norm_full.shape, F32))
    gain_one, shift_one = norm_full[0:1, :], norm_full[1:2, :]
    gain_two, shift_two = norm_full[2:3, :], norm_full[3:4, :]

    def first_norm(chunk):
        def one(b):
            at = pl.ds(pl.multiple_of(chunk * T + b * ROWS, ROWS), ROWS)
            normed, _ = normalize(ext[at, :].astype(F32))
            h1[at, :] = (normed * gain_one + shift_one).astype(BF16)

        each(0, T // ROWS, one)
        h1_t[:, chunk * T : (chunk + 1) * T] = h1[chunk * T : (chunk + 1) * T, :].T

    ext_copy(2).wait()
    first_norm(2)
    @pl.when((mine == 1) & takes_halo)
    def _():
        for k in range(pieces):
            halo_copy(k).wait_recv()
            halo_pass(k).start()

    gather_ring_start(OUT)
    gather_ring_start(UP)
    cot_copy.wait()
    cot_t[...] = cot_own[...].T
    gather_b(QKV)

    @pl.when(mine >= 1)
    def _():
        ext_copy(1).wait()

    @pl.when(mine >= 2)
    def _():
        ext_copy(0).wait()

    @pl.when((mine == 0) & takes_halo)
    def _():
        for k in range(pieces):
            halo_copy(k).wait_recv()

    first_norm(0)

    @pl.when((mine == 0) & takes_halo)
    def _():
        for k in range(pieces):
            halo_pass(k).wait_recv()

    first_norm(1)
    gather_ring_start(DOWN)

    lane = lax.broadcasted_iota(jnp.int32, (1, 128), 1)
    first_head = jnp.where(lane < HEAD_DIM, 1.0, 0.0).astype(BF16)
    second_head = jnp.where(lane < HEAD_DIM, 0.0, 1.0).astype(BF16)
    feature = lax.broadcasted_iota(jnp.int32, (128, TILE), 0)

    def two_heads(block):
        return jnp.concatenate([block * first_head, block * second_head], axis=0)

    def project(p):
        weight = flat(w_qkv[p])
        for chunk in range(3):
            at = pl.ds(chunk * T, T)
            if chunk == 2:
                out = nn(h1[at, :], weight)
                queries = out[:, 0:128].astype(BF16) * jnp.asarray(HEAD_DIM**-0.5, BF16)
                for i in range(T // TILE):
                    stack_q[p, i * 2 * TILE : (i + 1) * 2 * TILE, :] = two_heads(queries[i * TILE : (i + 1) * TILE])
                out = out[:, 128:384]
            else:
                out = nn(h1[at, :], flat(w_qkv[p, :, :, :, 128:384]))
            k_all[p, at, :] = out[:, 0:128].astype(BF16)
            v_all[p, at, :] = out[:, 128:256].astype(BF16)
            k_t[p, :, at] = k_all[p, at, :].T
            v_t[p, :, at] = v_all[p, at, :].T

    def own_halves(block):
        return jnp.where(feature < HEAD_DIM, block[:, 0:TILE], block[:, TILE : 2 * TILE])

    key_frames = KEYS // FRAME_TOKENS

    def bias_of(i):
        query_lane = lax.broadcasted_iota(jnp.int32, (key_frames, 1, 2 * TILE), 2)
        later = lax.rem(query_lane, TILE) >= FRAME_TOKENS
        low = jnp.where(later, clip_low[2 * i + 1], clip_low[2 * i])
        high = first_frame + 2 * i + later.astype(jnp.int32)
        key_frame = (
            first_frame
            - MOST_FRAMES
            + 2 * i
            + lax.broadcasted_iota(jnp.int32, (key_frames, 1, 2 * TILE), 0)
        )
        return jnp.where((key_frame >= low) & (key_frame <= high), 0.0, MASKED).astype(F32)

    biases = [bias_of(i) for i in range(T // TILE)]

    def attend(p, between):
        for i in range(T // TILE):
            for step in between.get(i, ()):
                step()
            own = pl.ds(i * TILE, TILE)
            window = pl.ds(i * TILE, KEYS)
            raw = scores.at[pl.ds(i % 2 * KEYS, KEYS)]
            raw[...] = nt(k_all[p, window, :], stack_q[p, i * 2 * TILE : (i + 1) * 2 * TILE, :])
            highest = jnp.full((8, 2 * TILE), MASKED, F32)
            for c in range(KEYS // TILE):
                block = raw[c * TILE : (c + 1) * TILE, :].reshape(2, FRAME_TOKENS, 2 * TILE)
                block = (block + biases[i][2 * c : 2 * c + 2]).reshape(TILE // 8, 8, 2 * TILE)
                highest = jnp.maximum(highest, jnp.max(block, axis=0))
            shift = biases[i] - jnp.max(highest, axis=0, keepdims=True)
            sums = jnp.zeros((8, 2 * TILE), F32)
            for c in range(KEYS // TILE):
                block = raw[c * TILE : (c + 1) * TILE, :].reshape(2, FRAME_TOKENS, 2 * TILE)
                block = jnp.exp(block + shift[2 * c : 2 * c + 2]).reshape(TILE // 8, 8, 2 * TILE)
                sums = sums + jnp.sum(block, axis=0)
                prob[p, (i + c) * TILE : (i + c + 1) * TILE, i * 2 * TILE : (i + 1) * 2 * TILE] = block.reshape(
                    TILE, 2 * TILE
                ).astype(BF16)
            scale = 1.0 / jnp.sum(sums, axis=0, keepdims=True)
            inverse[p, i] = scale
            low = prob[p, window, i * 2 * TILE : (i + 1) * 2 * TILE]
            mixed = own_halves(nn(v_t[p, :, window], low) * scale)
            attended[p, own, :] = mixed.T.astype(BF16)

    def clear(p):
        for i in range(T // TILE):
            columns = slice(i * 2 * TILE, (i + 1) * 2 * TILE)
            if i:
                prob[p, 0 : i * TILE, columns] = jnp.zeros((i * TILE, 2 * TILE), BF16)
            below = i * TILE + KEYS
            if below < 3 * T:
                prob[p, below : 3 * T, columns] = jnp.zeros((3 * T - below, 2 * TILE), BF16)

    each(0, H, clear)

    do = functools.partial
    project(mine)
    attend(mine, {3: [do(gather_a, OUT)]})
    gather_c(QKV)
    gather_a(UP)
    project(near)
    attend(near, {0: [do(gather_a, DOWN)], 2: [do(gather_b, OUT)]})
    gather_d(QKV)
    project(other_pair)
    attend(other_pair, {0: [do(gather_b, UP)], 1: [do(gather_b, DOWN)], 2: [do(gather_c, OUT)]})
    project(other_pair + 1)
    attend(other_pair + 1, {1: [do(gather_d, OUT)], 3: [do(gather_c, UP)]})
    gather_c(DOWN)

    acc = nt(attended[0], flat(w_out[0]))
    for p in range(1, H):
        acc = acc + nt(attended[p], flat(w_out[p]))
    resid[...] = acc

    def second_norm(b):
        at = rows_of(b, ROWS)
        whole = ext[pl.ds(pl.multiple_of(2 * T + b * ROWS, ROWS), ROWS), :].astype(F32) + resid[at, :]
        resid[at, :] = whole
        normed, _ = normalize(whole)
        h2[at, :] = (normed * gain_two + shift_two).astype(BF16)

    each(0, T // ROWS, second_norm)
    h2_t[...] = h2[...].T
    gather_d(UP)
    gather_d(DOWN)

    endings = ("down", "up", "out", "qkv")
    grads, from_core, from_side, from_x, from_ring = (
        [scratch.get(start + name) for name in endings] for start in ("g_", "c_", "e_", "x_", "s_")
    )
    grads[QKV] = w_up.at[:, :, :, :, pl.ds(0, w_qkv.shape[-1])]

    def in_order(k):
        return (other_pair, other_pair + 1, near, mine)[k]

    def scatter_core(kind, group, slot):
        return remote(
            grads[kind].at[group],
            from_core[kind].at[slot],
            sc_sem.at[0, kind, slot],
            sc_sem.at[1, kind, slot],
            other_core,
        )

    def scatter_side(kind, group):
        slot = group - mine_pair
        return remote(
            grads[kind].at[group, all_ring, 1 - side],
            from_side[kind].at[slot],
            se_sem.at[0, kind, slot],
            se_sem.at[1, kind, slot],
            other_side,
        )

    def cross_x():
        return remote(grads[UP].at[near], from_cross, sx_sem.at[0, UP], sx_sem.at[1, UP], other_x)

    def cross_side():
        return remote(
            grads[UP].at[mine, all_ring, 1 - side],
            from_side[UP].at[0],
            se_sem.at[0, UP, 0],
            se_sem.at[1, UP, 0],
            other_side,
        )

    def cross_a():
        cross_x().wait_recv()

        def add(there, b):
            grads[UP][mine, there, b] = (
                grads[UP][mine, there, b].astype(F32) + from_cross[there, b].astype(F32)
            ).astype(BF16)

        each(0, N, lambda there: add(there, 1 - side))
        cross_side().start()
        each(0, N, lambda there: add(there, side))

    def cross_b():
        cross_side().wait_recv()

        def add(there):
            grads[UP][mine, there, side] = (
                grads[UP][mine, there, side].astype(F32) + from_side[UP][0, there].astype(F32)
            ).astype(BF16)

        each(0, N, add)
        each(1, N, lambda i: scatter_ring(UP, i).start())

    def place_grad(kind, k, matrix):
        group = in_order(k)
        if k < 2:
            grads[kind][group] = cut(matrix, N)
            scatter_core(kind, group, k).start()
        else:
            slot = group - mine_pair
            scatter_core(kind, group, slot).wait_recv()
            grads[kind][group] = cut(matrix + flat(from_core[kind][slot]).astype(F32), N)
            if kind != UP:
                scatter_side(kind, group).start()
            elif k == 2:
                cross_x().start()

    def scatter_side_sum(kind, group):
        scatter_side(kind, group).wait_recv()
        slot = group - mine_pair

        def add(b):
            grads[kind][group, b, side] = (
                grads[kind][group, b, side].astype(F32) + from_side[kind][slot, b].astype(F32)
            ).astype(BF16)

        each(0, N, add)

    def scatter_x(kind):
        return remote(
            grads[kind].at[near, all_ring, side],
            from_x[kind],
            sx_sem.at[0, kind],
            sx_sem.at[1, kind],
            other_x,
        )

    def scatter_ring(kind, i):
        there, device = ring_peer(i)
        return remote(
            grads[kind].at[mine, there, side],
            from_ring[kind].at[ring],
            sz_send.at[kind, i],
            sz_recv.at[kind, ring],
            device,
        )

    def scatter_a(kind):
        scatter_side_sum(kind, near)
        scatter_x(kind).start()

    def scatter_b(kind):
        scatter_side_sum(kind, mine)
        scatter_x(kind).wait_recv()

        def add(b):
            grads[kind][mine, b, side] = (
                grads[kind][mine, b, side].astype(F32) + from_x[kind][b].astype(F32)
            ).astype(BF16)

        each(0, N, add)
        each(1, N, lambda i: scatter_ring(kind, i).start())

    def scatter_c(kind):
        landed = from_ring[kind]

        def one(i, carry):
            there, device = ring_peer(i)
            remote(
                grads[kind].at[mine, there, side],
                landed.at[there],
                sz_send.at[kind, i],
                sz_recv.at[kind, there],
                device,
            ).wait_recv()
            return carry + landed[there].astype(F32)

        return lax.fori_loop(1, N, one, grads[kind][mine, ring, side].astype(F32))

    mlp[...] = jnp.zeros_like(mlp)
    dh2[...] = jnp.zeros_like(dh2)
    half_hidden = hidden // 2

    def part_of(k, which, column, low_row, high_row):
        buffer = wide if k % 2 == 0 else scores
        start = (2 * which + column) * T
        return buffer.at[pl.ds(start + low_row, high_row - low_row), :]

    def inner(k):
        for column in range(2):
            columns = slice(column * half_hidden, (column + 1) * half_hidden)
            part_of(k, 0, column, 0, T)[...] = nn(h2[...], flat(w_up[in_order(k), :, :, :, columns]))
            part_of(k, 1, column, 0, T)[...] = nn(cot_own[...], flat(w_down[in_order(k), :, :, :, columns]))

    def slot(k):
        return pl.ds(k % 2 * hidden, hidden)

    def pointwise(k):
        for b in range(T // 128):
            for column in range(2):
                low_row, high_row = b * 128, (b + 1) * 128
                value, slope = gelu_both(part_of(k, 0, column, low_row, high_row)[...])
                at = pl.ds(k % 2 * hidden + column * half_hidden, half_hidden)
                act[low_row:high_row, at] = value.astype(BF16)
                dup[low_row:high_row, at] = (part_of(k, 1, column, low_row, high_row)[...] * slope).astype(BF16)

    def outer(k):
        mlp[...] += nt(act[:, slot(k)], flat(w_down[in_order(k)]))
        dh2[...] += nt(dup[:, slot(k)], flat(w_up[in_order(k)]))
        place_grad(DOWN, k, nn(cot_t[...], act[:, slot(k)]))
        place_grad(UP, k, nn(h2_t[...], dup[:, slot(k)]))

    inner(0)
    for k in range(H):
        if k + 1 < H:
            inner(k + 1)
        pointwise(k)
        outer(k)

    def finish_rows(target, low, at_sem):
        def slab(block):
            return target.at[rows_of(block, T)]

        keep = pltpu.make_async_copy(low, slab(mine), out_sem.at[at_sem, 0])
        landed = near_rows.at[at_sem]
        to_x = remote(low, landed, out_sem.at[at_sem, 1], out_sem.at[at_sem, 2], other_x)
        to_core = remote(low, slab(mine), out_sem.at[at_sem, 3], out_sem.at[at_sem, 4], other_core)
        passed = remote(landed, slab(near), out_sem.at[at_sem, 5], out_sem.at[at_sem, 6], other_core)
        store = pltpu.make_async_copy(landed, slab(near), out_sem.at[at_sem, 7])
        return keep, to_x, to_core, passed, store

    def sum_out(b):
        at = rows_of(b, ROWS)
        low_out[at, :] = (resid[at, :] + mlp[at, :]).astype(BF16)

    each(0, T // ROWS, sum_out)
    out_copies = finish_rows(block_out, low_out, 0)

    def second_back(b, carry):
        gain_sum, shift_sum = carry
        at = rows_of(b, ROWS)
        normed, inverse = normalize(resid[at, :])
        grad = dh2[at, :]
        mixed = cot_own[at, :].astype(F32) + norm_back(grad, normed, inverse, gain_two)
        resid[at, :] = mixed
        dr_low[at, :] = mixed.astype(BF16)
        gain_sum = gain_sum + jnp.sum(grad * normed, axis=0, keepdims=True)
        shift_sum = shift_sum + jnp.sum(grad, axis=0, keepdims=True)
        return gain_sum, shift_sum

    zero_row = jnp.zeros((1, width), F32)
    gain_two_grad, shift_two_grad = lax.fori_loop(0, T // ROWS, second_back, (zero_row, zero_row))

    def stack_d(p):
        return h1.at[pl.ds(0, 2 * T), pl.ds(pl.multiple_of(p * 128, 128), 128)]

    lane_first = lax.broadcasted_iota(jnp.int32, (TILE, 128), 1) < HEAD_DIM

    def deltas(p, d_att):
        for i in range(T // TILE):
            own = pl.ds(i * TILE, TILE)
            row = inverse[p, i]
            turned = jnp.concatenate([row[:, 0:TILE], row[:, TILE : 2 * TILE], jnp.zeros((6, TILE), F32)], axis=0).T
            scaled = d_att[i * TILE : (i + 1) * TILE].astype(F32) * jnp.where(lane_first, turned[:, 0:1], turned[:, 1:2])
            low = scaled.astype(BF16)
            stack_d(p)[i * 2 * TILE : (i + 1) * 2 * TILE, :] = two_heads(low)
            products = (low.astype(F32) * attended[p, own, :].astype(F32)).T
            delta[p, :, i * 2 * TILE : (i + 1) * 2 * TILE] = jnp.concatenate(
                [
                    jnp.sum(products[0:HEAD_DIM], axis=0, keepdims=True),
                    jnp.sum(products[HEAD_DIM:128], axis=0, keepdims=True),
                ],
                axis=1,
            )

    h2_t[...] = dr_low[...].T
    for k in range(H):
        p = in_order(k)
        deltas(p, nn(dr_low[...], flat(w_out[p])).astype(BF16))
        place_grad(OUT, k, nn(h2_t[...], attended[p]))

    gather_sent(UP)
    scatter_a(DOWN)
    cross_a()
    for copy in out_copies[:3]:
        copy.start()

    def dq_acc(p, i):
        return wide.at[pl.ds(pl.multiple_of((p * (T // TILE) + i) * TILE, TILE), TILE), pl.ds(0, TILE)]

    def attend_back(chunk, p):
        at = pl.ds(chunk * T, T)
        grads_p = stack_d(p)[...]
        for i in range(T // TILE):
            d_prob = scores.at[pl.ds(i * T, T)]
            d_prob[...] = nt(v_all[p, at, :], grads_p[i * 2 * TILE : (i + 1) * 2 * TILE])
        for r in range(T // TILE):
            rows = slice(r * TILE, (r + 1) * TILE)
            for i in range(T // TILE):
                columns = slice(i * 2 * TILE, (i + 1) * 2 * TILE)
                if (chunk == 0 and i > r) or (chunk == 2 and i < r):
                    d_scores[rows, columns] = jnp.zeros((TILE, 2 * TILE), BF16)
                else:
                    low = prob[p, chunk * T + r * TILE : chunk * T + (r + 1) * TILE, columns].astype(F32)
                    d_scores[rows, columns] = (low * (scores[i * T + r * TILE : i * T + (r + 1) * TILE, :] - delta[p, :, columns])).astype(BF16)
        dv_all[p, at, :] = nn(prob[p, at, :], grads_p).astype(BF16)
        dk_all[p, at, :] = nn(d_scores[...], stack_q[p]).astype(BF16)
        dq_part = nn(k_t[p, :, at], d_scores[...])
        for i in range(T // TILE):
            own = pl.ds(i * TILE, TILE)
            part = own_halves(dq_part[:, i * 2 * TILE : (i + 1) * 2 * TILE])
            if chunk == 0:
                dq_acc(p, i)[...] = part
            elif chunk == 1:
                dq_acc(p, i)[...] += part
            else:
                dq_all[p, own, :] = ((dq_acc(p, i)[...] + part) * (HEAD_DIM**-0.5)).T.astype(BF16)

    def back_copy(chunk):
        return remote(
            dup.at[:, pl.ds(chunk * width, width)],
            halo_in.at[chunk],
            back_sem.at[0, chunk],
            back_sem.at[1, chunk],
            device_at(place - 2 + chunk),
        )

    def sends_back(chunk):
        return place >= 2 - chunk

    def takes_back(chunk):
        return place < total - (2 - chunk)

    for chunk in range(2):

        @pl.when(jnp.logical_not(takes_back(chunk)))
        def _():
            halo_in[chunk] = jnp.zeros(halo_in.shape[1:], BF16)

    def first_sums(chunk, carry):
        def one(b, inner):
            gain_sum, shift_sum = inner
            at = pl.ds(pl.multiple_of(chunk * T + b * ROWS, ROWS), ROWS)
            normed, _ = normalize(ext[at, :].astype(F32))
            grad = dh1[rows_of(b, ROWS), :]
            if chunk < 2:
                dup[rows_of(b, ROWS), chunk * width : (chunk + 1) * width] = grad.astype(BF16)
            return (
                gain_sum + jnp.sum(grad * normed, axis=0, keepdims=True),
                shift_sum + jnp.sum(grad, axis=0, keepdims=True),
            )

        return lax.fori_loop(0, T // ROWS, one, carry)

    def halo_back(p, chunk):
        at = pl.ds(chunk * T, T)
        both = jnp.concatenate([dk_all[p, at, :], dv_all[p, at, :]], axis=1)
        return nt(both, flat(w_qkv[p, :, :, :, 128:384]))

    sums = (zero_row, zero_row)
    for chunk in range(2):
        dh1[...] = jnp.zeros_like(dh1)

        def one(p, chunk=chunk):
            attend_back(chunk, p)
            dh1[...] += halo_back(p, chunk)

        each(0, 2, one)
        if chunk == 1:
            scatter_a(OUT)
        each(2, 4, one)
        sums = first_sums(chunk, sums)

        @pl.when(sends_back(chunk))
        def _():
            back_copy(chunk).start()

        if chunk == 0:
            scatter_b(DOWN)
            cross_b()

    dh1[...] = jnp.zeros_like(dh1)
    for k in range(H):
        p = in_order(k)
        each(p, p + 1, lambda q: attend_back(2, q))
        weight = flat(w_qkv[p])
        at = pl.ds(2 * T, T)
        three = jnp.concatenate([dq_all[p], dk_all[p, at, :], dv_all[p, at, :]], axis=1)
        dh1[...] += nt(three, weight)
        both = jnp.concatenate([dk_all[p], dv_all[p]], axis=1)
        columns = [nn(h1_t[:, 2 * T : 3 * T], dq_all[p]), nn(h1_t[...], both)]
        place_grad(QKV, k, jnp.concatenate(columns, axis=1))
        if k == 1:
            out_copies[1].wait_recv()
            out_copies[3].start()
            out_copies[4].start()
        if k == 2:
            scatter_b(OUT)

    gain_one_grad, shift_one_grad = first_sums(2, sums)
    norm_sum[...] = jnp.concatenate(
        [gain_one_grad, shift_one_grad, gain_two_grad, shift_two_grad, jnp.zeros((4, width), F32)], axis=0
    )
    norm_to_core = remote(norm_sum, norm_c, small_sem.at[0], small_sem.at[1], other_core)
    norm_to_core.start()
    scatter_a(QKV)
    norm_to_core.wait()
    norm_sum[...] += norm_c[...]
    plane = (other_x, other_side, diagonal)
    norm_plane = [
        remote(norm_sum, norm_x.at[k], small_sem.at[2 + k], small_sem.at[5 + k], device)
        for k, device in enumerate(plane)
    ]
    for copy in norm_plane:
        copy.start()

    for chunk in range(2):

        @pl.when(takes_back(chunk))
        def _():
            back_copy(chunk).wait_recv()

    def first_back(b):
        at = rows_of(b, ROWS)
        normed, inverse = normalize(ext[pl.ds(pl.multiple_of(2 * T + b * ROWS, ROWS), ROWS), :].astype(F32))
        grad = dh1[at, :] + halo_in[0, at, :].astype(F32) + halo_in[1, at, :].astype(F32)
        dr_low[at, :] = (resid[at, :] + norm_back(grad, normed, inverse, gain_one)).astype(BF16)

    each(0, T // ROWS, first_back)
    grad_copies = finish_rows(input_grad, dr_low, 1)
    for copy in grad_copies[:3]:
        copy.start()
    scatter_b(QKV)
    for copy in norm_plane:
        copy.wait()
    norm_sum[...] += norm_x[0] + (norm_x[1] + norm_x[2])

    def norm_ring(i):
        return remote(
            norm_sum, norm_s.at[ring], norm_s_sem.at[0, i], norm_s_sem.at[1, ring], ring_peer(i)[1]
        )

    each(1, N, lambda i: norm_ring(i).start())

    for copy in moment_copies:
        copy.wait()
    down_total = scatter_c(DOWN)
    down_g[...] = down_total
    up_total = scatter_c(UP)
    up_g[...] = up_total
    out_total = scatter_c(OUT)
    out_g[...] = out_total

    def sums_of(master, moment, square, gradient):
        _, _, direction = lamb_direction(master, moment, square, gradient)
        return jnp.sum(master * master), jnp.sum(direction * direction)

    down_sums = sums_of(down_w[...], down_m[...], down_u[...], down_total)
    up_sums = sums_of(up_w[...], up_m[...], up_u[...], up_total)
    out_sums = sums_of(out_w[...], out_m[...], out_u[...], out_total)

    def norm_ring_wait(i, carry):
        there, device = ring_peer(i)
        remote(
            norm_sum, norm_s.at[there], norm_s_sem.at[0, i], norm_s_sem.at[1, there], device
        ).wait_recv()
        return carry + norm_s[there]

    norm_total = lax.fori_loop(1, N, norm_ring_wait, norm_sum[...])
    norm_mine = pltpu.roll(norm_total, lax.rem(width - s * R, width), axis=1)[0:4, 0:R]
    norm_g[...] = norm_mine
    once = jnp.where(h == 0, 1.0, 0.0).astype(F32)
    norm_sums = sums_of(norm_w[...], norm_m[...], norm_u[...], norm_mine)
    norm_sums = (norm_sums[0] * once, norm_sums[1] * once)

    qkv_total = scatter_c(QKV)
    weight_sum, update_sum = jnp.float32(0.0), jnp.float32(0.0)
    for t in range(3):
        part = qkv_total[:, t * 128 : (t + 1) * 128]
        qkv_g[t] = part
        pair = sums_of(qkv_w[t], qkv_m[t], qkv_u[t], part)
        weight_sum, update_sum = weight_sum + pair[0], update_sum + pair[1]
    qkv_sums = (weight_sum, update_sum)

    row = lax.broadcasted_iota(jnp.int32, (8, 128), 0)
    column = lax.broadcasted_iota(jnp.int32, (8, 128), 1)
    both = jnp.zeros((8, 128), F32)
    for number, pair in enumerate((qkv_sums, out_sums, up_sums, down_sums, norm_sums)):
        for which in range(2):
            both = jnp.where((row == which) & (column == number), pair[which], both)
    squares[...] = both

    def sq_copy(i):
        peer = lax.rem(place + i, total)
        return remote(squares, sq_s.at[place], sq_s_sem.at[0, i], sq_s_sem.at[1, place], device_at(peer))

    def sq_wait(i, carry):
        peer = lax.rem(place + i, total)
        remote(
            squares, sq_s.at[peer], sq_s_sem.at[0, i], sq_s_sem.at[1, peer], device_at(peer)
        ).wait_recv()
        return carry

    each(1, total, lambda i: sq_copy(i).start())
    grad_copies[1].wait_recv()
    grad_copies[3].start()
    grad_copies[4].start()
    lax.fori_loop(1, total, sq_wait, 0)
    sq_s[place] = both
    each(1, total, lambda i: sq_copy(i).wait_send())
    squares[...] = lax.fori_loop(0, total, lambda i, carry: carry + sq_s[i], jnp.zeros((8, 128), F32))

    for copies in (out_copies, grad_copies):
        keep, to_x, to_core, passed, store = copies
        keep.wait()
        store.wait()
        to_x.wait_send()
        to_core.wait_send()
        passed.wait_send()
        to_core.wait_recv()
        passed.wait_recv()

    for k in range(pieces):

        @pl.when(sends_halo)
        def _():
            halo_copy(k).wait_send()

        @pl.when((mine == 1) & takes_halo)
        def _():
            halo_pass(k).wait_send()

    for chunk in range(2):

        @pl.when(sends_back(chunk))
        def _():
            back_copy(chunk).wait_send()

    for kind in (QKV, OUT, DOWN):
        gather_sent(kind)
    for kind in (QKV, OUT, UP, DOWN):
        for k in range(2):
            scatter_core(kind, in_order(k), k).wait_send()
        if kind == UP:
            cross_x().wait_send()
            cross_side().wait_send()
        else:
            scatter_side(kind, near).wait_send()
            scatter_side(kind, mine).wait_send()
            scatter_x(kind).wait_send()

    def drain(i):
        norm_part(i).wait_send()

    each(1, S, drain)

    def drain_ring(i):
        norm_ring(i).wait_send()
        for kind in (QKV, OUT, UP, DOWN):
            scatter_ring(kind, i).wait_send()

    each(1, N, drain_ring)


def run_layer(mesh_sizes, tok, cot, frames, weights, moments, seconds):
    S, H = mesh_sizes
    rows_dev, width = tok.shape
    T = rows_dev // H
    R = weights[0].shape[1]
    N = S // 2
    assert H == 4 and S % 2 == 0 and 2 * T == MOST_FRAMES * FRAME_TOKENS and R * S == width
    hidden = weights[2].shape[1]
    assert hidden == T == 4 * TILE
    any_space = pl.BlockSpec(memory_space=pl.ANY)
    vmem = pl.BlockSpec(memory_space=pltpu.VMEM)
    smem = pl.BlockSpec(memory_space=pltpu.SMEM)
    dma = pltpu.SemaphoreType.DMA
    out_shape = (
        jax.ShapeDtypeStruct((rows_dev, width), BF16),
        jax.ShapeDtypeStruct((rows_dev, width), BF16),
        *[jax.ShapeDtypeStruct(w.shape, F32) for w in weights],
        jax.ShapeDtypeStruct((8, 128), F32),
    )
    cols = {"down": hidden, "up": hidden, "out": 128, "qkv": 384}
    kinds = ("down", "up", "out", "qkv")
    low, full = functools.partial(pltpu.VMEM, dtype=BF16), functools.partial(pltpu.VMEM, dtype=F32)
    scratch = dict(
        norm_parts=full((S, 8, 128)),
        norm_full=full((8, width)),
        ext=low((3 * T, width)),
        cot_own=low((T, width)),
        h1=low((3 * T, width)),
        h1_t=low((width, 3 * T)),
        k_all=low((H, 3 * T, 128)),
        v_all=low((H, 3 * T, 128)),
        prob=low((H, 3 * T, 2 * T)),
        scores=full((2 * KEYS, 2 * TILE)),
        inverse=full((H, T // TILE, 1, 2 * TILE)),
        stack_q=low((H, 2 * T, 128)),
        attended=low((H, T, 128)),
        resid=full((T, width)),
        h2=low((T, width)),
        h2_t=low((width, T)),
        cot_t=low((width, T)),
        mlp=full((T, width)),
        dh2=full((T, width)),
        wide=full((4 * T, 2 * TILE)),
        act=low((T, 2 * hidden)),
        dup=low((T, 2 * hidden)),
        low_out=low((T, width)),
        delta=full((H, 1, 2 * T)),
        halo_in=low((2, T, width)),
        norm_sum=full((8, width)),
        norm_c=full((8, width)),
        norm_x=full((3, 8, width)),
        norm_s=full((N, 8, width)),
        sq_s=full((S * H, 8, 128)),
        k_t=low((H, 128, 3 * T)),
        v_t=low((H, 128, 3 * T)),
        from_cross=low((N, 2, R, hidden)),
        loc_sem=dma((14,)),
        halo_sem=dma((2, 8)),
        normp_sem=dma((2, S)),
        gz_send=dma((4, N)),
        gz_recv=dma((4, N)),
        gf_sem=dma((2, 4)),
        gs_sem=dma((2, 4, 2)),
        gc_sem=dma((2, 4)),
        sc_sem=dma((2, 4, 2)),
        se_sem=dma((2, 4, 2)),
        sx_sem=dma((2, 4)),
        sz_send=dma((4, N)),
        sz_recv=dma((4, N)),
        small_sem=dma((14,)),
        norm_s_sem=dma((2, N)),
        sq_s_sem=dma((2, S * H)),
        out_sem=dma((2, 8)),
        near_rows=low((2, T, width)),
        back_sem=dma((2, 2)),
    )
    for kind in kinds:
        scratch["w_" + kind] = low((H, N, 2, R, cols[kind]))
        if kind != "qkv":
            scratch["g_" + kind] = low((H, N, 2, R, cols[kind]))
        scratch["c_" + kind] = low((2, N, 2, R, cols[kind]))
        scratch["e_" + kind] = low((2, N, R, cols[kind]))
        scratch["s_" + kind] = low((N, R, cols[kind]))
        if kind != "up":
            scratch["x_" + kind] = low((N, R, cols[kind]))
    operands = [tok, cot, frames, *weights]
    for moment, second in zip(moments, seconds):
        operands += [moment, second]
    return pl.pallas_call(
        functools.partial(layer_kernel, S, H),
        out_shape=out_shape,
        in_specs=[any_space, any_space, smem] + [vmem] * 5 + [any_space] * 10,
        out_specs=(any_space, any_space) + (vmem,) * 6,
        scratch_shapes=[scratch[name] for name in NAMES]
        + [pltpu.VMEM(array.shape, F32) for array in operands[8:18]],
        compiler_params=pltpu.CompilerParams(
            collective_id=0, has_side_effects=True, vmem_limit_bytes=63 * 2**20
        ),
        name="layer",
    )(*operands)


CHUNKS = 4


def update_kernel(count, *refs):
    block_low, grad_low = refs[0:2]
    sources = refs[2:23]
    block_out, input_grad = refs[23:25]
    targets = refs[25 : 25 + count]
    rest = refs[25 + count :]
    loaded, made = rest[0:21], rest[21 : 21 + count]
    low, wide, block, sem, load_sem, store_sem = rest[21 + count :]
    rows = low.shape[1]
    block_load = pltpu.make_async_copy(block_low, block, sem.at[0, 0])
    block_store = pltpu.make_async_copy(block, block_out, sem.at[0, 1])
    loads = [
        pltpu.make_async_copy(grad_low.at[pl.ds(c * rows, rows)], low.at[c], sem.at[1, c]) for c in range(CHUNKS)
    ]
    stores = [
        pltpu.make_async_copy(wide.at[c], input_grad.at[pl.ds(c * rows, rows)], sem.at[2, c])
        for c in range(CHUNKS)
    ]
    small_loads = [
        pltpu.make_async_copy(source, target, load_sem.at[k])
        for k, (source, target) in enumerate(zip(sources, loaded))
    ]
    small_stores = [
        pltpu.make_async_copy(source, target, store_sem.at[k])
        for k, (source, target) in enumerate(zip(made, targets))
    ]
    for copy in loads:
        copy.start()
    for copy in small_loads:
        copy.start()
    block_load.start()
    for c in range(CHUNKS):
        loads[c].wait()
        wide[c] = low[c].astype(F32)
        stores[c].start()
    for copy in small_loads:
        copy.wait()
    grads, masters, firsts, seconds = loaded[0:5], loaded[5:10], loaded[10:15], loaded[15:20]
    roots = jnp.sqrt(loaded[20][...])
    for number in (3, 2, 0, 1, 4):
        outs_here = made[5 * number : 5 * number + 5]
        ratio = roots[0:1, number : number + 1] / roots[1:2, number : number + 1]
        pieces = range(grads[number].shape[0]) if len(grads[number].shape) == 3 else (slice(None),)
        for piece in pieces:
            gradient, master = grads[number][piece], masters[number][piece]
            first, second, direction = lamb_direction(
                master, firsts[number][piece], seconds[number][piece], gradient
            )
            new_master = master - RATE * ratio * direction
            outs_here[0][piece] = gradient
            outs_here[1][piece] = first
            outs_here[2][piece] = second
            outs_here[3][piece] = new_master
            outs_here[4][piece] = new_master.astype(BF16)
        for copy in small_stores[5 * number : 5 * number + 5]:
            copy.start()
    made[25][...] = roots[0:2, 0:5]
    small_stores[25].start()
    block_load.wait()
    block_store.start()
    for copy in (*stores, *small_stores, block_store):
        copy.wait()


def run_update(block_low, grad_low, grads, masters, firsts, seconds, squares):
    any_space = pl.BlockSpec(memory_space=pl.ANY)
    operands = [block_low, grad_low, *grads, *masters, *firsts, *seconds, squares]
    rows, width = block_low.shape
    out_shape = [jax.ShapeDtypeStruct((rows, width), BF16), jax.ShapeDtypeStruct((rows, width), F32)]
    for grad in grads:
        out_shape += [jax.ShapeDtypeStruct(grad.shape, F32)] * 4 + [jax.ShapeDtypeStruct(grad.shape, BF16)]
    out_shape.append(jax.ShapeDtypeStruct((2, 5), F32))
    small = [(array.shape, array.dtype) for array in operands[2:] + out_shape[2:]]
    count = len(out_shape) - 2
    return pl.pallas_call(
        functools.partial(update_kernel, count),
        out_shape=tuple(out_shape),
        in_specs=[any_space] * len(operands),
        out_specs=(any_space,) * len(out_shape),
        scratch_shapes=[pltpu.VMEM(shape, dtype) for shape, dtype in small]
        + [
            pltpu.VMEM((CHUNKS, rows // CHUNKS, width), BF16),
            pltpu.VMEM((CHUNKS, rows // CHUNKS, width), F32),
            pltpu.VMEM((rows, width), BF16),
            pltpu.SemaphoreType.DMA((3, CHUNKS)),
            pltpu.SemaphoreType.DMA((21,)),
            pltpu.SemaphoreType.DMA((count,)),
        ],
        compiler_params=pltpu.CompilerParams(vmem_limit_bytes=63 * 2**20),
        name="update",
    )(*operands)


def local(mesh_sizes, *arrays):
    tokens, cotangent, frames = arrays[0:3]
    tensors = [list(arrays[3 + 3 * i : 6 + 3 * i]) for i in range(5)]
    for i in (1, 3):
        tensors[i] = [array.T for array in tensors[i]]
    masters, firsts, seconds = ([tensor[i] for tensor in tensors] for i in range(3))
    results = run_layer(mesh_sizes, tokens, cotangent, frames, masters, firsts, seconds)
    updated = run_update(results[0], results[1], results[2:7], masters, firsts, seconds, results[7])
    outs = list(updated[0:2])
    for i in range(5):
        five = updated[2 + 5 * i : 7 + 5 * i]
        outs += [array.T for array in five] if i in (1, 3) else list(five)
    outs.append(updated[27].T)
    return tuple(outs)


def solution(mesh):
    qkv, turned, straight, row = P(None, "seq", "head"), P("head", "seq"), P("seq", "head"), P(None, "seq")
    kinds = (qkv, turned, straight, turned, row)
    in_specs = [P("seq", None), P("seq", None), P()]
    out_specs = [P("seq", None), P("seq", None)]
    for kind in kinds:
        in_specs += [kind] * 3
        out_specs += [kind] * 5
    out_specs.append(P())
    return jax.shard_map(
        functools.partial(local, (mesh.shape["seq"], mesh.shape["head"])),
        mesh=mesh,
        in_specs=tuple(in_specs),
        out_specs=tuple(out_specs),
        check_vma=False,
    )
```

```python
import functools

import jax
import jax.numpy as jnp
from jax import lax
from jax.experimental import pallas as pl
from jax.experimental.pallas import tpu as pltpu
from jax.sharding import PartitionSpec as P

HEAD_DIM = 64
FRAME_TOKENS = 64
MOST_FRAMES = 16
STEP = 5

EPS_NORM = 1e-05
BETA_ONE = 0.5
BETA_TWO = 0.6
RATE = 0.3
DECAY = 0.01
EPS_ADAM = 1e-06
MASKED = -1e30

MESH = pl.DeviceIdType.MESH
F32 = jnp.float32
BF16 = jnp.bfloat16
TILE = 128
KEYS = MOST_FRAMES * FRAME_TOKENS + TILE
ROWS = 256

DOWN, UP, OUT, QKV = range(4)


def nn(a, b):
    return lax.dot_general(a, b, (((1,), (0,)), ((), ())), preferred_element_type=F32)


def nt(a, b):
    return lax.dot_general(a, b, (((1,), (1,)), ((), ())), preferred_element_type=F32)


def tn(a, b):
    return lax.dot_general(a, b, (((0,), (0,)), ((), ())), preferred_element_type=F32)


def normalize(values):
    average = jnp.mean(values, axis=-1, keepdims=True)
    centered = values - average
    variance = jnp.mean(centered * centered, axis=-1, keepdims=True)
    inverse = lax.rsqrt(variance + EPS_NORM)
    return centered * inverse, inverse


def norm_back(gradient, normed, inverse, gain_row):
    scaled = gradient * gain_row
    return inverse * (
        scaled
        - jnp.mean(scaled, axis=-1, keepdims=True)
        - normed * jnp.mean(scaled * normed, axis=-1, keepdims=True)
    )


def gelu_both(inner):
    root = 0.7978845608028654
    cube = 0.044715
    square = inner * inner
    curved = jnp.tanh(root * inner * (1.0 + cube * square))
    half = 0.5 * (1.0 + curved)
    value = inner * half
    slope = half + 0.5 * inner * (1.0 - curved * curved) * (root * (1.0 + 3.0 * cube * square))
    return value, slope


def lamb_direction(master, moment, square, gradient):
    new_first = BETA_ONE * moment + (1.0 - BETA_ONE) * gradient
    new_second = BETA_TWO * square + (1.0 - BETA_TWO) * gradient * gradient
    direction = (
        new_first
        / (1.0 - BETA_ONE**STEP)
        / (jnp.sqrt(new_second / (1.0 - BETA_TWO**STEP)) + EPS_ADAM)
        + DECAY * master
    )
    return new_first, new_second, direction


def flat(block):
    pieces, both, rows, columns = block.shape
    if rows % 16:
        block = block.astype(F32)
    return block.reshape(pieces * both * rows, columns).astype(BF16)


def cut(matrix, pieces):
    rows, columns = matrix.shape
    return matrix.reshape(pieces, 2, rows // (2 * pieces), columns).astype(BF16)


NAMES = (
    "w_qkv", "w_out", "w_up", "w_down", "norm_parts", "norm_full", "ext", "cot_own", "h1", "h1_t",
    "k_all", "v_all", "prob", "attended", "resid", "h2", "h2_t", "cot_t", "mlp", "dh2", "wide",
    "act", "dup", "low_out", "delta",
    "halo_in", "g_down", "g_up", "g_out", "c_down", "c_up", "c_out",
    "c_qkv", "e_down", "e_up", "e_out", "x_down", "y_down", "sl_sem", "x_out", "e_qkv", "x_qkv", "k_t", "v_t", "from_cross", "scores", "inverse", "stack_q", "s_down",
    "s_up", "s_out", "s_qkv", "norm_sum", "norm_c", "norm_x", "norm_s", "sq_s", "near_rows", "loc_sem",
    "halo_sem", "normp_sem", "gz_send", "gz_recv", "gf_sem", "gs_sem", "gc_sem", "sc_sem", "se_sem", "sx_sem",
    "sz_send", "sz_recv", "bs_sem", "bx_sem", "small_sem", "norm_s_sem", "sq_s_sem", "out_sem", "back_sem",
)


def layer_kernel(seq_count, head_count, *refs):
    tok, cot, frames = refs[0:3]
    qkv_w, out_w, up_w, down_w, norm_w = refs[3:8]
    moment_refs = refs[8:18]
    block_out, input_grad, qkv_g, out_g, up_g, down_g, norm_g, squares = refs[18:26]
    scratch = dict(zip(NAMES, refs[26:-10], strict=True))
    moments = refs[-10:]
    qkv_m, qkv_u, out_m, out_u, up_m, up_u, down_m, down_u, norm_m, norm_u = moments
    (w_qkv, w_out, w_up, w_down, norm_parts, norm_full, ext, cot_own, h1, h1_t, k_all, v_all) = (
        scratch[name] for name in NAMES[0:12]
    )
    (prob, attended, resid, h2, h2_t, cot_t, mlp, dh2, wide, act, dup, low_out) = (
        scratch[name] for name in NAMES[12:24]
    )
    delta, halo_in, scores, inverse, stack_q = (
        scratch[name] for name in ("delta", "halo_in", "scores", "inverse", "stack_q")
    )
    norm_sum, norm_c, norm_x, norm_s, sq_s, near_rows = (
        scratch[name] for name in ("norm_sum", "norm_c", "norm_x", "norm_s", "sq_s", "near_rows")
    )
    (loc_sem, halo_sem, normp_sem, gz_send, gz_recv, gf_sem, gs_sem, gc_sem, sc_sem, se_sem, sx_sem) = (
        scratch[name] for name in NAMES[-20:-9]
    )
    sz_send, sz_recv, k_t, v_t, from_cross, bs_sem, bx_sem, sl_sem = (
        scratch[name]
        for name in ("sz_send", "sz_recv", "k_t", "v_t", "from_cross", "bs_sem", "bx_sem", "sl_sem")
    )
    small_sem, norm_s_sem, sq_s_sem, out_sem, back_sem = (scratch[name] for name in NAMES[-5:])

    dk_all, dv_all, dq_all, dh1, d_scores, dr_low = k_all, v_all, attended, mlp, act, h2
    S, H = seq_count, head_count
    N = S // 2
    T = cot_own.shape[0]
    R = qkv_w.shape[1]
    hidden = up_w.shape[1]
    s = lax.axis_index("seq")
    h = lax.axis_index("head")
    hx = lax.div(h, 2)
    hc = lax.rem(h, 2)
    ring = lax.div(s, 2)
    side = lax.rem(s, 2)
    other_core = (s, h + 1 - 2 * hc)
    other_x = (s, lax.rem(h + 2, H))
    other_side = (s + 1 - 2 * side, h)
    mine = hc * 2 + hx
    near = hc * 2 + 1 - hx
    mine_pair = hc * 2
    other_pair = (1 - hc) * 2
    total = S * H
    place = s * H + mine

    def device_at(number):
        number = lax.rem(number + total, total)
        block = lax.rem(number, H)
        return (lax.div(number, H), lax.rem(block, 2) * 2 + lax.div(block, 2))

    def seq_peer(i):
        return lax.rem(s + i, S)

    def remote(src, dst, send, recv, device):
        return pltpu.make_async_remote_copy(
            src_ref=src, dst_ref=dst, send_sem=send, recv_sem=recv, device_id=device, device_id_type=MESH
        )

    def rows_of(index, count):
        return pl.ds(pl.multiple_of(index * count, count), count)

    def each(low, high, step):
        def one(i, carry):
            step(i)
            return carry

        lax.fori_loop(low, high, one, 0)

    cot_copy = pltpu.make_async_copy(cot.at[rows_of(mine, T)], cot_own, loc_sem.at[3])
    cot_copy.start()

    def ext_copy(chunk):
        return pltpu.make_async_copy(
            tok.at[rows_of(jnp.maximum(mine - 2 + chunk, 0), T)],
            ext.at[pl.ds(chunk * T, T)],
            loc_sem.at[chunk],
        )

    for chunk in (2, 1, 0):

        @pl.when(mine - 2 + chunk >= 0)
        def _():
            ext_copy(chunk).start()

    moment_copies = [
        pltpu.make_async_copy(source, target, loc_sem.at[4 + k])
        for k, (source, target) in enumerate(zip(moment_refs, moments))
    ]
    for copy in moment_copies:
        copy.start()

    for t in range(3):
        w_qkv[mine, ring, side, :, t * 128 : (t + 1) * 128] = qkv_w[t].astype(BF16)
    norm_parts[s] = jnp.zeros(norm_parts.shape[1:], F32)
    norm_parts[s, 0:4, 0:R] = norm_w[...].astype(BF16).astype(F32)

    barrier = pltpu.get_barrier_semaphore()

    def greet(device):
        pl.semaphore_signal(barrier, inc=1, device_id=device, device_id_type=MESH)

    each(1, total, lambda i: greet(device_at(place + i)))
    pl.semaphore_wait(barrier, total - 1)

    spans = {
        QKV: w_qkv,
        OUT: w_out,
        UP: w_up,
        DOWN: w_down,
    }
    side_first = {QKV: True, OUT: False, UP: True, DOWN: False}
    all_ring, both_sides = pl.ds(0, N), pl.ds(0, 2)

    def piece(kind, group, a, b):
        return spans[kind].at[group, a, b]

    def ring_peer(i):
        there = lax.rem(ring + i, N)
        return there, (there * 2 + side, h)

    def gather_ring(kind, i):
        own = piece(kind, mine, ring, side)
        return remote(own, own, gz_send.at[kind, i], gz_recv.at[kind, ring], ring_peer(i)[1])

    def gather_ring_start(kind):
        each(1, N, lambda i: gather_ring(kind, i).start())

    def gather_ring_wait(kind):
        def one(i):
            there, device = ring_peer(i)
            block = piece(kind, mine, there, side)
            remote(block, block, gz_send.at[kind, i], gz_recv.at[kind, there], device).wait_recv()

        each(1, N, one)

    def gather_first(kind, sent):
        if side_first[kind]:
            block, device = piece(kind, mine, all_ring, side if sent else 1 - side), other_side
        else:
            block, device = piece(kind, mine if sent else near, all_ring, side), other_x
        return remote(block, block, gf_sem.at[0, kind], gf_sem.at[1, kind], device)

    def gather_second(kind, sent, late):
        if side_first[kind]:
            block = piece(kind, mine if sent else near, all_ring, 1 - side if late else side)
            device = other_x
        else:
            block = piece(kind, near if late else mine, all_ring, side if sent else 1 - side)
            device = other_side
        part = int(late)
        return remote(block, block, gs_sem.at[0, kind, part], gs_sem.at[1, kind, part], device)

    def gather_core(kind, pair):
        block = piece(kind, pl.ds(pair, 2), all_ring, both_sides)
        return remote(block, block, gc_sem.at[0, kind], gc_sem.at[1, kind], other_core)

    def gather_a(kind):
        gather_ring_wait(kind)
        gather_first(kind, True).start()
        gather_second(kind, True, False).start()

    def gather_b(kind):
        gather_first(kind, False).wait_recv()
        gather_second(kind, True, True).start()

    def gather_c(kind):
        gather_second(kind, False, False).wait_recv()
        gather_second(kind, False, True).wait_recv()
        gather_core(kind, mine_pair).start()

    def gather_d(kind):
        gather_core(kind, other_pair).wait_recv()

    diagonal = (other_side[0], other_x[1])

    def gather_sent(kind):
        gather_first(kind, True).wait_send()
        gather_second(kind, True, False).wait_send()
        gather_second(kind, True, True).wait_send()
        gather_core(kind, mine_pair).wait_send()
        each(1, N, lambda i: gather_ring(kind, i).wait_send())

    def norm_part(i):
        return remote(
            norm_parts.at[s], norm_parts.at[s], normp_sem.at[0, i], normp_sem.at[1, s], (seq_peer(i), h)
        )

    each(1, S, lambda i: norm_part(i).start())
    gather_ring_start(QKV)

    pieces = 4
    half = T // pieces

    def halo_copy(k):
        return remote(
            tok.at[rows_of(jnp.minimum(mine + 2, H - 1) * pieces + k, half)],
            ext.at[pl.ds(k * half, half)],
            halo_sem.at[0, k],
            halo_sem.at[1, k],
            (seq_peer(1), h),
        )

    def halo_pass(k):
        return remote(
            ext.at[pl.ds(k * half, half)],
            ext.at[pl.ds(T + k * half, half)],
            halo_sem.at[0, pieces + k],
            halo_sem.at[1, pieces + k],
            other_x,
        )

    sends_halo = (hc == 0) & (s < S - 1)
    takes_halo = (hc == 0) & (s > 0)

    @pl.when(sends_halo)
    def _():
        for k in range(pieces):
            halo_copy(k).start()

    @pl.when((hc == 0) & (s == 0))
    def _():
        ext[0:T, :] = jnp.zeros((T, ext.shape[1]), BF16)

    @pl.when((mine == 0) & (s == 0))
    def _():
        ext[T : 2 * T, :] = jnp.zeros((T, ext.shape[1]), BF16)

    w_out[mine, ring, side] = out_w[...].astype(BF16)
    w_up[mine, ring, side] = up_w[...].astype(BF16)
    w_down[mine, ring, side] = down_w[...].astype(BF16)

    first_frame = place * (T // FRAME_TOKENS)
    own_frames = T // FRAME_TOKENS

    def clip_step(c, carry):
        end, lows = carry
        start = end
        end = start + frames[c]
        lows = tuple(
            jnp.where((start <= first_frame + f) & (first_frame + f < end), start, lows[f])
            for f in range(own_frames)
        )
        return end, lows

    _, clip_low = lax.fori_loop(
        0, frames.shape[0], clip_step, (jnp.int32(0), tuple(jnp.int32(0) for _ in range(own_frames)))
    )

    gather_a(QKV)
    def norm_part_wait(i, carry):
        peer = seq_peer(i)
        part = norm_parts.at[peer]
        remote(part, part, normp_sem.at[0, i], normp_sem.at[1, peer], (peer, h)).wait_recv()
        return carry

    lax.fori_loop(1, S, norm_part_wait, 0)
    width = norm_full.shape[1]

    def norm_place(i, carry):
        part = norm_parts[i]
        wide = jnp.concatenate([part, jnp.zeros((8, width - 128), F32)], axis=1)
        return carry + pltpu.roll(wide, i * R, axis=1)

    norm_full[...] = lax.fori_loop(0, S, norm_place, jnp.zeros(norm_full.shape, F32))
    gain_one, shift_one = norm_full[0:1, :], norm_full[1:2, :]
    gain_two, shift_two = norm_full[2:3, :], norm_full[3:4, :]

    def first_norm(chunk):
        def one(b):
            at = pl.ds(pl.multiple_of(chunk * T + b * ROWS, ROWS), ROWS)
            normed, _ = normalize(ext[at, :].astype(F32))
            h1[at, :] = (normed * gain_one + shift_one).astype(BF16)

        each(0, T // ROWS, one)
        h1_t[:, chunk * T : (chunk + 1) * T] = h1[chunk * T : (chunk + 1) * T, :].T

    ext_copy(2).wait()
    first_norm(2)
    @pl.when((mine == 1) & takes_halo)
    def _():
        for k in range(pieces):
            halo_copy(k).wait_recv()
            halo_pass(k).start()

    gather_ring_start(OUT)
    gather_ring_start(UP)
    cot_copy.wait()
    cot_t[...] = cot_own[...].T
    gather_b(QKV)

    @pl.when(mine >= 1)
    def _():
        ext_copy(1).wait()

    @pl.when(mine >= 2)
    def _():
        ext_copy(0).wait()

    @pl.when((mine == 0) & takes_halo)
    def _():
        for k in range(pieces):
            halo_copy(k).wait_recv()

    first_norm(0)

    @pl.when((mine == 0) & takes_halo)
    def _():
        for k in range(pieces):
            halo_pass(k).wait_recv()

    first_norm(1)
    gather_ring_start(DOWN)

    lane = lax.broadcasted_iota(jnp.int32, (1, 128), 1)
    first_head = jnp.where(lane < HEAD_DIM, 1.0, 0.0).astype(BF16)
    second_head = jnp.where(lane < HEAD_DIM, 0.0, 1.0).astype(BF16)
    feature = lax.broadcasted_iota(jnp.int32, (128, TILE), 0)

    def two_heads(block):
        return jnp.concatenate([block * first_head, block * second_head], axis=0)

    def project(p):
        weight = flat(w_qkv[p])
        for chunk in range(3):
            at = pl.ds(chunk * T, T)
            if chunk == 2:
                out = nn(h1[at, :], weight)
                queries = out[:, 0:128].astype(BF16) * jnp.asarray(HEAD_DIM**-0.5, BF16)
                for i in range(T // TILE):
                    stack_q[p, i * 2 * TILE : (i + 1) * 2 * TILE, :] = two_heads(queries[i * TILE : (i + 1) * TILE])
                out = out[:, 128:384]
            else:
                out = nn(h1[at, :], flat(w_qkv[p, :, :, :, 128:384]))
            k_all[p, at, :] = out[:, 0:128].astype(BF16)
            v_all[p, at, :] = out[:, 128:256].astype(BF16)
            k_t[p, :, at] = k_all[p, at, :].T
            v_t[p, :, at] = v_all[p, at, :].T

    def own_halves(block):
        return jnp.where(feature < HEAD_DIM, block[:, 0:TILE], block[:, TILE : 2 * TILE])

    key_frames = KEYS // FRAME_TOKENS

    def bias_of(i):
        query_lane = lax.broadcasted_iota(jnp.int32, (key_frames, 1, 2 * TILE), 2)
        later = lax.rem(query_lane, TILE) >= FRAME_TOKENS
        low = jnp.where(later, clip_low[2 * i + 1], clip_low[2 * i])
        high = first_frame + 2 * i + later.astype(jnp.int32)
        key_frame = (
            first_frame
            - MOST_FRAMES
            + 2 * i
            + lax.broadcasted_iota(jnp.int32, (key_frames, 1, 2 * TILE), 0)
        )
        return jnp.where((key_frame >= low) & (key_frame <= high), 0.0, MASKED).astype(F32)

    biases = [bias_of(i) for i in range(T // TILE)]

    def attend(p, between):
        for i in range(T // TILE):
            for step in between.get(i, ()):
                step()
            own = pl.ds(i * TILE, TILE)
            window = pl.ds(i * TILE, KEYS)
            raw = scores.at[pl.ds(i % 2 * KEYS, KEYS)]
            raw[...] = nt(k_all[p, window, :], stack_q[p, i * 2 * TILE : (i + 1) * 2 * TILE, :])
            highest = jnp.full((8, 2 * TILE), MASKED, F32)
            for c in range(KEYS // TILE):
                block = raw[c * TILE : (c + 1) * TILE, :].reshape(2, FRAME_TOKENS, 2 * TILE)
                block = (block + biases[i][2 * c : 2 * c + 2]).reshape(TILE // 8, 8, 2 * TILE)
                highest = jnp.maximum(highest, jnp.max(block, axis=0))
            shift = biases[i] - jnp.max(highest, axis=0, keepdims=True)
            sums = jnp.zeros((8, 2 * TILE), F32)
            for c in range(KEYS // TILE):
                block = raw[c * TILE : (c + 1) * TILE, :].reshape(2, FRAME_TOKENS, 2 * TILE)
                block = jnp.exp(block + shift[2 * c : 2 * c + 2]).reshape(TILE // 8, 8, 2 * TILE)
                sums = sums + jnp.sum(block, axis=0)
                prob[p, (i + c) * TILE : (i + c + 1) * TILE, i * 2 * TILE : (i + 1) * 2 * TILE] = block.reshape(
                    TILE, 2 * TILE
                ).astype(BF16)
            scale = 1.0 / jnp.sum(sums, axis=0, keepdims=True)
            inverse[p, i] = scale
            low = prob[p, window, i * 2 * TILE : (i + 1) * 2 * TILE]
            mixed = own_halves(nn(v_t[p, :, window], low) * scale)
            attended[p, own, :] = mixed.T.astype(BF16)

    def clear(p):
        for i in range(T // TILE):
            columns = slice(i * 2 * TILE, (i + 1) * 2 * TILE)
            if i:
                prob[p, 0 : i * TILE, columns] = jnp.zeros((i * TILE, 2 * TILE), BF16)
            below = i * TILE + KEYS
            if below < 3 * T:
                prob[p, below : 3 * T, columns] = jnp.zeros((3 * T - below, 2 * TILE), BF16)

    each(0, H, clear)

    do = functools.partial
    project(mine)
    attend(mine, {3: [do(gather_a, OUT)]})
    gather_c(QKV)
    gather_a(UP)
    project(near)
    attend(near, {0: [do(gather_a, DOWN)], 2: [do(gather_b, OUT)]})
    gather_d(QKV)
    project(other_pair)
    attend(other_pair, {0: [do(gather_b, UP)], 1: [do(gather_b, DOWN)], 2: [do(gather_c, OUT)]})
    project(other_pair + 1)
    attend(other_pair + 1, {1: [do(gather_d, OUT)], 3: [do(gather_c, UP)]})
    gather_c(DOWN)

    acc = nt(attended[0], flat(w_out[0]))
    for p in range(1, H):
        acc = acc + nt(attended[p], flat(w_out[p]))
    resid[...] = acc

    def second_norm(b):
        at = rows_of(b, ROWS)
        whole = ext[pl.ds(pl.multiple_of(2 * T + b * ROWS, ROWS), ROWS), :].astype(F32) + resid[at, :]
        resid[at, :] = whole
        normed, _ = normalize(whole)
        h2[at, :] = (normed * gain_two + shift_two).astype(BF16)

    each(0, T // ROWS, second_norm)
    h2_t[...] = h2[...].T
    gather_d(UP)
    gather_d(DOWN)

    endings = ("down", "up", "out", "qkv")
    grads, from_core, from_side, from_x, from_ring = (
        [scratch.get(start + name) for name in endings] for start in ("g_", "c_", "e_", "x_", "s_")
    )
    grads[QKV] = w_up.at[:, :, :, :, pl.ds(0, w_qkv.shape[-1])]

    def in_order(k):
        return (other_pair, other_pair + 1, near, mine)[k]

    def scatter_core(kind, group, slot):
        return remote(
            grads[kind].at[group],
            from_core[kind].at[slot],
            sc_sem.at[0, kind, slot],
            sc_sem.at[1, kind, slot],
            other_core,
        )

    def scatter_side(kind, group):
        slot = group - mine_pair
        return remote(
            grads[kind].at[group, all_ring, 1 - side],
            from_side[kind].at[slot],
            se_sem.at[0, kind, slot],
            se_sem.at[1, kind, slot],
            other_side,
        )

    def cross_x():
        return remote(grads[UP].at[near], from_cross, sx_sem.at[0, UP], sx_sem.at[1, UP], other_x)

    def cross_side():
        return remote(
            grads[UP].at[mine, all_ring, 1 - side],
            from_side[UP].at[0],
            se_sem.at[0, UP, 0],
            se_sem.at[1, UP, 0],
            other_side,
        )

    def cross_a():
        cross_x().wait_recv()

        def add(there, b):
            grads[UP][mine, there, b] = (
                grads[UP][mine, there, b].astype(F32) + from_cross[there, b].astype(F32)
            ).astype(BF16)

        each(0, N, lambda there: add(there, 1 - side))
        cross_side().start()
        each(0, N, lambda there: add(there, side))

    def cross_b():
        cross_side().wait_recv()

        def add(there):
            grads[UP][mine, there, side] = (
                grads[UP][mine, there, side].astype(F32) + from_side[UP][0, there].astype(F32)
            ).astype(BF16)

        each(0, N, add)
        each(1, N, lambda i: scatter_ring(UP, i).start())

    from_ring_late, for_x, for_x_in = scratch["s_down"], scratch["y_down"], scratch["x_down"]

    def late_ring(kind, group, i):
        slot = group - mine_pair
        there, device = ring_peer(i)
        return remote(
            grads[kind].at[group, there, side],
            from_ring_late.at[slot, ring],
            sl_sem.at[0, slot, i],
            sl_sem.at[1, slot, ring],
            device,
        )

    def late_a(kind):
        for group in (near, mine):
            scatter_side_sum(kind, group)
            each(1, N, lambda i: late_ring(kind, group, i).start())

    def late_sum(kind, group):
        slot = group - mine_pair

        def one(i, carry):
            there, device = ring_peer(i)
            landed = from_ring_late.at[slot, there]
            remote(
                grads[kind].at[group, there, side],
                landed,
                sl_sem.at[0, slot, i],
                sl_sem.at[1, slot, there],
                device,
            ).wait_recv()
            return carry + landed[...].astype(F32)

        return lax.fori_loop(1, N, one, grads[kind][group, ring, side].astype(F32))

    def late_x(kind):
        return remote(for_x, for_x_in, sx_sem.at[0, kind], sx_sem.at[1, kind], other_x)

    def late_b(kind):
        for_x[...] = late_sum(kind, near).astype(BF16)
        late_x(kind).start()

    def late_c(kind):
        total = late_sum(kind, mine)
        late_x(kind).wait_recv()
        return total + for_x_in[...].astype(F32)

    def side_block(group, b):
        slot = group - mine_pair
        return remote(
            grads[QKV].at[group, b, 1 - side],
            from_side[QKV].at[slot, b],
            bs_sem.at[0, slot, b],
            bs_sem.at[1, slot, b],
            other_side,
        )

    def x_block(b):
        return remote(
            grads[QKV].at[near, b, side], from_x[QKV].at[b], bx_sem.at[0, b], bx_sem.at[1, b], other_x
        )

    def block_of(i):
        return lax.rem(ring + i, N)

    def blocks_a():
        def one(i):
            b = block_of(i)
            side_block(near, b).wait_recv()
            grads[QKV][near, b, side] = (
                grads[QKV][near, b, side].astype(F32) + from_side[QKV][near - mine_pair, b].astype(F32)
            ).astype(BF16)
            x_block(b).start()

        each(1, N + 1, one)

    def blocks_b():
        def one(i):
            b = block_of(i)
            side_block(mine, b).wait_recv()
            x_block(b).wait_recv()
            grads[QKV][mine, b, side] = (
                grads[QKV][mine, b, side].astype(F32)
                + from_side[QKV][mine - mine_pair, b].astype(F32)
                + from_x[QKV][b].astype(F32)
            ).astype(BF16)

            @pl.when(i < N)
            def _():
                scatter_ring(QKV, i).start()

        each(1, N + 1, one)

    def place_grad(kind, k, matrix):
        group = in_order(k)
        if k < 2:
            grads[kind][group] = cut(matrix, N)
            scatter_core(kind, group, k).start()
        else:
            slot = group - mine_pair
            scatter_core(kind, group, slot).wait_recv()
            grads[kind][group] = cut(matrix + flat(from_core[kind][slot]).astype(F32), N)
            if kind == QKV:
                each(1, N + 1, lambda i: side_block(group, block_of(i)).start())
            elif kind != UP:
                scatter_side(kind, group).start()
            elif k == 2:
                cross_x().start()

    def scatter_side_sum(kind, group):
        scatter_side(kind, group).wait_recv()
        slot = group - mine_pair

        def add(b):
            grads[kind][group, b, side] = (
                grads[kind][group, b, side].astype(F32) + from_side[kind][slot, b].astype(F32)
            ).astype(BF16)

        each(0, N, add)

    def scatter_x(kind):
        return remote(
            grads[kind].at[near, all_ring, side],
            from_x[kind],
            sx_sem.at[0, kind],
            sx_sem.at[1, kind],
            other_x,
        )

    def scatter_ring(kind, i):
        there, device = ring_peer(i)
        return remote(
            grads[kind].at[mine, there, side],
            from_ring[kind].at[ring],
            sz_send.at[kind, i],
            sz_recv.at[kind, ring],
            device,
        )

    def scatter_a(kind):
        scatter_side_sum(kind, near)
        scatter_x(kind).start()

    def scatter_b(kind):
        scatter_side_sum(kind, mine)
        scatter_x(kind).wait_recv()

        def add(b):
            grads[kind][mine, b, side] = (
                grads[kind][mine, b, side].astype(F32) + from_x[kind][b].astype(F32)
            ).astype(BF16)

        each(0, N, add)
        each(1, N, lambda i: scatter_ring(kind, i).start())

    def scatter_c(kind):
        landed = from_ring[kind]

        def one(i, carry):
            there, device = ring_peer(i)
            remote(
                grads[kind].at[mine, there, side],
                landed.at[there],
                sz_send.at[kind, i],
                sz_recv.at[kind, there],
                device,
            ).wait_recv()
            return carry + landed[there].astype(F32)

        return lax.fori_loop(1, N, one, grads[kind][mine, ring, side].astype(F32))

    mlp[...] = jnp.zeros_like(mlp)
    dh2[...] = jnp.zeros_like(dh2)
    half_hidden = hidden // 2

    def part_of(k, which, column, low_row, high_row):
        buffer = wide if k % 2 == 0 else scores
        start = (2 * which + column) * T
        return buffer.at[pl.ds(start + low_row, high_row - low_row), :]

    def inner(k):
        for column in range(2):
            columns = slice(column * half_hidden, (column + 1) * half_hidden)
            part_of(k, 0, column, 0, T)[...] = nn(h2[...], flat(w_up[in_order(k), :, :, :, columns]))
            part_of(k, 1, column, 0, T)[...] = nn(cot_own[...], flat(w_down[in_order(k), :, :, :, columns]))

    def slot(k):
        return pl.ds(k % 2 * hidden, hidden)

    def pointwise(k):
        for b in range(T // 128):
            for column in range(2):
                low_row, high_row = b * 128, (b + 1) * 128
                value, slope = gelu_both(part_of(k, 0, column, low_row, high_row)[...])
                at = pl.ds(k % 2 * hidden + column * half_hidden, half_hidden)
                act[low_row:high_row, at] = value.astype(BF16)
                dup[low_row:high_row, at] = (part_of(k, 1, column, low_row, high_row)[...] * slope).astype(BF16)

    def outer(k):
        mlp[...] += nt(act[:, slot(k)], flat(w_down[in_order(k)]))
        dh2[...] += nt(dup[:, slot(k)], flat(w_up[in_order(k)]))
        place_grad(DOWN, k, nn(cot_t[...], act[:, slot(k)]))
        place_grad(UP, k, nn(h2_t[...], dup[:, slot(k)]))

    inner(0)
    for k in range(H):
        if k + 1 < H:
            inner(k + 1)
        pointwise(k)
        outer(k)

    def finish_rows(target, low, at_sem):
        def slab(block):
            return target.at[rows_of(block, T)]

        keep = pltpu.make_async_copy(low, slab(mine), out_sem.at[at_sem, 0])
        landed = near_rows.at[at_sem]
        to_x = remote(low, landed, out_sem.at[at_sem, 1], out_sem.at[at_sem, 2], other_x)
        to_core = remote(low, slab(mine), out_sem.at[at_sem, 3], out_sem.at[at_sem, 4], other_core)
        passed = remote(landed, slab(near), out_sem.at[at_sem, 5], out_sem.at[at_sem, 6], other_core)
        store = pltpu.make_async_copy(landed, slab(near), out_sem.at[at_sem, 7])
        return keep, to_x, to_core, passed, store

    def sum_out(b):
        at = rows_of(b, ROWS)
        low_out[at, :] = (resid[at, :] + mlp[at, :]).astype(BF16)

    each(0, T // ROWS, sum_out)
    out_copies = finish_rows(block_out, low_out, 0)

    def second_back(b, carry):
        gain_sum, shift_sum = carry
        at = rows_of(b, ROWS)
        normed, inverse = normalize(resid[at, :])
        grad = dh2[at, :]
        mixed = cot_own[at, :].astype(F32) + norm_back(grad, normed, inverse, gain_two)
        resid[at, :] = mixed
        dr_low[at, :] = mixed.astype(BF16)
        gain_sum = gain_sum + jnp.sum(grad * normed, axis=0, keepdims=True)
        shift_sum = shift_sum + jnp.sum(grad, axis=0, keepdims=True)
        return gain_sum, shift_sum

    zero_row = jnp.zeros((1, width), F32)
    gain_two_grad, shift_two_grad = lax.fori_loop(0, T // ROWS, second_back, (zero_row, zero_row))

    def stack_d(p):
        return h1.at[pl.ds(0, 2 * T), pl.ds(pl.multiple_of(p * 128, 128), 128)]

    lane_first = lax.broadcasted_iota(jnp.int32, (TILE, 128), 1) < HEAD_DIM

    def deltas(p, d_att):
        for i in range(T // TILE):
            own = pl.ds(i * TILE, TILE)
            row = inverse[p, i]
            turned = jnp.concatenate([row[:, 0:TILE], row[:, TILE : 2 * TILE], jnp.zeros((6, TILE), F32)], axis=0).T
            scaled = d_att[i * TILE : (i + 1) * TILE].astype(F32) * jnp.where(lane_first, turned[:, 0:1], turned[:, 1:2])
            low = scaled.astype(BF16)
            stack_d(p)[i * 2 * TILE : (i + 1) * 2 * TILE, :] = two_heads(low)
            products = (low.astype(F32) * attended[p, own, :].astype(F32)).T
            delta[p, :, i * 2 * TILE : (i + 1) * 2 * TILE] = jnp.concatenate(
                [
                    jnp.sum(products[0:HEAD_DIM], axis=0, keepdims=True),
                    jnp.sum(products[HEAD_DIM:128], axis=0, keepdims=True),
                ],
                axis=1,
            )

    h2_t[...] = dr_low[...].T
    for k in range(H):
        p = in_order(k)
        deltas(p, nn(dr_low[...], flat(w_out[p])).astype(BF16))
        place_grad(OUT, k, nn(h2_t[...], attended[p]))

    gather_sent(UP)
    late_a(DOWN)
    cross_a()
    for copy in out_copies[:3]:
        copy.start()

    def dq_acc(p, i):
        return wide.at[pl.ds(pl.multiple_of((p * (T // TILE) + i) * TILE, TILE), TILE), pl.ds(0, TILE)]

    def attend_back(chunk, p):
        at = pl.ds(chunk * T, T)
        grads_p = stack_d(p)[...]
        for i in range(T // TILE):
            d_prob = scores.at[pl.ds(i * T, T)]
            d_prob[...] = nt(v_all[p, at, :], grads_p[i * 2 * TILE : (i + 1) * 2 * TILE])
        for r in range(T // TILE):
            rows = slice(r * TILE, (r + 1) * TILE)
            for i in range(T // TILE):
                columns = slice(i * 2 * TILE, (i + 1) * 2 * TILE)
                if (chunk == 0 and i > r) or (chunk == 2 and i < r):
                    d_scores[rows, columns] = jnp.zeros((TILE, 2 * TILE), BF16)
                else:
                    low = prob[p, chunk * T + r * TILE : chunk * T + (r + 1) * TILE, columns].astype(F32)
                    d_scores[rows, columns] = (low * (scores[i * T + r * TILE : i * T + (r + 1) * TILE, :] - delta[p, :, columns])).astype(BF16)
        dv_all[p, at, :] = nn(prob[p, at, :], grads_p).astype(BF16)
        dk_all[p, at, :] = nn(d_scores[...], stack_q[p]).astype(BF16)
        dq_part = nn(k_t[p, :, at], d_scores[...])
        for i in range(T // TILE):
            own = pl.ds(i * TILE, TILE)
            part = own_halves(dq_part[:, i * 2 * TILE : (i + 1) * 2 * TILE])
            if chunk == 0:
                dq_acc(p, i)[...] = part
            elif chunk == 1:
                dq_acc(p, i)[...] += part
            else:
                dq_all[p, own, :] = ((dq_acc(p, i)[...] + part) * (HEAD_DIM**-0.5)).T.astype(BF16)

    def back_copy(chunk):
        return remote(
            dup.at[:, pl.ds(chunk * width, width)],
            halo_in.at[chunk],
            back_sem.at[0, chunk],
            back_sem.at[1, chunk],
            device_at(place - 2 + chunk),
        )

    def sends_back(chunk):
        return place >= 2 - chunk

    def takes_back(chunk):
        return place < total - (2 - chunk)

    for chunk in range(2):

        @pl.when(jnp.logical_not(takes_back(chunk)))
        def _():
            halo_in[chunk] = jnp.zeros(halo_in.shape[1:], BF16)

    def first_sums(chunk, carry):
        def one(b, inner):
            gain_sum, shift_sum = inner
            at = pl.ds(pl.multiple_of(chunk * T + b * ROWS, ROWS), ROWS)
            normed, _ = normalize(ext[at, :].astype(F32))
            grad = dh1[rows_of(b, ROWS), :]
            if chunk < 2:
                dup[rows_of(b, ROWS), chunk * width : (chunk + 1) * width] = grad.astype(BF16)
            return (
                gain_sum + jnp.sum(grad * normed, axis=0, keepdims=True),
                shift_sum + jnp.sum(grad, axis=0, keepdims=True),
            )

        return lax.fori_loop(0, T // ROWS, one, carry)

    def halo_back(p, chunk):
        at = pl.ds(chunk * T, T)
        both = jnp.concatenate([dk_all[p, at, :], dv_all[p, at, :]], axis=1)
        return nt(both, flat(w_qkv[p, :, :, :, 128:384]))

    sums = (zero_row, zero_row)
    for chunk in range(2):
        dh1[...] = jnp.zeros_like(dh1)

        def one(p, chunk=chunk):
            attend_back(chunk, p)
            dh1[...] += halo_back(p, chunk)

        each(0, 2, one)
        if chunk == 1:
            scatter_a(OUT)
        each(2, 4, one)
        sums = first_sums(chunk, sums)

        @pl.when(sends_back(chunk))
        def _():
            back_copy(chunk).start()

        if chunk == 0:
            cross_b()

    dh1[...] = jnp.zeros_like(dh1)
    for k in range(H):
        p = in_order(k)
        each(p, p + 1, lambda q: attend_back(2, q))
        weight = flat(w_qkv[p])
        at = pl.ds(2 * T, T)
        three = jnp.concatenate([dq_all[p], dk_all[p, at, :], dv_all[p, at, :]], axis=1)
        dh1[...] += nt(three, weight)
        both = jnp.concatenate([dk_all[p], dv_all[p]], axis=1)
        columns = [nn(h1_t[:, 2 * T : 3 * T], dq_all[p]), nn(h1_t[...], both)]
        place_grad(QKV, k, jnp.concatenate(columns, axis=1))
        if k == 1:
            out_copies[1].wait_recv()
            out_copies[3].start()
            out_copies[4].start()
        if k == 2:
            scatter_b(OUT)
            late_b(DOWN)

    gain_one_grad, shift_one_grad = first_sums(2, sums)
    norm_sum[...] = jnp.concatenate(
        [gain_one_grad, shift_one_grad, gain_two_grad, shift_two_grad, jnp.zeros((4, width), F32)], axis=0
    )
    norm_to_core = remote(norm_sum, norm_c, small_sem.at[0], small_sem.at[1], other_core)
    norm_to_core.start()
    blocks_a()
    norm_to_core.wait()
    norm_sum[...] += norm_c[...]
    plane = (other_x, other_side, diagonal)
    norm_plane = [
        remote(norm_sum, norm_x.at[k], small_sem.at[2 + k], small_sem.at[5 + k], device)
        for k, device in enumerate(plane)
    ]
    for copy in norm_plane:
        copy.start()

    for chunk in range(2):

        @pl.when(takes_back(chunk))
        def _():
            back_copy(chunk).wait_recv()

    def first_back(b):
        at = rows_of(b, ROWS)
        normed, inverse = normalize(ext[pl.ds(pl.multiple_of(2 * T + b * ROWS, ROWS), ROWS), :].astype(F32))
        grad = dh1[at, :] + halo_in[0, at, :].astype(F32) + halo_in[1, at, :].astype(F32)
        dr_low[at, :] = (resid[at, :] + norm_back(grad, normed, inverse, gain_one)).astype(BF16)

    each(0, T // ROWS, first_back)
    grad_copies = finish_rows(input_grad, dr_low, 1)
    for copy in grad_copies[:3]:
        copy.start()
    for copy in norm_plane:
        copy.wait()
    norm_sum[...] += norm_x[0] + (norm_x[1] + norm_x[2])

    def norm_ring(i):
        return remote(
            norm_sum, norm_s.at[ring], norm_s_sem.at[0, i], norm_s_sem.at[1, ring], ring_peer(i)[1]
        )

    each(1, N, lambda i: norm_ring(i).start())
    blocks_b()

    for copy in moment_copies:
        copy.wait()
    down_total = late_c(DOWN)
    down_g[...] = down_total
    up_total = scatter_c(UP)
    up_g[...] = up_total
    out_total = scatter_c(OUT)
    out_g[...] = out_total

    def sums_of(master, moment, square, gradient):
        _, _, direction = lamb_direction(master, moment, square, gradient)
        return jnp.sum(master * master), jnp.sum(direction * direction)

    down_sums = sums_of(down_w[...], down_m[...], down_u[...], down_total)
    up_sums = sums_of(up_w[...], up_m[...], up_u[...], up_total)
    out_sums = sums_of(out_w[...], out_m[...], out_u[...], out_total)

    def norm_ring_wait(i, carry):
        there, device = ring_peer(i)
        remote(
            norm_sum, norm_s.at[there], norm_s_sem.at[0, i], norm_s_sem.at[1, there], device
        ).wait_recv()
        return carry + norm_s[there]

    norm_total = lax.fori_loop(1, N, norm_ring_wait, norm_sum[...])
    norm_mine = pltpu.roll(norm_total, lax.rem(width - s * R, width), axis=1)[0:4, 0:R]
    norm_g[...] = norm_mine
    once = jnp.where(h == 0, 1.0, 0.0).astype(F32)
    norm_sums = sums_of(norm_w[...], norm_m[...], norm_u[...], norm_mine)
    norm_sums = (norm_sums[0] * once, norm_sums[1] * once)

    qkv_total = scatter_c(QKV)
    weight_sum, update_sum = jnp.float32(0.0), jnp.float32(0.0)
    for t in range(3):
        part = qkv_total[:, t * 128 : (t + 1) * 128]
        qkv_g[t] = part
        pair = sums_of(qkv_w[t], qkv_m[t], qkv_u[t], part)
        weight_sum, update_sum = weight_sum + pair[0], update_sum + pair[1]
    qkv_sums = (weight_sum, update_sum)

    row = lax.broadcasted_iota(jnp.int32, (8, 128), 0)
    column = lax.broadcasted_iota(jnp.int32, (8, 128), 1)
    both = jnp.zeros((8, 128), F32)
    for number, pair in enumerate((qkv_sums, out_sums, up_sums, down_sums, norm_sums)):
        for which in range(2):
            both = jnp.where((row == which) & (column == number), pair[which], both)
    squares[...] = both

    def sq_copy(i):
        peer = lax.rem(place + i, total)
        return remote(squares, sq_s.at[place], sq_s_sem.at[0, i], sq_s_sem.at[1, place], device_at(peer))

    def sq_wait(i, carry):
        peer = lax.rem(place + i, total)
        remote(
            squares, sq_s.at[peer], sq_s_sem.at[0, i], sq_s_sem.at[1, peer], device_at(peer)
        ).wait_recv()
        return carry

    each(1, total, lambda i: sq_copy(i).start())
    grad_copies[1].wait_recv()
    grad_copies[3].start()
    grad_copies[4].start()
    lax.fori_loop(1, total, sq_wait, 0)
    sq_s[place] = both
    each(1, total, lambda i: sq_copy(i).wait_send())
    squares[...] = lax.fori_loop(0, total, lambda i, carry: carry + sq_s[i], jnp.zeros((8, 128), F32))

    for copies in (out_copies, grad_copies):
        keep, to_x, to_core, passed, store = copies
        keep.wait()
        store.wait()
        to_x.wait_send()
        to_core.wait_send()
        passed.wait_send()
        to_core.wait_recv()
        passed.wait_recv()

    for k in range(pieces):

        @pl.when(sends_halo)
        def _():
            halo_copy(k).wait_send()

        @pl.when((mine == 1) & takes_halo)
        def _():
            halo_pass(k).wait_send()

    for chunk in range(2):

        @pl.when(sends_back(chunk))
        def _():
            back_copy(chunk).wait_send()

    for kind in (QKV, OUT, DOWN):
        gather_sent(kind)
    for kind in (QKV, OUT, UP, DOWN):
        for k in range(2):
            scatter_core(kind, in_order(k), k).wait_send()
        if kind == UP:
            cross_x().wait_send()
            cross_side().wait_send()
        elif kind != QKV:
            scatter_side(kind, near).wait_send()
            scatter_side(kind, mine).wait_send()
            (late_x if kind == DOWN else scatter_x)(kind).wait_send()

    def drain(i):
        norm_part(i).wait_send()

    each(1, S, drain)

    def drain_blocks(b):
        side_block(near, b).wait_send()
        side_block(mine, b).wait_send()
        x_block(b).wait_send()

    each(0, N, drain_blocks)

    def drain_ring(i):
        norm_ring(i).wait_send()
        for kind in (QKV, OUT, UP):
            scatter_ring(kind, i).wait_send()
        late_ring(DOWN, near, i).wait_send()
        late_ring(DOWN, mine, i).wait_send()

    each(1, N, drain_ring)


def run_layer(mesh_sizes, tok, cot, frames, weights, moments, seconds):
    S, H = mesh_sizes
    rows_dev, width = tok.shape
    T = rows_dev // H
    R = weights[0].shape[1]
    N = S // 2
    assert H == 4 and S % 2 == 0 and 2 * T == MOST_FRAMES * FRAME_TOKENS and R * S == width
    hidden = weights[2].shape[1]
    assert hidden == T == 4 * TILE
    any_space = pl.BlockSpec(memory_space=pl.ANY)
    vmem = pl.BlockSpec(memory_space=pltpu.VMEM)
    smem = pl.BlockSpec(memory_space=pltpu.SMEM)
    dma = pltpu.SemaphoreType.DMA
    out_shape = (
        jax.ShapeDtypeStruct((rows_dev, width), BF16),
        jax.ShapeDtypeStruct((rows_dev, width), BF16),
        *[jax.ShapeDtypeStruct(w.shape, F32) for w in weights],
        jax.ShapeDtypeStruct((8, 128), F32),
    )
    cols = {"down": hidden, "up": hidden, "out": 128, "qkv": 384}
    kinds = ("down", "up", "out", "qkv")
    low, full = functools.partial(pltpu.VMEM, dtype=BF16), functools.partial(pltpu.VMEM, dtype=F32)
    scratch = dict(
        norm_parts=full((S, 8, 128)),
        norm_full=full((8, width)),
        ext=low((3 * T, width)),
        cot_own=low((T, width)),
        h1=low((3 * T, width)),
        h1_t=low((width, 3 * T)),
        k_all=low((H, 3 * T, 128)),
        v_all=low((H, 3 * T, 128)),
        prob=low((H, 3 * T, 2 * T)),
        scores=full((2 * KEYS, 2 * TILE)),
        inverse=full((H, T // TILE, 1, 2 * TILE)),
        stack_q=low((H, 2 * T, 128)),
        attended=low((H, T, 128)),
        resid=full((T, width)),
        h2=low((T, width)),
        h2_t=low((width, T)),
        cot_t=low((width, T)),
        mlp=full((T, width)),
        dh2=full((T, width)),
        wide=full((4 * T, 2 * TILE)),
        act=low((T, 2 * hidden)),
        dup=low((T, 2 * hidden)),
        low_out=low((T, width)),
        delta=full((H, 1, 2 * T)),
        halo_in=low((2, T, width)),
        norm_sum=full((8, width)),
        norm_c=full((8, width)),
        norm_x=full((3, 8, width)),
        norm_s=full((N, 8, width)),
        sq_s=full((S * H, 8, 128)),
        k_t=low((H, 128, 3 * T)),
        v_t=low((H, 128, 3 * T)),
        from_cross=low((N, 2, R, hidden)),
        loc_sem=dma((14,)),
        halo_sem=dma((2, 8)),
        normp_sem=dma((2, S)),
        gz_send=dma((4, N)),
        gz_recv=dma((4, N)),
        gf_sem=dma((2, 4)),
        gs_sem=dma((2, 4, 2)),
        gc_sem=dma((2, 4)),
        sc_sem=dma((2, 4, 2)),
        se_sem=dma((2, 4, 2)),
        sx_sem=dma((2, 4)),
        sl_sem=dma((2, 2, N)),
        bs_sem=dma((2, 2, N)),
        bx_sem=dma((2, N)),
        sz_send=dma((4, N)),
        sz_recv=dma((4, N)),
        small_sem=dma((14,)),
        norm_s_sem=dma((2, N)),
        sq_s_sem=dma((2, S * H)),
        out_sem=dma((2, 8)),
        near_rows=low((2, T, width)),
        back_sem=dma((2, 2)),
    )
    for kind in kinds:
        scratch["w_" + kind] = low((H, N, 2, R, cols[kind]))
        if kind != "qkv":
            scratch["g_" + kind] = low((H, N, 2, R, cols[kind]))
        scratch["c_" + kind] = low((2, N, 2, R, cols[kind]))
        scratch["e_" + kind] = low((2, N, R, cols[kind]))
        scratch["s_" + kind] = low((N, R, cols[kind]))
        if kind in ("out", "qkv"):
            scratch["x_" + kind] = low((N, R, cols[kind]))
    scratch["s_down"] = low((2, N, R, hidden))
    scratch["x_down"] = low((R, hidden))
    scratch["y_down"] = low((R, hidden))
    operands = [tok, cot, frames, *weights]
    for moment, second in zip(moments, seconds):
        operands += [moment, second]
    return pl.pallas_call(
        functools.partial(layer_kernel, S, H),
        out_shape=out_shape,
        in_specs=[any_space, any_space, smem] + [vmem] * 5 + [any_space] * 10,
        out_specs=(any_space, any_space) + (vmem,) * 6,
        scratch_shapes=[scratch[name] for name in NAMES]
        + [pltpu.VMEM(array.shape, F32) for array in operands[8:18]],
        compiler_params=pltpu.CompilerParams(
            collective_id=0, has_side_effects=True, vmem_limit_bytes=63 * 2**20
        ),
        name="layer",
    )(*operands)


CHUNKS = 4


def update_kernel(count, *refs):
    block_low, grad_low = refs[0:2]
    sources = refs[2:23]
    block_out, input_grad = refs[23:25]
    targets = refs[25 : 25 + count]
    rest = refs[25 + count :]
    loaded, made = rest[0:21], rest[21 : 21 + count]
    low, wide, block, sem, load_sem, store_sem = rest[21 + count :]
    rows = low.shape[1]
    block_load = pltpu.make_async_copy(block_low, block, sem.at[0, 0])
    block_store = pltpu.make_async_copy(block, block_out, sem.at[0, 1])
    loads = [
        pltpu.make_async_copy(grad_low.at[pl.ds(c * rows, rows)], low.at[c], sem.at[1, c]) for c in range(CHUNKS)
    ]
    stores = [
        pltpu.make_async_copy(wide.at[c], input_grad.at[pl.ds(c * rows, rows)], sem.at[2, c])
        for c in range(CHUNKS)
    ]
    small_loads = [
        pltpu.make_async_copy(source, target, load_sem.at[k])
        for k, (source, target) in enumerate(zip(sources, loaded))
    ]
    small_stores = [
        pltpu.make_async_copy(source, target, store_sem.at[k])
        for k, (source, target) in enumerate(zip(made, targets))
    ]
    for copy in loads:
        copy.start()
    for copy in small_loads:
        copy.start()
    block_load.start()
    for c in range(CHUNKS):
        loads[c].wait()
        wide[c] = low[c].astype(F32)
        stores[c].start()
    for copy in small_loads:
        copy.wait()
    grads, masters, firsts, seconds = loaded[0:5], loaded[5:10], loaded[10:15], loaded[15:20]
    roots = jnp.sqrt(loaded[20][...])
    for number in (3, 2, 0, 1, 4):
        outs_here = made[5 * number : 5 * number + 5]
        ratio = roots[0:1, number : number + 1] / roots[1:2, number : number + 1]
        pieces = range(grads[number].shape[0]) if len(grads[number].shape) == 3 else (slice(None),)
        for piece in pieces:
            gradient, master = grads[number][piece], masters[number][piece]
            first, second, direction = lamb_direction(
                master, firsts[number][piece], seconds[number][piece], gradient
            )
            new_master = master - RATE * ratio * direction
            outs_here[0][piece] = gradient
            outs_here[1][piece] = first
            outs_here[2][piece] = second
            outs_here[3][piece] = new_master
            outs_here[4][piece] = new_master.astype(BF16)
        for copy in small_stores[5 * number : 5 * number + 5]:
            copy.start()
    made[25][...] = roots[0:2, 0:5]
    small_stores[25].start()
    block_load.wait()
    block_store.start()
    for copy in (*stores, *small_stores, block_store):
        copy.wait()


def run_update(block_low, grad_low, grads, masters, firsts, seconds, squares):
    any_space = pl.BlockSpec(memory_space=pl.ANY)
    operands = [block_low, grad_low, *grads, *masters, *firsts, *seconds, squares]
    rows, width = block_low.shape
    out_shape = [jax.ShapeDtypeStruct((rows, width), BF16), jax.ShapeDtypeStruct((rows, width), F32)]
    for grad in grads:
        out_shape += [jax.ShapeDtypeStruct(grad.shape, F32)] * 4 + [jax.ShapeDtypeStruct(grad.shape, BF16)]
    out_shape.append(jax.ShapeDtypeStruct((2, 5), F32))
    small = [(array.shape, array.dtype) for array in operands[2:] + out_shape[2:]]
    count = len(out_shape) - 2
    return pl.pallas_call(
        functools.partial(update_kernel, count),
        out_shape=tuple(out_shape),
        in_specs=[any_space] * len(operands),
        out_specs=(any_space,) * len(out_shape),
        scratch_shapes=[pltpu.VMEM(shape, dtype) for shape, dtype in small]
        + [
            pltpu.VMEM((CHUNKS, rows // CHUNKS, width), BF16),
            pltpu.VMEM((CHUNKS, rows // CHUNKS, width), F32),
            pltpu.VMEM((rows, width), BF16),
            pltpu.SemaphoreType.DMA((3, CHUNKS)),
            pltpu.SemaphoreType.DMA((21,)),
            pltpu.SemaphoreType.DMA((count,)),
        ],
        compiler_params=pltpu.CompilerParams(vmem_limit_bytes=63 * 2**20),
        name="update",
    )(*operands)


def local(mesh_sizes, *arrays):
    tokens, cotangent, frames = arrays[0:3]
    tensors = [list(arrays[3 + 3 * i : 6 + 3 * i]) for i in range(5)]
    for i in (1, 3):
        tensors[i] = [array.T for array in tensors[i]]
    masters, firsts, seconds = ([tensor[i] for tensor in tensors] for i in range(3))
    results = run_layer(mesh_sizes, tokens, cotangent, frames, masters, firsts, seconds)
    updated = run_update(results[0], results[1], results[2:7], masters, firsts, seconds, results[7])
    outs = list(updated[0:2])
    for i in range(5):
        five = updated[2 + 5 * i : 7 + 5 * i]
        outs += [array.T for array in five] if i in (1, 3) else list(five)
    outs.append(updated[27].T)
    return tuple(outs)


def solution(mesh):
    qkv, turned, straight, row = P(None, "seq", "head"), P("head", "seq"), P("seq", "head"), P(None, "seq")
    kinds = (qkv, turned, straight, turned, row)
    in_specs = [P("seq", None), P("seq", None), P()]
    out_specs = [P("seq", None), P("seq", None)]
    for kind in kinds:
        in_specs += [kind] * 3
        out_specs += [kind] * 5
    out_specs.append(P())
    return jax.shard_map(
        functools.partial(local, (mesh.shape["seq"], mesh.shape["head"])),
        mesh=mesh,
        in_specs=tuple(in_specs),
        out_specs=tuple(out_specs),
        check_vma=False,
    )
```
